32 devices in a mesh: wide: 8 (over z, x), narrow: 4 (over y, core).
Axes of the slice: x: 2, y: 2, z: 4, core: 2. Of those that a mesh axis runs over, the one named last changes fastest.
Arguments:
- params: float32 [3129344], P(('wide', 'narrow')), may hold values from -2 to 2
- first_moment: float32 [3129344], P(('wide', 'narrow')), may hold values from -0.00390625 to 0.00390625
- second_moment: float32 [3129344], P(('wide', 'narrow')), may hold values from 2.746582e-09 to 4.3945313e-08
- ct_image: bfloat16 [16, 32, 32], P('wide', 'narrow'), may hold values from -10 to 10
- labels: int32 [16, 32, 32], P('wide', 'narrow'), may hold values from 0 to 2
- valid_mask: int32 [16, 32, 32], P('wide', 'narrow'), may hold values from 0 to 1
Outputs:
- new_params: float32 [3129344], P(('wide', 'narrow'))
- new_first: float32 [3129344], P(('wide', 'narrow'))
- new_second: float32 [3129344], P(('wide', 'narrow'))
- loss_sum: float32 [], replicated
- valid_count: float32 [], replicated
The draws below stay inside these ranges and needn't reach their ends.
All inputs are finite; a program needn't handle non-finite values.
Results may differ from the reference program's by a relative error of at most 0.0077.
Values may be sent and summed in bfloat16 or wider, within the bound.
A program may use at most 128 MiB of HBM per device.

```python
import math
import jax
import jax.numpy as jnp
from jax import lax

C1 = 128
C2 = 256
GATE = 64
CLASSES = 3
NZ = 32
STEP = 10
NX = 16
NY = 32
PARAMS = 3129344


def param_pieces():
    return [(27 * C1, 27.0 ** (-0.5), 0.0), (27 * C1 * C1, (27.0 * C1) ** (-0.5), 0.0), (27 * C1 * C2, (27.0 * C1) ** (-0.5), 0.0), (C1 * GATE, C1 ** (-0.5), 0.0), (C2 * GATE, C2 ** (-0.5), 0.0), (GATE, GATE ** (-0.5), 0.0), (27 * (C1 + C2) * C1, (27.0 * (C1 + C2)) ** (-0.5), 0.0), (27 * C1 * C1, (27.0 * C1) ** (-0.5), 0.0), ((C1 + 1) * CLASSES, C1 ** (-0.5), 0.0), (4 * C1 + C2, 0.1, 1.0), (4 * C1 + C2, 0.1, 0.0)]


def draw_params(key, part):
    key = jax.random.fold_in(key, 11)
    noise_v = jnp.clip(jax.random.normal(key, (PARAMS,), jnp.float32), -4.0, 4.0)
    scales = []
    centers = []
    used_len = 0
    for length, spread, center in param_pieces():
        ramp_up = 0.6 + 1.2 * jnp.arange(length, dtype=jnp.float32) / length
        scales.append(spread * ramp_up)
        centers.append(jnp.full((length,), center, jnp.float32))
        used_len = used_len + length
    scales.append(jnp.full((PARAMS - used_len,), 0.05, jnp.float32))
    centers.append(jnp.zeros((PARAMS - used_len,), jnp.float32))
    return jnp.concatenate(centers) + jnp.concatenate(scales) * noise_v


def draw_ct_image(key, part):
    key = jax.random.fold_in(key, 12)
    across = jnp.arange(NX, dtype=jnp.float32)[:, None, None] / (NX - 1)
    down_y = jnp.arange(NY, dtype=jnp.float32)[None, :, None] / (NY - 1)
    noise_v = jnp.clip(jax.random.normal(key, (NX, NY, NZ), jnp.float32), -3.2, 3.2)
    volume = (1.0 + across + down_y) * noise_v
    return volume.astype(jnp.bfloat16)


def draw_valid_mask(key, part):
    key = jax.random.fold_in(key, 13)
    across = jnp.arange(NX, dtype=jnp.int32)[:, None, None]
    down_y = jnp.arange(NY, dtype=jnp.int32)[None, :, None]
    limit_v = 250 + 250 * across // NX + 250 * down_y // NY
    rolled = jax.random.randint(key, (NX, NY, NZ), 0, 1000)
    return (rolled < limit_v).astype(jnp.int32)


def touch_ends(entries, own_key, smallest, high):
    shape = entries.shape
    spot = [jax.random.randint(jax.random.fold_in(own_key, axis), (), 0, shape[axis]) for axis in range(len(shape))]
    entries = entries.at[tuple(spot)].set(smallest)
    longest = shape.index(max(shape))
    spot[longest] = (spot[longest] + 1) % shape[longest]
    return entries.at[tuple(spot)].set(high)


def block_levels(key, shape, split, least, top_value):
    def one(axis_at, parts):
        draws = jax.random.uniform(jax.random.fold_in(jax.random.fold_in(key, 6), axis_at), (parts,), jnp.float32, least / len(split), top_value / len(split))
        return jnp.repeat(jnp.exp(draws), shape[axis_at] // parts).reshape((-1,) + (1,) * (len(shape) - axis_at - 1))

    factor_of = one(*split[0])
    for cut in split[1:]:
        factor_of = factor_of * one(*cut)
    return factor_of


def noise(rng, shape, scale, reach, split=(), kind=jnp.bfloat16):
    values = scale * jax.random.normal(rng, shape, jnp.float32)
    if split:
        values = values * block_levels(rng, shape, split, -0.22, 0.18)
    return jnp.clip(values, -reach, reach).astype(kind)


def setup_inputs(seed: int = 0) -> dict:
    seeds = jax.random.split(jax.random.key(seed), 7)
    return {
        "params": draw_params(jax.random.fold_in(seeds[6], 71), 0),
        "first_moment": noise(seeds[1], (PARAMS,), (0.033 * (NX * NY * NZ) ** -0.5), 0.00390625, ((0, 32),), jnp.float32),
        "second_moment": jnp.clip(jnp.exp(math.log(4.394531316620487e-08) - 2.7725887 * jax.random.uniform(seeds[2], (PARAMS,), jnp.float32) ** block_levels(seeds[2], (PARAMS,), ((0, 32),), -0.2, 0.2)), 2.7465820728878043e-09, 4.394531316620487e-08),
        "ct_image": draw_ct_image(jax.random.fold_in(seeds[6], 71), 0),
        "labels": touch_ends(jax.random.randint(seeds[4], (NX, NY, NZ), 0, CLASSES), jax.random.fold_in(seeds[4], 1), 0, CLASSES - 1).astype(jnp.int32),
        "valid_mask": draw_valid_mask(jax.random.fold_in(seeds[6], 71), 0),
    }


@jax.custom_vjp
def low(v):
    return lax.optimization_barrier(v.astype(jnp.bfloat16)).astype(jnp.float32)

@jax.custom_vjp
def low_back(v):
    return v

def low_keep(v):
    return (low(v), None)

def low_pass(kept, grad):
    return (grad,)

def back_keep(v):
    return (v, None)

def back_low(kept, grad):
    return (low(grad),)
low.defvjp(low_keep, low_pass)
low_back.defvjp(back_keep, back_low)
EPS_NORM = 1e-05
BETA_ONE = 0.9
BETA_TWO = 0.999
EPS_ADAM = 1e-06
DECAY_RATE = 0.01
LEARN_RATE = 0.3
PRECISE = lax.Precision.HIGHEST

def layout_table():
    return [(27, 1, C1), (27, C1, C1), (27, C1, C2), (C1, GATE), (C2, GATE), (GATE,), (27, C1 + C2, C1), (27, C1, C1), (C1 + 1, CLASSES), (4 * C1 + C2,), (4 * C1 + C2,)]

def table_lengths():
    lengths = []
    for tensor_shape in layout_table():
        length = 1
        for extent in tensor_shape:
            length = length * extent
        lengths.append(length)
    return lengths

def unpack_weights(flat_weights):
    pieces = []
    offset = 0
    for tensor_shape, length in zip(layout_table(), table_lengths()):
        pieces.append(flat_weights[offset:offset + length].reshape(tensor_shape))
        offset = offset + length
    return pieces

def segment_ids(total_len):
    positions = jnp.arange(total_len, dtype=jnp.int32)
    result = jnp.zeros((total_len,), jnp.int32)
    start_at = 0
    for length in table_lengths():
        start_at = start_at + length
        result = result + (positions >= start_at).astype(jnp.int32)
    return result

def conv_full(volume, kernel):
    filters = kernel.reshape(3, 3, 3, kernel.shape[1], kernel.shape[2])
    return lax.conv_general_dilated(volume[None], filters, (1, 1, 1), 'SAME', dimension_numbers=('NDHWC', 'DHWIO', 'NDHWC'), precision=PRECISE)[0]

def norm_full(raw, gain_v, bias_v):
    mean_v = lax.optimization_barrier(jnp.mean(raw, axis=(0, 1, 2)))
    spread = lax.optimization_barrier(jnp.mean(raw * raw, axis=(0, 1, 2))) - mean_v * mean_v
    return (raw - mean_v) * lax.rsqrt(spread + EPS_NORM) * gain_v + bias_v

def pool_mean(volume):
    sx, sy, sz, width_c = volume.shape
    return lax.optimization_barrier(jnp.mean(volume.reshape(sx // 2, 2, sy // 2, 2, sz // 2, 2, width_c), axis=(1, 3, 5)))

def upsample(volume):
    return jnp.repeat(jnp.repeat(jnp.repeat(volume, 2, 0), 2, 1), 2, 2)

def channel_mix(volume, matrix):
    return jnp.einsum('xyzc,cd->xyzd', volume, matrix, precision=PRECISE)

def forward(flat_params, volume, labels, valid_float):
    w_in, w_enc, w_mid, w_x, w_g, w_psi, w_dec1, w_dec2, w_head, gains, shifts = unpack_weights(low(flat_params))
    bounds = [0, C1, 2 * C1, 2 * C1 + C2, 3 * C1 + C2, 4 * C1 + C2]

    def norm_at(raw, layer_id):
        return norm_full(raw, gains[bounds[layer_id]:bounds[layer_id + 1]], shifts[bounds[layer_id]:bounds[layer_id + 1]])
    raw_entry = low_back(conv_full(volume[..., None], w_in))
    act_entry = low(jax.nn.silu(norm_at(raw_entry, 0)))
    raw_encode = low_back(conv_full(act_entry, w_enc))
    skip_out = jax.nn.silu(norm_at(raw_encode, 1))
    pooled = low(pool_mean(skip_out))
    raw_middle = low_back(conv_full(pooled, w_mid))
    coarse = low(low_back(jax.nn.silu(norm_at(raw_middle, 2))))
    gate_fine = low_back(channel_mix(low(skip_out), w_x))
    gate_coarse = low_back(channel_mix(coarse, w_g))
    mixed_in = gate_fine + upsample(gate_coarse)
    attention = jax.nn.sigmoid(jnp.dot(jax.nn.silu(mixed_in), w_psi, precision=PRECISE))
    joined = jnp.concatenate([low(skip_out * attention[..., None]), upsample(coarse)], -1)
    raw_decode = low_back(conv_full(joined, w_dec1))
    act_decode = low(jax.nn.silu(norm_at(raw_decode, 3)))
    raw_final = low_back(conv_full(act_decode, w_dec2))
    act_final = low(jax.nn.silu(norm_at(raw_final, 4)))
    logits = low_back(channel_mix(act_final, w_head[:C1]) + w_head[C1])
    log_total = jax.nn.logsumexp(logits, -1)
    picked = lax.optimization_barrier(jnp.sum(logits * jax.nn.one_hot(labels, CLASSES, dtype=logits.dtype), -1))
    loss_sum = jnp.sum(valid_float * (log_total - picked))
    valid_count = jnp.sum(valid_float)
    return (loss_sum / valid_count, (loss_sum, valid_count))

def reference(params, first_moment, second_moment, ct_image, labels, valid_mask):
    volume = ct_image.astype(jnp.float32)
    valid_float = valid_mask.astype(jnp.float32)
    loss_mean, pullback, extras = jax.vjp(lambda flat_params: forward(flat_params, volume, labels, valid_float), params, has_aux=True)
    gradient = pullback(jnp.ones_like(loss_mean))[0]
    new_first = BETA_ONE * first_moment + (1.0 - BETA_ONE) * gradient
    new_second = BETA_TWO * second_moment + (1.0 - BETA_TWO) * gradient * gradient
    update = new_first / (1.0 - BETA_ONE ** STEP) / (jnp.sqrt(new_second / (1.0 - BETA_TWO ** STEP)) + EPS_ADAM) + DECAY_RATE * params
    segment = segment_ids(params.shape[0])
    segment_count = len(layout_table()) + 1
    weight_sq = jax.ops.segment_sum(params * params, segment, num_segments=segment_count)
    update_sq = jax.ops.segment_sum(update * update, segment, num_segments=segment_count)
    trust_ratio = jnp.sqrt(weight_sq) / jnp.sqrt(update_sq)
    new_params = params - LEARN_RATE * trust_ratio[segment] * update
    return (new_params, new_first, new_second, extras[0], extras[1])
```

```python
import functools

import jax
import jax.numpy as jnp
from jax import lax
from jax.experimental import pallas as pl
from jax.experimental.pallas import tpu as pltpu
from jax.sharding import PartitionSpec as P

C1 = 128
C2 = 256
GATE = 64
CLASSES = 3
STEP = 10

EPS_NORM = 1e-05
BETA_ONE = 0.9
BETA_TWO = 0.999
EPS_ADAM = 1e-06
DECAY_RATE = 0.01
LEARN_RATE = 0.3

F32 = jnp.float32
BF16 = jnp.bfloat16
MESH = pl.DeviceIdType.MESH
LANES = 128
TILE = 16 * LANES

LENGTHS = (
    27 * C1,
    27 * C1 * C1,
    27 * C1 * C2,
    C1 * GATE,
    C2 * GATE,
    GATE,
    27 * (C1 + C2) * C1,
    27 * C1 * C1,
    (C1 + 1) * CLASSES,
    4 * C1 + C2,
    4 * C1 + C2,
)
STARTS = tuple(sum(LENGTHS[:i]) for i in range(len(LENGTHS)))
USED = sum(LENGTHS)

FRONT = 32 * LANES - STARTS[1]
SPLIT = STARTS[6]
ROW_IN = STARTS[0] + FRONT
ROW_IN = ROW_IN // LANES
ROW_ENC = (STARTS[1] + FRONT) // LANES
ROW_MID = (STARTS[2] + FRONT) // LANES
ROW_X = (STARTS[3] + FRONT) // LANES
ROW_G = (STARTS[4] + FRONT) // LANES
ROW_PSI = (STARTS[5] + FRONT) // LANES
ROWS_A = -(-(SPLIT + FRONT) // TILE) * 16
ROW_DEC1 = ROWS_A
ROW_DEC2 = ROW_DEC1 + (STARTS[7] - SPLIT) // LANES
ROW_TAIL = ROW_DEC1 + (STARTS[8] - SPLIT) // LANES

DIRS = tuple((dx, dy) for dx in (-1, 0, 1) for dy in (-1, 0, 1) if (dx, dy) != (0, 0))

N_AR = 10
N_HALO = 9


def dot(a, b):
    return jnp.dot(a, b, preferred_element_type=F32)


def dot_nt(a, b):
    return lax.dot_general(a, b, (((1,), (1,)), ((), ())), preferred_element_type=F32)


def dot_tn(a, b):
    return lax.dot_general(a, b, (((0,), (0,)), ((), ())), preferred_element_type=F32)


def iota(shape, dim):
    return lax.broadcasted_iota(jnp.int32, shape, dim)


def onehot(cond):
    return jnp.where(cond, 1.0, 0.0).astype(BF16)


def silu_grad(v, s):
    return s * (1.0 + v * (1.0 - s))


def step_kernel(cfg, ct_ref, lab_ref, val_ref, w_ref, g_ref, out_ref, *scr):
    names = cfg["names"]
    s = dict(zip(names, scr))
    nw, nn = cfg["nw"], cfg["nn"]
    total = nw * nn
    X, Y, Z = cfg["ext"]
    XE, YE = X + 2, Y + 2
    CX, CY, CZ = X // 2, Y // 2, Z // 2
    V = X * Y * Z
    VC = CX * CY * CZ
    voxels = float(V * total)
    coarse_voxels = voxels / 8.0
    w = lax.axis_index("wide")
    n = lax.axis_index("narrow")
    me = w * nn + n

    def dev(p):
        return (p // nn, lax.rem(p, nn))

    barrier = pltpu.get_barrier_semaphore()

    def greet(d, carry):
        pl.semaphore_signal(
            barrier, inc=1, device_id=dev(lax.rem(me + d, total)), device_id_type=MESH
        )
        return carry

    lax.fori_loop(1, total, greet, 0)
    pl.semaphore_wait(barrier, total - 1)

    slots, ar_send, ar_recv = s["slots"], s["ar_send"], s["ar_recv"]

    def ar_start(r, rows):
        rows = list(rows) + [jnp.zeros((1, LANES), F32)] * (4 - len(rows))
        slots[r, me] = jnp.concatenate(rows, 0)

        def push(d, carry):
            pltpu.make_async_remote_copy(
                slots.at[r, me],
                slots.at[r, me],
                ar_send.at[r],
                ar_recv.at[r],
                device_id=dev(lax.rem(me + d, total)),
                device_id_type=MESH,
            ).start()
            return carry

        lax.fori_loop(1, total, push, 0)

    def ar_whole(r):
        others = slots.at[r, pl.ds(0, total - 1)]
        return pltpu.make_async_remote_copy(
            others, others, ar_send.at[r], ar_recv.at[r], device_id=(w, n), device_id_type=MESH
        )

    def ar_wait(r):
        ar_whole(r).wait_recv()
        return jnp.sum(slots[r], axis=0)

    side, side_send, side_recv = s["side"], s["side_send"], s["side_recv"]

    def side_start(rows):
        rows = list(rows) + [jnp.zeros((1, LANES), F32)] * (8 - len(rows))
        side[me] = jnp.concatenate(rows, 0)

        def push(d, carry):
            pltpu.make_async_remote_copy(
                side.at[me],
                side.at[me],
                side_send,
                side_recv,
                device_id=dev(lax.rem(me + d, total)),
                device_id_type=MESH,
            ).start()
            return carry

        lax.fori_loop(1, total, push, 0)

    def side_whole():
        others = side.at[pl.ds(0, total - 1)]
        return pltpu.make_async_remote_copy(
            others, others, side_send, side_recv, device_id=(w, n), device_id_type=MESH
        )

    halo_send, halo_recv = s["halo_send"], s["halo_recv"]

    def halo_copy(h, ref, i):
        dx, dy = DIRS[i]
        ex, ey = ref.shape[0] - 2, ref.shape[1] - 2

        def source(d, size):
            return pl.ds(1, size) if d == 0 else pl.ds(size if d > 0 else 1, 1)

        def target(d, size):
            return pl.ds(1, size) if d == 0 else pl.ds(0 if d > 0 else size + 1, 1)

        return pltpu.make_async_remote_copy(
            ref.at[source(dx, ex), source(dy, ey)],
            ref.at[target(dx, ex), target(dy, ey)],
            halo_send.at[h, i],
            halo_recv.at[h, i],
            device_id=(lax.rem(w + dx + nw, nw), lax.rem(n + dy + nn, nn)),
            device_id_type=MESH,
        )

    def halo_start(h, ref):
        for i in range(8):
            halo_copy(h, ref, i).start()

    def halo_wait(h, ref):
        for i in range(8):
            halo_copy(h, ref, i).wait_recv()

    def clear_edges(ref, depth):
        ex, ey = ref.shape[0], ref.shape[1]

        @pl.when(w == 0)
        def _():
            ref[0:depth] = jnp.zeros((depth,) + ref.shape[1:], ref.dtype)

        @pl.when(w == nw - 1)
        def _():
            ref[ex - depth : ex] = jnp.zeros((depth,) + ref.shape[1:], ref.dtype)

        @pl.when(n == 0)
        def _():
            ref[:, 0:depth] = jnp.zeros((ex, depth) + ref.shape[2:], ref.dtype)

        @pl.when(n == nn - 1)
        def _():
            ref[:, ey - depth : ey] = jnp.zeros((ex, depth) + ref.shape[2:], ref.dtype)

    def z_three(flat, length):
        rows = flat.shape[0]
        at = jnp.bitwise_and(iota(flat.shape, 0), length - 1)
        before = jnp.where(at == 0, 0.0, pltpu.roll(flat, 1, 0))
        after = jnp.where(at == length - 1, 0.0, pltpu.roll(flat, rows - 1, 0))
        return before.astype(BF16), flat.astype(BF16), after.astype(BF16)

    def put_three(ref, flat, base, stride):
        shape = ref.shape[:3] + (LANES,)
        for c, part in enumerate(z_three(flat, ref.shape[2])):
            lo = c * stride + base
            ref[:, :, :, lo : lo + LANES] = part.reshape(shape)

    def merge_frame(full, low):
        ex, ey = full.shape[0], full.shape[1]
        full[0] = low[0].astype(F32)
        full[ex - 1] = low[ex - 1].astype(F32)
        full[1 : ex - 1, 0] = low[1 : ex - 1, 0].astype(F32)
        full[1 : ex - 1, ey - 1] = low[1 : ex - 1, ey - 1].astype(F32)

    def conv(ref, weight, row0, ext):
        x, y = ext
        rows = x * y * ref.shape[2]
        depth = ref.shape[3]
        acc = None
        for ab in range(9):
            a, b = ab // 3, ab % 3
            window = ref[a : a + x, b : b + y].reshape(rows, depth)
            part = dot(window, weight[row0 + ab * depth : row0 + (ab + 1) * depth, :])
            acc = part if acc is None else acc + part
        return acc

    def conv_back(ref, weight, row0, cin, cout, ext):
        x, y = ext
        rows = x * y * ref.shape[2]
        acc = None
        for ab in range(9):
            a, b = ab // 3, ab % 3
            for c in range(3):
                window = ref[a : a + x, b : b + y, :, c * cout : (c + 1) * cout]
                tap = 26 - (3 * ab + c)
                part = dot_nt(
                    window.reshape(rows, cout),
                    weight[row0 + tap * cin : row0 + (tap + 1) * cin, :],
                )
                acc = part if acc is None else acc + part
        return acc

    def conv_grad(ref, low, row0, ext):
        x, y = ext
        rows = x * y * ref.shape[2]
        depth = ref.shape[3]
        for ab in range(9):
            a, b = ab // 3, ab % 3
            window = ref[a : a + x, b : b + y].reshape(rows, depth)
            g_ref[row0 + ab * depth : row0 + (ab + 1) * depth, :] = dot_tn(window, low).astype(BF16)

    def col_sum(v):
        return jnp.sum(v, axis=0, keepdims=True)

    def own(ref):
        return ref[1 : ref.shape[0] - 1, 1 : ref.shape[1] - 1]

    def flat(v):
        return v.reshape(-1, v.shape[-1])

    pair = s["pair"]

    def pool(v):
        v = v.reshape(X, Y, Z, LANES)
        v = v[0] + v[1]
        v = v.reshape(CY, 2, Z, LANES)
        v = v[:, 0] + v[:, 1]
        pair[0 : CY * Z] = v.reshape(CY * Z, LANES)
        return pair[pl.ds(0, VC, stride=2), :] + pair[pl.ds(1, VC, stride=2), :]

    def spread(v):
        pair[pl.ds(0, VC, stride=2), :] = v
        pair[pl.ds(1, VC, stride=2), :] = v
        u = pair[0 : CY * Z].reshape(CY, 1, Z, LANES)
        u = jnp.broadcast_to(u, (CY, 2, Z, LANES)).reshape(1, Y, Z, LANES)
        return jnp.broadcast_to(u, (X, Y, Z, LANES)).reshape(V, LANES)

    def stats(total_rows, count):
        half = total_rows.shape[0] // 2
        parts = [total_rows[i : i + 1] for i in range(2 * half)]
        mean = jnp.concatenate(parts[:half], 1) / count
        spread_v = jnp.concatenate(parts[half:], 1) / count - mean * mean
        return mean, lax.rsqrt(spread_v + EPS_NORM)

    cts, ct_send, ct_recv = s["cts"], s["ct_send"], s["ct_recv"]
    cts[4] = ct_ref[...]

    def ct_copy(i):
        dx, dy = DIRS[i]
        return pltpu.make_async_remote_copy(
            cts.at[4],
            cts.at[3 * (1 - dx) + 1 - dy],
            ct_send.at[i],
            ct_recv.at[i],
            device_id=(lax.rem(w + dx + nw, nw), lax.rem(n + dy + nn, nn)),
            device_id_type=MESH,
        )

    for i in range(8):
        ct_copy(i).start()

    tail = w_ref[ROW_TAIL : ROW_TAIL + 16, :].astype(F32)
    used_rows = CLASSES * (C1 + 1) // LANES
    used_lanes = CLASSES * (C1 + 1) % LANES
    rolled = pltpu.roll(tail, LANES - used_lanes, 1)
    lane_id = iota((1, LANES), 1)

    def tail_row(q):
        r = used_rows + q
        return jnp.where(
            lane_id < LANES - used_lanes, rolled[r : r + 1], rolled[r + 1 : r + 2]
        )

    gains = [tail_row(q) for q in range(6)]
    shifts = [tail_row(6 + q) for q in range(6)]
    gain = [gains[0], gains[1], jnp.concatenate(gains[2:4], 1), gains[4], gains[5]]
    shift = [shifts[0], shifts[1], jnp.concatenate(shifts[2:4], 1), shifts[4], shifts[5]]

    def select_head(j, r):
        return onehot(
            LANES * r + iota((LANES, LANES), 0) == CLASSES * iota((LANES, LANES), 1) + j
        )

    tail_low = tail.astype(BF16)
    head_rows = []
    for j in range(CLASSES):
        row = None
        for r in range(CLASSES):
            part = dot(tail_low, select_head(j, r))[r : r + 1]
            row = part if row is None else row + part
        head_rows.append(row)
    head_t = jnp.concatenate(head_rows + [jnp.zeros((8 - CLASSES, LANES), F32)], 0).astype(BF16)
    bias_row = tail[used_rows : used_rows + 1]
    bias_col = jnp.sum(
        jnp.where(iota((8, LANES), 0) == iota((8, LANES), 1), bias_row, 0.0), axis=1, keepdims=True
    )
    bias_col = jnp.where(iota((8, 1), 0) < CLASSES, bias_col, 0.0)
    psi = w_ref[ROW_PSI : ROW_PSI + 16, :].astype(F32)[0:1]
    psi = jnp.where(lane_id < GATE, psi, 0.0)

    def pick_half(h, rows):
        return onehot(iota((2 * rows, rows), 0) == 2 * iota((2 * rows, rows), 1) + h)

    def widen(block, rows):
        block = block.astype(F32)
        lower = jnp.where(lane_id < GATE, block, 0.0).astype(BF16)
        upper = jnp.where(lane_id < GATE, pltpu.roll(block, GATE, 1), 0.0).astype(BF16)
        both = dot(pick_half(0, rows), lower) + dot(pick_half(1, rows), upper)
        return both.astype(BF16)

    def narrow_back(block, rows):
        low = block.astype(BF16)
        lower = dot_tn(pick_half(0, rows), low)
        upper = dot_tn(pick_half(1, rows), low)
        return (lower + pltpu.roll(upper, GATE, 1)).astype(BF16)

    w_x = widen(w_ref[ROW_X : ROW_X + C1 // 2, :], C1 // 2)
    w_g = widen(w_ref[ROW_G : ROW_G + C2 // 2, :], C2 // 2)

    front = w_ref[0:32, :].astype(F32)
    we = s["we"]
    for ab in range(9):
        taps = [
            jnp.broadcast_to(front[ROW_IN + 3 * ab + c : ROW_IN + 3 * ab + c + 1], (Z, LANES))
            for c in range(3)
        ]
        taps.append(jnp.zeros((LANES - 3 * Z, LANES), F32))
        we[ab * LANES : (ab + 1) * LANES] = jnp.concatenate(taps, 0).astype(BF16)

    shuffle = onehot(
        iota((C2, C2), 1)
        == jnp.bitwise_and(iota((C2, C2), 0), 1) * C1 + lax.shift_right_logical(iota((C2, C2), 0), 1)
    )
    wm = s["wm"]
    for tap in range(27):
        part = dot_tn(shuffle, w_ref[ROW_MID + C2 * tap : ROW_MID + C2 * (tap + 1), :]).astype(BF16)
        wm[tap * C1 : (tap + 1) * C1, 0:LANES] = part[0:LANES]
        wm[tap * C1 : (tap + 1) * C1, LANES:C2] = part[LANES:C2]

    valid = val_ref[...]
    count_row = jnp.broadcast_to(jnp.sum(valid, axis=1, keepdims=True), (1, LANES))

    for i in range(8):
        ct_copy(i).wait_recv()

    entry = s["entry"]
    zz, ll = iota((Z, LANES), 0), iota((Z, LANES), 1)
    band = jnp.where((jnp.bitwise_and(ll, Z - 1) == zz + ll // Z - 1) & (ll < 3 * Z), 1.0, 0.0)
    for ex in range(X + 4):
        bx = (ex - 2 + X) // X
        lx = ex - 2 - (bx - 1) * X
        for ey in range(Y + 4):
            by = (ey - 2 + Y) // Y
            ly = ey - 2 - (by - 1) * Y
            row = cts[3 * bx + by, lx * Y + ly : lx * Y + ly + 1]
            entry[ex, ey] = (jnp.broadcast_to(row, (Z, LANES)) * band).astype(BF16)
    clear_edges(entry, 2)
    raw1 = s["raw1"]
    raw1[...] = conv(entry, we, 0, (XE, YE)).reshape(XE, YE, Z, LANES)
    mine = flat(own(raw1))
    ar_start(0, [col_sum(mine), col_sum(mine * mine), count_row])
    sums = ar_wait(0)
    valid_count = sums[2:3, 0:1]
    mean1, inv1 = stats(sums[0:2], voxels)
    v = (flat(raw1[...]) - mean1) * inv1 * gain[0] + shift[0]
    pad1 = s["pad1"]
    put_three(pad1, v * jax.nn.sigmoid(v), 0, C1)
    clear_edges(pad1, 1)

    raw2, low2 = s["raw2"], s["low2"]
    mine = conv(pad1, w_ref, ROW_ENC, (X, Y))
    raw2[1 : XE - 1, 1 : YE - 1] = mine.reshape(X, Y, Z, C1)
    low2[1 : XE - 1, 1 : YE - 1] = mine.astype(BF16).reshape(X, Y, Z, C1)
    ar_start(1, [col_sum(mine), col_sum(mine * mine)])
    halo_start(0, low2)
    sums = ar_wait(1)
    mean2, inv2 = stats(sums[0:2], voxels)
    v = (mine - mean2) * inv2 * gain[1] + shift[1]
    skip_own = v * jax.nn.sigmoid(v)

    pool_in = s["pool_in"]
    pool_in[1 : CX + 1, 1 : CY + 1] = (pool(skip_own) * 0.125).astype(BF16).reshape(CX, CY, CZ, C1)
    halo_start(1, pool_in)
    halo_wait(0, low2)
    merge_frame(raw2, low2)
    v = (flat(raw2[...]) - mean2) * inv2 * gain[1] + shift[1]
    skip = s["skip"]
    skip_all = v * jax.nn.sigmoid(v)
    skip[...] = skip_all.reshape(XE, YE, Z, C1)
    mix = s["mix"]
    mix[...] = dot(skip_all.astype(BF16), w_x).reshape(XE, YE, Z, LANES)
    halo_wait(1, pool_in)
    clear_edges(pool_in, 1)
    pad_mid = s["pad_mid"]
    put_three(pad_mid, flat(pool_in[...].astype(F32)), 0, C1)
    raw3, low3 = s["raw3"], s["low3"]
    mine = conv(pad_mid, wm, 0, (CX, CY))
    raw3[1 : CX + 1, 1 : CY + 1] = mine.reshape(CX, CY, CZ, C2)
    low3[1 : CX + 1, 1 : CY + 1] = mine.astype(BF16).reshape(CX, CY, CZ, C2)
    sum_v, square_v = col_sum(mine), col_sum(mine * mine)
    ar_start(
        2, [sum_v[:, 0:C1], sum_v[:, C1:C2], square_v[:, 0:C1], square_v[:, C1:C2]]
    )
    halo_start(2, low3)
    sums = ar_wait(2)
    mean3, inv3 = stats(sums, coarse_voxels)
    halo_wait(2, low3)
    merge_frame(raw3, low3)
    v = (flat(raw3[...]) - mean3) * inv3 * gain[2] + shift[2]
    coarse = (v * jax.nn.sigmoid(v)).astype(BF16).reshape(CX + 2, CY + 2, CZ, C2)
    coarse_own = flat(coarse[1 : CX + 1, 1 : CY + 1])
    frame = (CY + 2) * CZ
    doubled = onehot(
        iota((2 * frame, frame), 1) == lax.shift_right_logical(iota((2 * frame, frame), 0), 1)
    )
    tall = s["tall"]
    for cx in range(CX + 2):
        tall[cx] = (
            dot(doubled, coarse[cx].reshape(frame, C2)).astype(BF16).reshape(CY + 2, Z, C2)
        )

    def expand(u):
        u = jnp.concatenate([u[(i + 1) // 2 : (i + 1) // 2 + 1] for i in range(XE)], 0)
        return jnp.concatenate([u[:, (j + 1) // 2 : (j + 1) // 2 + 1] for j in range(YE)], 1)

    gate_c = dot(flat(tall[...]), w_g).reshape(CX + 2, CY + 2, Z, LANES)
    mixed_in = flat(mix[...] + expand(gate_c))
    mix[...] = mixed_in.reshape(XE, YE, Z, LANES)
    mixed = mixed_in * jax.nn.sigmoid(mixed_in)
    att = jax.nn.sigmoid(jnp.sum(mixed * psi, axis=1, keepdims=True))
    attention = s["attention"]
    attention[...] = jnp.broadcast_to(att, (XE * YE * Z, LANES)).reshape(XE, YE, Z, LANES)
    pad_join = s["pad_join"]
    put_three(pad_join, flat(skip[...] * attention[...]), 0, C1 + C2)
    for half in range(2):
        piece = flat(tall[:, :, :, half * C1 : (half + 1) * C1].astype(F32))
        for c, part in enumerate(z_three(piece, Z)):
            lo = c * (C1 + C2) + C1 + half * C1
            pad_join[:, :, :, lo : lo + C1] = expand(part.reshape(CX + 2, CY + 2, Z, C1))
    clear_edges(pad_join, 1)

    raw4, low4 = s["raw4"], s["low4"]
    mine = conv(pad_join, w_ref, ROW_DEC1, (X, Y))
    raw4[1 : XE - 1, 1 : YE - 1] = mine.reshape(X, Y, Z, C1)
    low4[1 : XE - 1, 1 : YE - 1] = mine.astype(BF16).reshape(X, Y, Z, C1)
    ar_start(3, [col_sum(mine), col_sum(mine * mine)])
    halo_start(3, low4)
    sums = ar_wait(3)
    mean4, inv4 = stats(sums[0:2], voxels)
    halo_wait(3, low4)
    merge_frame(raw4, low4)
    v = (flat(raw4[...]) - mean4) * inv4 * gain[3] + shift[3]
    pad4 = s["pad4"]
    put_three(pad4, v * jax.nn.sigmoid(v), 0, C1)
    clear_edges(pad4, 1)

    raw5, low5 = s["raw5"], s["low5"]
    mine = conv(pad4, w_ref, ROW_DEC2, (X, Y))
    raw5[1 : XE - 1, 1 : YE - 1] = mine.reshape(X, Y, Z, C1)
    low5[1 : XE - 1, 1 : YE - 1] = mine.astype(BF16).reshape(X, Y, Z, C1)
    ar_start(4, [col_sum(mine), col_sum(mine * mine)])
    halo_start(4, low5)
    sums = ar_wait(4)
    mean5, inv5 = stats(sums[0:2], voxels)
    hat = (mine - mean5) * inv5
    v = hat * gain[4] + shift[4]
    sg = jax.nn.sigmoid(v)
    act = (v * sg).astype(BF16)

    logits = dot_nt(head_t, act) + bias_col
    real = iota((8, V), 0) < CLASSES
    logits = jnp.where(real, logits, -1e30)
    hot = iota((8, V), 0) == lab_ref[...]
    top = jnp.max(logits, axis=0, keepdims=True)
    log_total = top + jnp.log(jnp.sum(jnp.exp(logits - top), axis=0, keepdims=True))
    picked = jnp.sum(jnp.where(hot, logits, 0.0), axis=0, keepdims=True)
    loss = jnp.sum(valid * (log_total - picked), axis=1, keepdims=True)
    probs = jnp.exp(logits - log_total)
    g_logits = valid * (probs - jnp.where(hot, 1.0, 0.0)) / valid_count
    g_low = g_logits.astype(BF16)
    head_grad = dot(g_low, act)
    bias_grad = jnp.sum(g_low.astype(F32), axis=1, keepdims=True)
    bias_line = jnp.sum(
        jnp.where(iota((8, LANES), 0) == iota((8, LANES), 1), bias_grad, 0.0), axis=0, keepdims=True
    )
    dy = dot_tn(g_low, head_t) * silu_grad(v, sg)

    def norm_back(r, h, dy, hat, raw, mean, inv, gain_v, ext, count, names2, extra):
        dyf, dyl = s[names2[0]], s[names2[1]]
        ex, ey = ext[0] + 2, ext[1] + 2
        width = dy.shape[1]
        shaped = dy.reshape(ext + (width,))
        dyf[1 : ex - 1, 1 : ey - 1] = shaped
        dyl[1 : ex - 1, 1 : ey - 1] = shaped.astype(BF16)
        first, second = col_sum(dy), col_sum(dy * hat)
        rows = [first[:, i : i + LANES] for i in range(0, width, LANES)]
        rows += [second[:, i : i + LANES] for i in range(0, width, LANES)]
        ar_start(r, rows + extra)
        halo_start(h, dyl)
        return rows

    def norm_back_end(r, h, raw, mean, inv, gain_v, count, names2):
        dyf, dyl = s[names2[0]], s[names2[1]]
        sums = ar_wait(r)
        halo_wait(h, dyl)
        merge_frame(dyf, dyl)
        width = dyf.shape[3]
        k = width // LANES
        one = jnp.concatenate([sums[i : i + 1] for i in range(k)], 1)
        two = jnp.concatenate([sums[k + i : k + i + 1] for i in range(k)], 1)
        hat_all = (flat(raw[...]) - mean) * inv
        back = inv * gain_v * (flat(dyf[...]) - one / count - hat_all * (two / count))
        return sums, back

    grad_shift, grad_gain = {}, {}
    fine = (X, Y, Z)
    norm_back(5, 5, dy, hat, raw5, mean5, inv5, gain[4], fine, voxels, ("dy5", "dyl5"),
              [jnp.broadcast_to(loss, (1, LANES))])
    halo_wait(4, low5)
    merge_frame(raw5, low5)
    sums, back = norm_back_end(5, 5, raw5, mean5, inv5, gain[4], voxels, ("dy5", "dyl5"))
    grad_shift[4], grad_gain[4] = [sums[0:1]], [sums[1:2]]
    loss_row = sums[2:3]
    dpad = s["dpad5"]
    put_three(dpad, back, 0, C1)
    clear_edges(dpad, 1)
    grad_act = conv_back(dpad, w_ref, ROW_DEC2, C1, C1, (X, Y))
    hat = (flat(own(raw4)) - mean4) * inv4
    v = hat * gain[3] + shift[3]
    dy = grad_act * silu_grad(v, jax.nn.sigmoid(v))
    norm_back(6, 6, dy, hat, raw4, mean4, inv4, gain[3], fine, voxels, ("dy4", "dyl4"), [])
    conv_grad(pad4, flat(own(dpad)[:, :, :, C1 : 2 * C1]), ROW_DEC2, (X, Y))
    sums, back = norm_back_end(6, 6, raw4, mean4, inv4, gain[3], voxels, ("dy4", "dyl4"))
    grad_shift[3], grad_gain[3] = [sums[0:1]], [sums[1:2]]
    dpad = s["dpad4"]
    put_three(dpad, back, 0, C1)
    clear_edges(dpad, 1)
    low_raw4 = flat(own(dpad)[:, :, :, C1 : 2 * C1])
    grad_join = conv_back(dpad, w_ref, ROW_DEC1, C1 + C2, C1, (X, Y))

    grad_gated = grad_join[:, 0:C1]
    skip_own = flat(own(skip))
    att_own = flat(own(attention))
    mixed_own = flat(own(mix))
    sg = jax.nn.sigmoid(mixed_own)
    d_att = jnp.sum(grad_gated * skip_own, axis=1, keepdims=True)
    d_logit = d_att * att_own * (1.0 - att_own)
    psi_grad = col_sum(mixed_own * sg * d_logit)
    d_mixed = d_logit * psi * silu_grad(mixed_own, sg)
    low_fine = d_mixed.astype(BF16)
    low_gc = pool(d_mixed).astype(BF16)
    d_coarse = [
        pool(grad_join[:, C1 : 2 * C1]),
        pool(grad_join[:, 2 * C1 : 3 * C1]),
    ]
    d_coarse = jnp.concatenate(d_coarse, 1) + dot_nt(low_gc, w_g)
    d_coarse = d_coarse.astype(BF16).astype(F32)
    hat = (flat(own(raw3)) - mean3) * inv3
    v = hat * gain[2] + shift[2]
    dy = d_coarse * silu_grad(v, jax.nn.sigmoid(v))
    norm_back(7, 7, dy, hat, raw3, mean3, inv3, gain[2], (CX, CY, CZ), coarse_voxels, ("dy3", "dyl3"), [])
    side_start([head_grad[0:1], head_grad[1:2], head_grad[2:3], bias_line, psi_grad])
    d_skip = s["d_skip"]
    d_skip[...] = grad_gated * att_own + dot_nt(low_fine, w_x)
    conv_grad(pad_join, low_raw4, ROW_DEC1, (X, Y))
    g_ref[ROW_X : ROW_X + C1 // 2, :] = narrow_back(
        dot_tn(skip_own.astype(BF16), low_fine), C1 // 2
    )
    g_ref[ROW_G : ROW_G + C2 // 2, :] = narrow_back(dot_tn(coarse_own, low_gc), C2 // 2)
    sums, back = norm_back_end(7, 7, raw3, mean3, inv3, gain[2], coarse_voxels, ("dy3", "dyl3"))
    grad_shift[2], grad_gain[2] = [sums[0:1], sums[1:2]], [sums[2:3], sums[3:4]]
    dpad = s["dpad3"]
    put_three(dpad, back[:, 0:C1], 0, C2)
    put_three(dpad, back[:, C1:C2], C1, C2)
    clear_edges(dpad, 1)
    low_raw3 = flat(own(dpad)[:, :, :, C2 : 2 * C2])
    d_pool = conv_back(dpad, wm, 0, C1, C2, (CX, CY))
    grad_skip = d_skip[...] + spread(d_pool) * 0.125
    hat = (flat(own(raw2)) - mean2) * inv2
    v = hat * gain[1] + shift[1]
    dy = grad_skip * silu_grad(v, jax.nn.sigmoid(v))
    norm_back(8, 8, dy, hat, raw2, mean2, inv2, gain[1], fine, voxels, ("dy2", "dyl2"), [])
    for ab in range(9):
        window = pad_mid[ab // 3 : ab // 3 + CX, ab % 3 : ab % 3 + CY].reshape(VC, 3 * C1)
        block = dot_tn(window, low_raw3).astype(BF16)
        for c in range(3):
            stacked = block[c * C1 : (c + 1) * C1]
            stacked = jnp.concatenate([stacked[:, 0:C1], stacked[:, C1:C2]], 0)
            lo = ROW_MID + (3 * ab + c) * C2
            g_ref[lo : lo + C2, :] = dot(shuffle, stacked).astype(BF16)
    sums, back = norm_back_end(8, 8, raw2, mean2, inv2, gain[1], voxels, ("dy2", "dyl2"))
    grad_shift[1], grad_gain[1] = [sums[0:1]], [sums[1:2]]
    dpad = s["dpad2"]
    put_three(dpad, back, 0, C1)
    clear_edges(dpad, 1)
    low_raw2 = flat(own(dpad)[:, :, :, C1 : 2 * C1])
    grad_act = conv_back(dpad, w_ref, ROW_ENC, C1, C1, (X, Y))
    hat1 = (flat(own(raw1)) - mean1) * inv1
    v = hat1 * gain[0] + shift[0]
    dy = grad_act * silu_grad(v, jax.nn.sigmoid(v))
    ar_start(9, [col_sum(dy), col_sum(dy * hat1)])
    conv_grad(pad1, low_raw2, ROW_ENC, (X, Y))
    sums = ar_wait(9)
    grad_shift[0], grad_gain[0] = [sums[0:1]], [sums[1:2]]
    back = inv1 * gain[0] * (dy - sums[0:1] / voxels - hat1 * (sums[1:2] / voxels))
    low_raw1 = back.astype(BF16)
    in_rows = []
    for ab in range(9):
        a, b = ab // 3, ab % 3
        window = entry[a + 1 : a + 1 + X, b + 1 : b + 1 + Y].reshape(V, LANES)
        block = dot_tn(window, low_raw1)
        for c in range(3):
            in_rows.append(col_sum(block[c * Z : (c + 1) * Z]))
    in_rows = [jnp.zeros((ROW_IN, LANES), F32)] + in_rows
    g_ref[0:32, :] = jnp.concatenate(in_rows, 0).astype(BF16)

    side_whole().wait_recv()
    small = jnp.sum(side[...], axis=0)
    flat_rows = []
    for r in range(CLASSES):
        row = None
        for j in range(CLASSES):
            part = lax.dot_general(
                small,
                select_head(j, r).astype(F32),
                (((1,), (1,)), ((), ())),
                preferred_element_type=F32,
                precision=lax.Precision.HIGHEST,
            )[j : j + 1]
            row = part if row is None else row + part
        flat_rows.append(row)
    later = []
    for group in (grad_gain, grad_shift):
        for layer in range(5):
            later += group[layer]
    later = [pltpu.roll(row, used_lanes, 1) for row in later]
    flat_rows.append(jnp.where(lane_id < used_lanes, small[3:4], later[0]))
    for q in range(1, 12):
        flat_rows.append(jnp.where(lane_id < used_lanes, later[q - 1], later[q]))
    flat_rows.append(jnp.where(lane_id < used_lanes, later[11], 0.0))
    out_ref[0:16] = jnp.concatenate(flat_rows, 0)
    out_ref[16:24] = jnp.concatenate(
        [
            jnp.where(lane_id < GATE, small[4:5], 0.0),
            loss_row,
            jnp.broadcast_to(valid_count, (1, LANES)),
            jnp.zeros((5, LANES), F32),
        ],
        0,
    )

    for r in range(N_AR):
        ar_whole(r).wait_send()
    side_whole().wait_send()
    for i in range(8):
        ct_copy(i).wait_send()
    for h, name in enumerate(
        ("low2", "pool_in", "low3", "low4", "low5", "dyl5", "dyl4", "dyl3", "dyl2")
    ):
        for i in range(8):
            halo_copy(h, s[name], i).wait_send()


def step_call(nw, nn, ext, ct, lab, val, weights):
    X, Y, Z = ext
    XE, YE = X + 2, Y + 2
    CX, CY, CZ = X // 2, Y // 2, Z // 2
    total = nw * nn
    framed = (XE, YE, Z)
    small = (CX + 2, CY + 2, CZ)
    dma = pltpu.SemaphoreType.DMA
    scratch = {
        "slots": pltpu.VMEM((N_AR, total, 4, LANES), F32),
        "ar_send": dma((N_AR,)),
        "ar_recv": dma((N_AR,)),
        "side": pltpu.VMEM((total, 8, LANES), F32),
        "side_send": dma,
        "side_recv": dma,
        "halo_send": dma((N_HALO, 8)),
        "halo_recv": dma((N_HALO, 8)),
        "cts": pltpu.VMEM((9, X * Y, LANES), F32),
        "ct_send": dma((8,)),
        "ct_recv": dma((8,)),
        "pair": pltpu.VMEM((CY * Z, LANES), F32),
        "we": pltpu.VMEM((9 * LANES, LANES), BF16),
        "wm": pltpu.VMEM((27 * C1, C2), BF16),
        "entry": pltpu.VMEM((X + 4, Y + 4, Z, LANES), BF16),
        "raw1": pltpu.VMEM(framed + (C1,), F32),
        "pad1": pltpu.VMEM(framed + (3 * C1,), BF16),
        "raw2": pltpu.VMEM(framed + (C1,), F32),
        "low2": pltpu.VMEM(framed + (C1,), BF16),
        "pool_in": pltpu.VMEM(small + (C1,), BF16),
        "skip": pltpu.VMEM(framed + (C1,), F32),
        "mix": pltpu.VMEM(framed + (LANES,), F32),
        "attention": pltpu.VMEM(framed + (LANES,), F32),
        "pad_mid": pltpu.VMEM(small + (3 * C1,), BF16),
        "raw3": pltpu.VMEM(small + (C2,), F32),
        "low3": pltpu.VMEM(small + (C2,), BF16),
        "tall": pltpu.VMEM((CX + 2, CY + 2, Z, C2), BF16),
        "pad_join": pltpu.VMEM(framed + (3 * (C1 + C2),), BF16),
        "raw4": pltpu.VMEM(framed + (C1,), F32),
        "low4": pltpu.VMEM(framed + (C1,), BF16),
        "pad4": pltpu.VMEM(framed + (3 * C1,), BF16),
        "raw5": pltpu.VMEM(framed + (C1,), F32),
        "low5": pltpu.VMEM(framed + (C1,), BF16),
        "dy5": pltpu.VMEM(framed + (C1,), F32),
        "dyl5": pltpu.VMEM(framed + (C1,), BF16),
        "dpad5": pltpu.VMEM(framed + (3 * C1,), BF16),
        "dy4": pltpu.VMEM(framed + (C1,), F32),
        "dyl4": pltpu.VMEM(framed + (C1,), BF16),
        "dpad4": pltpu.VMEM(framed + (3 * C1,), BF16),
        "dy3": pltpu.VMEM(small + (C2,), F32),
        "dyl3": pltpu.VMEM(small + (C2,), BF16),
        "dpad3": pltpu.VMEM(small + (3 * C2,), BF16),
        "dy2": pltpu.VMEM(framed + (C1,), F32),
        "dyl2": pltpu.VMEM(framed + (C1,), BF16),
        "dpad2": pltpu.VMEM(framed + (3 * C1,), BF16),
        "d_skip": pltpu.VMEM((X * Y * Z, C1), F32),
    }
    cfg = {"nw": nw, "nn": nn, "ext": ext, "names": tuple(scratch)}
    vmem = pl.BlockSpec(memory_space=pltpu.VMEM)
    return pl.pallas_call(
        functools.partial(step_kernel, cfg),
        out_shape=(
            jax.ShapeDtypeStruct(weights.shape, BF16),
            jax.ShapeDtypeStruct((24, LANES), F32),
        ),
        in_specs=[vmem] * 4,
        out_specs=(vmem, vmem),
        scratch_shapes=list(scratch.values()),
        compiler_params=pltpu.CompilerParams(
            collective_id=0, has_side_effects=True, vmem_limit_bytes=60 * 1024 * 1024
        ),
    )(ct, lab, val, weights)


def on_device(params, first_moment, second_moment, ct_image, labels, valid_mask):
    shard_len = params.shape[0]
    n_wide = lax.axis_size("wide")
    n_narrow = lax.axis_size("narrow")
    devices = n_wide * n_narrow
    place = lax.axis_index(("wide", "narrow"))
    ext = ct_image.shape
    gathered = lax.all_gather(params.astype(BF16), ("wide", "narrow"), axis=0, tiled=True)
    part_a = jnp.concatenate(
        [jnp.zeros((FRONT,), BF16), gathered[: ROWS_A * LANES - FRONT]]
    ).reshape(-1, LANES)
    n_b = -(-(shard_len * devices - SPLIT) // TILE) * TILE
    part_b = jnp.concatenate(
        [gathered[SPLIT:], jnp.zeros((n_b - (shard_len * devices - SPLIT),), BF16)]
    ).reshape(-1, LANES)
    weights = jnp.concatenate([part_a, part_b], 0)
    ct = ct_image.astype(F32).reshape(-1, ext[2])
    ct = jnp.concatenate([ct, ct, ct, jnp.zeros((ct.shape[0], LANES - 3 * ext[2]), F32)], 1)
    grads, small = step_call(
        n_wide,
        n_narrow,
        ext,
        ct,
        labels.reshape(1, -1),
        valid_mask.astype(F32).reshape(1, -1),
        weights,
    )
    first = (place == 0).astype(F32)
    flat_grad = jnp.concatenate(
        [
            grads[ROW_IN:ROW_PSI].reshape(-1).astype(F32),
            small[16, :GATE] * first,
            grads[ROW_DEC1:ROW_TAIL].reshape(-1).astype(F32),
            small[0:16].reshape(-1)[: USED - STARTS[8]] * first,
            jnp.zeros((shard_len * devices - USED,), F32),
        ]
    )
    loss_sum = small[17, 0]
    valid_count = small[18, 0]
    gradient = lax.psum_scatter(flat_grad, ("wide", "narrow"), scatter_dimension=0, tiled=True)
    new_first = BETA_ONE * first_moment + (1.0 - BETA_ONE) * gradient
    new_second = BETA_TWO * second_moment + (1.0 - BETA_TWO) * gradient * gradient
    update = (
        new_first
        / (1.0 - BETA_ONE**STEP)
        / (jnp.sqrt(new_second / (1.0 - BETA_TWO**STEP)) + EPS_ADAM)
        + DECAY_RATE * params
    )
    seg_lower = jnp.array(STARTS + (USED,), jnp.int32)
    seg_upper = jnp.array(STARTS[1:] + (USED, shard_len * devices), jnp.int32)
    position = place * shard_len + lax.iota(jnp.int32, shard_len)
    member_map = (
        (position[:, None] >= seg_lower[None]) & (position[:, None] < seg_upper[None])
    ).astype(F32)
    weight_sq = jnp.dot(params * params, member_map, precision=lax.Precision.HIGHEST)
    update_sq = jnp.dot(update * update, member_map, precision=lax.Precision.HIGHEST)
    weight_sq, update_sq = lax.psum((weight_sq, update_sq), ("wide", "narrow"))
    trust_ratio = jnp.sqrt(weight_sq) / jnp.sqrt(update_sq)
    new_params = (
        params
        - LEARN_RATE * jnp.dot(member_map, trust_ratio, precision=lax.Precision.HIGHEST) * update
    )
    return (new_params, new_first, new_second, loss_sum, valid_count)


def solution(mesh):
    in_specs = (
        P(("wide", "narrow")),
        P(("wide", "narrow")),
        P(("wide", "narrow")),
        P("wide", "narrow", None),
        P("wide", "narrow", None),
        P("wide", "narrow", None),
    )
    out_specs = (P(("wide", "narrow")), P(("wide", "narrow")), P(("wide", "narrow")), P(), P())
    return jax.shard_map(
        on_device, mesh=mesh, in_specs=in_specs, out_specs=out_specs, check_vma=False
    )
```

```python
import functools

import jax
import jax.numpy as jnp
from jax import lax
from jax.experimental import pallas as pl
from jax.experimental.pallas import tpu as pltpu
from jax.sharding import PartitionSpec as P

C1 = 128
C2 = 256
GATE = 64
CLASSES = 3
STEP = 10

EPS_NORM = 1e-05
BETA_ONE = 0.9
BETA_TWO = 0.999
EPS_ADAM = 1e-06
DECAY_RATE = 0.01
LEARN_RATE = 0.3

F32 = jnp.float32
BF16 = jnp.bfloat16
MESH = pl.DeviceIdType.MESH
LANES = 128
TILE = 16 * LANES

LENGTHS = (
    27 * C1,
    27 * C1 * C1,
    27 * C1 * C2,
    C1 * GATE,
    C2 * GATE,
    GATE,
    27 * (C1 + C2) * C1,
    27 * C1 * C1,
    (C1 + 1) * CLASSES,
    4 * C1 + C2,
    4 * C1 + C2,
)
STARTS = tuple(sum(LENGTHS[:i]) for i in range(len(LENGTHS)))
USED = sum(LENGTHS)

FRONT = 32 * LANES - STARTS[1]
SPLIT = STARTS[6]
ROW_IN = STARTS[0] + FRONT
ROW_IN = ROW_IN // LANES
ROW_ENC = (STARTS[1] + FRONT) // LANES
ROW_MID = (STARTS[2] + FRONT) // LANES
ROW_X = (STARTS[3] + FRONT) // LANES
ROW_G = (STARTS[4] + FRONT) // LANES
ROW_PSI = (STARTS[5] + FRONT) // LANES
ROWS_A = -(-(SPLIT + FRONT) // TILE) * 16
ROW_DEC1 = ROWS_A
ROW_DEC2 = ROW_DEC1 + (STARTS[7] - SPLIT) // LANES
ROW_TAIL = ROW_DEC1 + (STARTS[8] - SPLIT) // LANES

DIRS = tuple((dx, dy) for dx in (-1, 0, 1) for dy in (-1, 0, 1) if (dx, dy) != (0, 0))

N_AR = 11
N_HALO = 9
PIECES = 3


def grid_of(nw, nn):
    nx = max(k for k in range(1, nw + 1) if nw % k == 0 and k * k <= nw)
    ny = max(nn // 2, 1)
    return nw // nx, nx, ny, nn // ny


class Layout:
    def __init__(self, shard_len, total):
        self.rows = shard_len // LANES
        self.total = total
        self.turn = -(-SPLIT // shard_len)
        self.shift_a = FRONT // LANES
        self.shift_b = ROWS_A - SPLIT // LANES - 1
        begin = [self.first(p) for p in range(total + 1)]
        edge = []
        for p in range(1, total + 1):
            low = self.rows * p + (self.shift_b if p >= self.turn else self.shift_a)
            edge.append(low // 16)
        self.body = min(edge[p] - begin[p] for p in range(total))
        self.gap = max(begin[p + 1] - begin[p] - self.body for p in range(total))
        self.begin = begin
        self.half = -(-self.body // 2)
        self.fix = 16 * (1 + self.gap)
        self.window = 16 * (1 + self.body + self.gap)
        self.window += 16 * ((self.window // 16) % 2)
        self.weight_rows = 16 * begin[total]
        self.grad_rows = max(16 * (begin[p] - 1) for p in range(total)) + self.window
        self.grad_rows = max(self.grad_rows, self.weight_rows)

    def first(self, p):
        late = (p + self.total - self.turn) // self.total
        return (self.rows * p + self.shift_a + 15 + (self.shift_b + 1 - self.shift_a) * late) // 16


def dot(a, b):
    return jnp.dot(a, b, preferred_element_type=F32)


def dot_nt(a, b):
    return lax.dot_general(a, b, (((1,), (1,)), ((), ())), preferred_element_type=F32)


def dot_tn(a, b):
    return lax.dot_general(a, b, (((0,), (0,)), ((), ())), preferred_element_type=F32)


def iota(shape, dim):
    return lax.broadcasted_iota(jnp.int32, shape, dim)


def onehot(cond):
    return jnp.where(cond, 1.0, 0.0).astype(BF16)


def silu_grad(v, s):
    return s * (1.0 + v * (1.0 - s))


def step_kernel(
    cfg,
    ct_ref,
    lab_ref,
    val_ref,
    param_ref,
    first_ref,
    second_ref,
    param_out,
    first_out,
    second_out,
    scalar_out,
    *scr,
):
    names = cfg["names"]
    s = dict(zip(names, scr))
    w_ref, g_ref = s["weights"], s["grads"]
    lay = cfg["lay"]
    nw, nn = cfg["nw"], cfg["nn"]
    total = nw * nn
    X, Y, Z = cfg["ext"]
    XE, YE = X + 2, Y + 2
    CX, CY, CZ = X // 2, Y // 2, Z // 2
    V = X * Y * Z
    VC = CX * CY * CZ
    voxels = float(V * total)
    coarse_voxels = voxels / 8.0
    w = lax.axis_index("wide")
    n = lax.axis_index("narrow")
    me = w * nn + n

    def dev(p):
        return (p // nn, lax.rem(p, nn))

    barrier = pltpu.get_barrier_semaphore()

    def greet(d, carry):
        pl.semaphore_signal(
            barrier, inc=1, device_id=dev(lax.rem(me + d, total)), device_id_type=MESH
        )
        return carry

    lax.fori_loop(1, total, greet, 0)

    nz, nx, ny, nc = grid_of(nw, nn)
    here = (w // nx, lax.rem(w, nx), n // nc, lax.rem(n, nc))
    sizes = (nz, nx, ny, nc)

    def place(r):
        z, x, y, c = [
            h if d == 0 else lax.rem(h + d % k, k) for h, d, k in zip(here, r, sizes)
        ]
        return z * nx + x, y * nc + c

    def number(r):
        a, b = place(r)
        return a * nn + b

    natural = s["natural"]
    lead = 32
    natural[0:lead] = jnp.zeros((lead, LANES), F32)
    natural[lead : lead + lay.rows] = param_ref[...]
    rest = natural.shape[0] - lead - lay.rows
    natural[lead + lay.rows :] = jnp.zeros((rest, LANES), F32)
    begin = lay.first(me)
    off_a = lay.rows * me + lay.shift_a - 16 * (begin - 1)
    off_b = off_a + lay.shift_b - lay.shift_a
    lane = iota((1, LANES), 1)
    span = 16 * (1 + lay.body + lay.gap)
    row_at = iota((span, LANES), 0) + 16 * (begin - 1)
    as_a = natural[pl.ds(lead - off_a, span), :]
    late = pltpu.roll(natural[pl.ds(lead - off_b, span), :], LANES // 2, 1)
    early = pltpu.roll(natural[pl.ds(lead - off_b - 1, span), :], LANES // 2, 1)
    as_b = jnp.where(lane < LANES // 2, early, late)
    share = jnp.where(row_at < ROWS_A, as_a, as_b).astype(BF16)
    fix = s["fix"]
    body = 16 * lay.body

    def at_tile(t):
        return pl.multiple_of(16 * t, 16)

    w_ref[pl.ds(at_tile(begin), body), :] = share[16 : 16 + body]
    fix[me] = jnp.concatenate([share[0:16], share[16 + body : 16 + body + 16 * lay.gap]], 0)
    pl.semaphore_wait(barrier, total - 1)

    gather_send, gather_recv = s["gather_send"], s["gather_recv"]
    sent = [0] * PIECES

    def flat_id(r):
        z, x, y, c = [d % k for d, k in zip(r, sizes)]
        return ((z * nx + x) * ny + y) * nc + c

    def piece_ref(r, piece):
        p = number(r)
        if piece == 2:
            return fix.at[p]
        lo = 0 if piece == 0 else lay.half
        size = lay.half if piece == 0 else lay.body - lay.half
        return w_ref.at[pl.ds(at_tile(lay.first(p) + lo), 16 * size)]

    def gather_copy(r, d, piece):
        ref = piece_ref(r, piece)
        there = tuple(a - b for a, b in zip(r, d))
        return pltpu.make_async_remote_copy(
            ref,
            ref,
            gather_send.at[piece],
            gather_recv.at[flat_id(there), piece],
            device_id=place(d),
            device_id_type=MESH,
        )

    def gather_push(r, dests, pieces):
        for d in dests:
            for piece in pieces:
                gather_copy(r, d, piece).start()
                sent[piece] += 1

    def gather_take(r):
        for piece in range(PIECES):
            gather_copy(r, (0, 0, 0, 0), piece).wait_recv()

    along_z = [(k, 0, 0, 0) for k in range(1, nz)]
    along_x = [(0, k, 0, 0) for k in range(1, nx)]
    along_y = [(0, 0, k, 0) for k in range(1, ny)]
    sibling = [(0, 0, 0, k) for k in range(1, nc)]
    every = (0, 1, 2)
    gather_push((0, 0, 0, 0), along_x + along_y + along_z + sibling, every)
    for kz in range(nz):
        if kz:
            gather_take((kz, 0, 0, 0))
            gather_push((kz, 0, 0, 0), along_x + along_y + sibling, every)
        for kx in range(1, nx):
            gather_take((kz, kx, 0, 0))
            gather_push((kz, kx, 0, 0), along_y, (0, 2))
            gather_push((kz, kx, 0, 0), sibling, every)
        for ky in range(1, ny):
            gather_take((kz, 0, ky, 0))
            gather_push((kz, 0, ky, 0), along_x, (1,))
            gather_push((kz, 0, ky, 0), sibling, every)
    for kz in range(nz):
        for kx in range(1, nx):
            for ky in range(1, ny):
                gather_take((kz, kx, ky, 0))
                gather_push((kz, kx, ky, 0), sibling, every)
    for kz in range(nz):
        for kx in range(nx):
            for ky in range(ny):
                for kc in range(1, nc):
                    gather_take((kz, kx, ky, kc))
    for p in range(total):
        tile = lay.begin[p] + lay.body
        if p == 0:
            w_ref[16 * (lay.begin[0] - 1) : 16 * lay.begin[0]] = fix[0, 0:16]
        for i in range(lay.begin[p + 1] - tile):
            part = fix[p, 16 * (1 + i) : 16 * (2 + i)]
            if tile + i == lay.begin[p + 1] - 1 and p + 1 < total:
                part = part + fix[p + 1, 0:16]
            w_ref[16 * (tile + i) : 16 * (tile + i + 1)] = part

    def gather_end():
        for piece, count in enumerate(sent):
            if piece == 2:
                ref = fix
                unit = 1
            else:
                ref = w_ref
                unit = 16 * (lay.half if piece == 0 else lay.body - lay.half)
            most = ref.shape[0] // unit
            while count:
                k = min(count, most)
                whole = ref.at[pl.ds(0, k * unit)]
                pltpu.make_async_remote_copy(
                    whole,
                    whole,
                    gather_send.at[piece],
                    gather_recv.at[0, piece],
                    device_id=(w, n),
                    device_id_type=MESH,
                ).wait_send()
                count -= k

    cc, dx_in, dy_in = s["red_c"], s["red_dx"], s["red_dy"]
    ex_in, ey_in, zz_in = s["red_ex"], s["red_ey"], s["red_z"]
    red_send, red_recv = s["red_send"], s["red_recv"]
    win_rows = lay.window
    mid_row = win_rows // 2
    halves = (pl.ds(0, mid_row), pl.ds(mid_row, mid_row))
    started = []

    def grad_window(r_abs_z, rx, ry, rc):
        x = lax.rem(here[1] + rx, nx) if rx else here[1]
        y = lax.rem(here[2] + ry, ny) if ry else here[2]
        c = lax.rem(here[3] + rc, nc) if rc else here[3]
        p = (r_abs_z * nx + x) * nn + y * nc + c
        return pl.ds(at_tile(lay.first(p) - 1), win_rows)

    tags = {}

    def tag(key):
        return tags.setdefault(key, len(tags))

    def red_copy(src, dst, key, d):
        i = tag(key)
        return pltpu.make_async_remote_copy(
            src, dst, red_send.at[i], red_recv.at[i], device_id=place(d), device_id_type=MESH
        )

    def red_go(*a):
        copy = red_copy(*a)
        copy.start()
        started.append(copy)

    def red_one(zd, rx, ry):
        return [
            (g_ref.at[grad_window(zd, rx, ry, k)], cc.at[zd, rx, ry, k - 1], (1, zd, rx, ry, k), (0, 0, 0, k))
            for k in range(1, nc)
        ]

    def others(size):
        return range(1, size)

    def red_two(zd):
        moves = []
        for rx in others(nx):
            for ry in others(ny):
                moves.append(
                    (cc.at[zd, rx, ry, 0, halves[0]], dx_in.at[zd, nx - rx - 1, ry - 1],
                     (2, zd, nx - rx, ry, 0), (0, rx, 0, 0))
                )
                moves.append(
                    (cc.at[zd, rx, ry, 0, halves[1]], dy_in.at[zd, rx - 1, ny - ry - 1],
                     (2, zd, rx, ny - ry, 1), (0, 0, ry, 0))
                )
        return moves

    def red_three(zd):
        moves = []
        for rx in others(nx):
            moves.append((cc.at[zd, rx, 0, 0], ex_in.at[zd, nx - rx - 1], (3, zd, nx - rx, 0), (0, rx, 0, 0)))
        for ry in others(ny):
            moves.append((cc.at[zd, 0, ry, 0], ey_in.at[zd, ny - ry - 1], (3, zd, 0, ny - ry), (0, 0, ry, 0)))
        return moves

    def red_start_one(planes):
        for zd in planes:
            for rx in range(nx):
                for ry in range(ny):
                    for move in red_one(zd, rx, ry):
                        red_go(*move)

    def red_end_one(planes):
        for zd in planes:
            for rx in range(nx):
                for ry in range(ny):
                    for move in red_one(zd, rx, ry):
                        red_copy(*move).wait_recv()
                    total_w = g_ref[grad_window(zd, rx, ry, 0), :].astype(F32)
                    for k in range(1, nc):
                        total_w = total_w + cc[zd, rx, ry, k - 1].astype(F32)
                    cc[zd, rx, ry, 0] = total_w.astype(BF16)
            for move in red_two(zd):
                red_go(*move)

    def red_end_two(planes):
        for zd in planes:
            for move in red_two(zd):
                red_copy(*move).wait_recv()
            for ry in others(ny):
                part = cc[zd, 0, ry, 0, halves[0]].astype(F32)
                for sx in others(nx):
                    part = part + dx_in[zd, sx - 1, ry - 1].astype(F32)
                cc[zd, 0, ry, 0, halves[0]] = part.astype(BF16)
            for rx in others(nx):
                part = cc[zd, rx, 0, 0, halves[1]].astype(F32)
                for sy in others(ny):
                    part = part + dy_in[zd, rx - 1, sy - 1].astype(F32)
                cc[zd, rx, 0, 0, halves[1]] = part.astype(BF16)
            for move in red_three(zd):
                red_go(*move)

    def red_last(zd, k):
        return pltpu.make_async_remote_copy(
            cc.at[zd, 0, 0, 0],
            zz_in.at[nz - k - 1],
            red_send.at[tag((4, zd))],
            red_recv.at[tag((5, nz - k))],
            device_id=place((k, 0, 0, 0)),
            device_id_type=MESH,
        )

    def red_end_three(planes):
        for zd in planes:
            for move in red_three(zd):
                red_copy(*move).wait_recv()
            part = cc[zd, 0, 0, 0].astype(F32)
            for sx in others(nx):
                part = part + ex_in[zd, sx - 1].astype(F32)
            for sy in others(ny):
                part = part + ey_in[zd, sy - 1].astype(F32)
            cc[zd, 0, 0, 0] = part.astype(BF16)
            for k in others(nz):

                @pl.when(lax.rem(here[0] + k, nz) == zd)
                def _():
                    red_last(zd, k).start()

    acc = s["acc"]

    def red_end_last(planes):
        for zd in planes:

            @pl.when(here[0] == zd)
            def _():
                part = cc[zd, 0, 0, 0].astype(F32)
                for k in others(nz):
                    red_last(zd, nz - k).wait_recv()
                for k in others(nz):
                    part = part + zz_in[k - 1].astype(F32)
                acc[16 : 16 + win_rows] = part

    def red_finish():
        for copy in started:
            copy.wait_send()
        for zd in range(nz):

            @pl.when(here[0] != zd)
            def _():
                red_last(zd, 1).wait_send()

    slots, ar_send, ar_recv = s["slots"], s["ar_send"], s["ar_recv"]

    def ar_start(r, rows):
        rows = list(rows) + [jnp.zeros((1, LANES), F32)] * (4 - len(rows))
        slots[r, me] = jnp.concatenate(rows, 0)

        def push(d, carry):
            pltpu.make_async_remote_copy(
                slots.at[r, me],
                slots.at[r, me],
                ar_send.at[r],
                ar_recv.at[r],
                device_id=dev(lax.rem(me + d, total)),
                device_id_type=MESH,
            ).start()
            return carry

        lax.fori_loop(1, total, push, 0)

    def ar_whole(r):
        others = slots.at[r, pl.ds(0, total - 1)]
        return pltpu.make_async_remote_copy(
            others, others, ar_send.at[r], ar_recv.at[r], device_id=(w, n), device_id_type=MESH
        )

    def ar_wait(r):
        ar_whole(r).wait_recv()
        return jnp.sum(slots[r], axis=0)

    side, side_send, side_recv = s["side"], s["side_send"], s["side_recv"]

    def side_start(rows):
        rows = list(rows) + [jnp.zeros((1, LANES), F32)] * (8 - len(rows))
        side[me] = jnp.concatenate(rows, 0)

        def push(d, carry):
            pltpu.make_async_remote_copy(
                side.at[me],
                side.at[me],
                side_send,
                side_recv,
                device_id=dev(lax.rem(me + d, total)),
                device_id_type=MESH,
            ).start()
            return carry

        lax.fori_loop(1, total, push, 0)

    def side_whole():
        others = side.at[pl.ds(0, total - 1)]
        return pltpu.make_async_remote_copy(
            others, others, side_send, side_recv, device_id=(w, n), device_id_type=MESH
        )

    halo_send, halo_recv = s["halo_send"], s["halo_recv"]

    def halo_copy(h, ref, i):
        dx, dy = DIRS[i]
        ex, ey = ref.shape[0] - 2, ref.shape[1] - 2

        def source(d, size):
            return pl.ds(1, size) if d == 0 else pl.ds(size if d > 0 else 1, 1)

        def target(d, size):
            return pl.ds(1, size) if d == 0 else pl.ds(0 if d > 0 else size + 1, 1)

        return pltpu.make_async_remote_copy(
            ref.at[source(dx, ex), source(dy, ey)],
            ref.at[target(dx, ex), target(dy, ey)],
            halo_send.at[h, i],
            halo_recv.at[h, i],
            device_id=(lax.rem(w + dx + nw, nw), lax.rem(n + dy + nn, nn)),
            device_id_type=MESH,
        )

    def halo_start(h, ref):
        for i in range(8):
            halo_copy(h, ref, i).start()

    def halo_wait(h, ref):
        for i in range(8):
            halo_copy(h, ref, i).wait_recv()

    def clear_edges(ref, depth):
        ex, ey = ref.shape[0], ref.shape[1]

        @pl.when(w == 0)
        def _():
            ref[0:depth] = jnp.zeros((depth,) + ref.shape[1:], ref.dtype)

        @pl.when(w == nw - 1)
        def _():
            ref[ex - depth : ex] = jnp.zeros((depth,) + ref.shape[1:], ref.dtype)

        @pl.when(n == 0)
        def _():
            ref[:, 0:depth] = jnp.zeros((ex, depth) + ref.shape[2:], ref.dtype)

        @pl.when(n == nn - 1)
        def _():
            ref[:, ey - depth : ey] = jnp.zeros((ex, depth) + ref.shape[2:], ref.dtype)

    def z_three(flat, length):
        rows = flat.shape[0]
        at = jnp.bitwise_and(iota(flat.shape, 0), length - 1)
        before = jnp.where(at == 0, 0.0, pltpu.roll(flat, 1, 0))
        after = jnp.where(at == length - 1, 0.0, pltpu.roll(flat, rows - 1, 0))
        return before.astype(BF16), flat.astype(BF16), after.astype(BF16)

    def put_three(ref, flat, base, stride):
        shape = ref.shape[:3] + (LANES,)
        for c, part in enumerate(z_three(flat, ref.shape[2])):
            lo = c * stride + base
            ref[:, :, :, lo : lo + LANES] = part.reshape(shape)

    def merge_frame(full, low):
        ex, ey = full.shape[0], full.shape[1]
        full[0] = low[0].astype(F32)
        full[ex - 1] = low[ex - 1].astype(F32)
        full[1 : ex - 1, 0] = low[1 : ex - 1, 0].astype(F32)
        full[1 : ex - 1, ey - 1] = low[1 : ex - 1, ey - 1].astype(F32)

    def conv(ref, weight, row0, ext):
        x, y = ext
        rows = x * y * ref.shape[2]
        depth = ref.shape[3]
        acc = None
        for ab in range(9):
            a, b = ab // 3, ab % 3
            window = ref[a : a + x, b : b + y].reshape(rows, depth)
            part = dot(window, weight[row0 + ab * depth : row0 + (ab + 1) * depth, :])
            acc = part if acc is None else acc + part
        return acc

    def conv_back(ref, weight, row0, cin, cout, ext):
        x, y = ext
        rows = x * y * ref.shape[2]
        acc = None
        for ab in range(9):
            a, b = ab // 3, ab % 3
            for c in range(3):
                window = ref[a : a + x, b : b + y, :, c * cout : (c + 1) * cout]
                tap = 26 - (3 * ab + c)
                part = dot_nt(
                    window.reshape(rows, cout),
                    weight[row0 + tap * cin : row0 + (tap + 1) * cin, :],
                )
                acc = part if acc is None else acc + part
        return acc

    def conv_grad(ref, low, row0, ext):
        x, y = ext
        rows = x * y * ref.shape[2]
        depth = ref.shape[3]
        for ab in range(9):
            a, b = ab // 3, ab % 3
            window = ref[a : a + x, b : b + y].reshape(rows, depth)
            g_ref[row0 + ab * depth : row0 + (ab + 1) * depth, :] = dot_tn(window, low).astype(BF16)

    def col_sum(v):
        return jnp.sum(v, axis=0, keepdims=True)

    def own(ref):
        return ref[1 : ref.shape[0] - 1, 1 : ref.shape[1] - 1]

    def flat(v):
        return v.reshape(-1, v.shape[-1])

    pair = s["pair"]

    def pool(v):
        v = v.reshape(X, Y, Z, LANES)
        v = v[0] + v[1]
        v = v.reshape(CY, 2, Z, LANES)
        v = v[:, 0] + v[:, 1]
        pair[0 : CY * Z] = v.reshape(CY * Z, LANES)
        return pair[pl.ds(0, VC, stride=2), :] + pair[pl.ds(1, VC, stride=2), :]

    def spread(v):
        pair[pl.ds(0, VC, stride=2), :] = v
        pair[pl.ds(1, VC, stride=2), :] = v
        u = pair[0 : CY * Z].reshape(CY, 1, Z, LANES)
        u = jnp.broadcast_to(u, (CY, 2, Z, LANES)).reshape(1, Y, Z, LANES)
        return jnp.broadcast_to(u, (X, Y, Z, LANES)).reshape(V, LANES)

    def stats(total_rows, count):
        half = total_rows.shape[0] // 2
        parts = [total_rows[i : i + 1] for i in range(2 * half)]
        mean = jnp.concatenate(parts[:half], 1) / count
        spread_v = jnp.concatenate(parts[half:], 1) / count - mean * mean
        return mean, lax.rsqrt(spread_v + EPS_NORM)

    def last_of(zd):
        low = 16 * (lay.begin[zd * nx * nn] - 1)
        return 2 if low < ROW_MID else 1 if low < ROW_PSI else 0

    wave_a, wave_b, wave_c = [[zd for zd in range(nz) if last_of(zd) == k] for k in range(3)]
    g_ref[0:32] = jnp.zeros((32, LANES), BF16)
    g_ref[ROW_PSI:ROWS_A] = jnp.zeros((ROWS_A - ROW_PSI, LANES), BF16)
    g_ref[ROW_TAIL:] = jnp.zeros((g_ref.shape[0] - ROW_TAIL, LANES), BF16)

    cts, ct_send, ct_recv = s["cts"], s["ct_send"], s["ct_recv"]
    cts[4] = ct_ref[...]

    def ct_copy(i):
        dx, dy = DIRS[i]
        return pltpu.make_async_remote_copy(
            cts.at[4],
            cts.at[3 * (1 - dx) + 1 - dy],
            ct_send.at[i],
            ct_recv.at[i],
            device_id=(lax.rem(w + dx + nw, nw), lax.rem(n + dy + nn, nn)),
            device_id_type=MESH,
        )

    for i in range(8):
        ct_copy(i).start()

    tail = w_ref[ROW_TAIL : ROW_TAIL + 16, :].astype(F32)
    used_rows = CLASSES * (C1 + 1) // LANES
    used_lanes = CLASSES * (C1 + 1) % LANES
    rolled = pltpu.roll(tail, LANES - used_lanes, 1)
    lane_id = iota((1, LANES), 1)

    def tail_row(q):
        r = used_rows + q
        return jnp.where(
            lane_id < LANES - used_lanes, rolled[r : r + 1], rolled[r + 1 : r + 2]
        )

    gains = [tail_row(q) for q in range(6)]
    shifts = [tail_row(6 + q) for q in range(6)]
    gain = [gains[0], gains[1], jnp.concatenate(gains[2:4], 1), gains[4], gains[5]]
    shift = [shifts[0], shifts[1], jnp.concatenate(shifts[2:4], 1), shifts[4], shifts[5]]

    def select_head(j, r):
        return onehot(
            LANES * r + iota((LANES, LANES), 0) == CLASSES * iota((LANES, LANES), 1) + j
        )

    tail_low = tail.astype(BF16)
    head_rows = []
    for j in range(CLASSES):
        row = None
        for r in range(CLASSES):
            part = dot(tail_low, select_head(j, r))[r : r + 1]
            row = part if row is None else row + part
        head_rows.append(row)
    head_t = jnp.concatenate(head_rows + [jnp.zeros((8 - CLASSES, LANES), F32)], 0).astype(BF16)
    bias_row = tail[used_rows : used_rows + 1]
    bias_col = jnp.sum(
        jnp.where(iota((8, LANES), 0) == iota((8, LANES), 1), bias_row, 0.0), axis=1, keepdims=True
    )
    bias_col = jnp.where(iota((8, 1), 0) < CLASSES, bias_col, 0.0)
    psi = w_ref[ROW_PSI : ROW_PSI + 16, :].astype(F32)[0:1]
    psi = jnp.where(lane_id < GATE, psi, 0.0)

    def pick_half(h, rows):
        return onehot(iota((2 * rows, rows), 0) == 2 * iota((2 * rows, rows), 1) + h)

    def widen(block, rows):
        block = block.astype(F32)
        lower = jnp.where(lane_id < GATE, block, 0.0).astype(BF16)
        upper = jnp.where(lane_id < GATE, pltpu.roll(block, GATE, 1), 0.0).astype(BF16)
        both = dot(pick_half(0, rows), lower) + dot(pick_half(1, rows), upper)
        return both.astype(BF16)

    def narrow_back(block, rows):
        low = block.astype(BF16)
        lower = dot_tn(pick_half(0, rows), low)
        upper = dot_tn(pick_half(1, rows), low)
        return (lower + pltpu.roll(upper, GATE, 1)).astype(BF16)

    w_x = widen(w_ref[ROW_X : ROW_X + C1 // 2, :], C1 // 2)
    w_g = widen(w_ref[ROW_G : ROW_G + C2 // 2, :], C2 // 2)

    front = w_ref[0:32, :].astype(F32)
    we = s["we"]
    for ab in range(9):
        taps = [
            jnp.broadcast_to(front[ROW_IN + 3 * ab + c : ROW_IN + 3 * ab + c + 1], (Z, LANES))
            for c in range(3)
        ]
        taps.append(jnp.zeros((LANES - 3 * Z, LANES), F32))
        we[ab * LANES : (ab + 1) * LANES] = jnp.concatenate(taps, 0).astype(BF16)

    shuffle = onehot(
        iota((C2, C2), 1)
        == jnp.bitwise_and(iota((C2, C2), 0), 1) * C1 + lax.shift_right_logical(iota((C2, C2), 0), 1)
    )
    wm = s["wm"]
    for tap in range(27):
        part = dot_tn(shuffle, w_ref[ROW_MID + C2 * tap : ROW_MID + C2 * (tap + 1), :]).astype(BF16)
        wm[tap * C1 : (tap + 1) * C1, 0:LANES] = part[0:LANES]
        wm[tap * C1 : (tap + 1) * C1, LANES:C2] = part[LANES:C2]

    valid = val_ref[...]
    count_row = jnp.broadcast_to(jnp.sum(valid, axis=1, keepdims=True), (1, LANES))

    for i in range(8):
        ct_copy(i).wait_recv()

    entry = s["entry"]
    zz, ll = iota((Z, LANES), 0), iota((Z, LANES), 1)
    band = jnp.where((jnp.bitwise_and(ll, Z - 1) == zz + ll // Z - 1) & (ll < 3 * Z), 1.0, 0.0)
    for ex in range(X + 4):
        bx = (ex - 2 + X) // X
        lx = ex - 2 - (bx - 1) * X
        for ey in range(Y + 4):
            by = (ey - 2 + Y) // Y
            ly = ey - 2 - (by - 1) * Y
            row = cts[3 * bx + by, lx * Y + ly : lx * Y + ly + 1]
            entry[ex, ey] = (jnp.broadcast_to(row, (Z, LANES)) * band).astype(BF16)
    clear_edges(entry, 2)
    raw1 = s["raw1"]
    raw1[...] = conv(entry, we, 0, (XE, YE)).reshape(XE, YE, Z, LANES)
    mine = flat(own(raw1))
    ar_start(0, [col_sum(mine), col_sum(mine * mine), count_row])
    sums = ar_wait(0)
    valid_count = sums[2:3, 0:1]
    mean1, inv1 = stats(sums[0:2], voxels)
    v = (flat(raw1[...]) - mean1) * inv1 * gain[0] + shift[0]
    pad1 = s["pad1"]
    put_three(pad1, v * jax.nn.sigmoid(v), 0, C1)
    clear_edges(pad1, 1)

    raw2, low2 = s["raw2"], s["low2"]
    mine = conv(pad1, w_ref, ROW_ENC, (X, Y))
    raw2[1 : XE - 1, 1 : YE - 1] = mine.reshape(X, Y, Z, C1)
    low2[1 : XE - 1, 1 : YE - 1] = mine.astype(BF16).reshape(X, Y, Z, C1)
    ar_start(1, [col_sum(mine), col_sum(mine * mine)])
    halo_start(0, low2)
    sums = ar_wait(1)
    mean2, inv2 = stats(sums[0:2], voxels)
    v = (mine - mean2) * inv2 * gain[1] + shift[1]
    skip_own = v * jax.nn.sigmoid(v)

    pool_in = s["pool_in"]
    pool_in[1 : CX + 1, 1 : CY + 1] = (pool(skip_own) * 0.125).astype(BF16).reshape(CX, CY, CZ, C1)
    halo_start(1, pool_in)
    halo_wait(0, low2)
    merge_frame(raw2, low2)
    v = (flat(raw2[...]) - mean2) * inv2 * gain[1] + shift[1]
    skip = s["skip"]
    skip_all = v * jax.nn.sigmoid(v)
    skip[...] = skip_all.reshape(XE, YE, Z, C1)
    mix = s["mix"]
    mix[...] = dot(skip_all.astype(BF16), w_x).reshape(XE, YE, Z, LANES)
    halo_wait(1, pool_in)
    clear_edges(pool_in, 1)
    pad_mid = s["pad_mid"]
    put_three(pad_mid, flat(pool_in[...].astype(F32)), 0, C1)
    raw3, low3 = s["raw3"], s["low3"]
    mine = conv(pad_mid, wm, 0, (CX, CY))
    raw3[1 : CX + 1, 1 : CY + 1] = mine.reshape(CX, CY, CZ, C2)
    low3[1 : CX + 1, 1 : CY + 1] = mine.astype(BF16).reshape(CX, CY, CZ, C2)
    sum_v, square_v = col_sum(mine), col_sum(mine * mine)
    ar_start(
        2, [sum_v[:, 0:C1], sum_v[:, C1:C2], square_v[:, 0:C1], square_v[:, C1:C2]]
    )
    halo_start(2, low3)
    sums = ar_wait(2)
    mean3, inv3 = stats(sums, coarse_voxels)
    halo_wait(2, low3)
    merge_frame(raw3, low3)
    v = (flat(raw3[...]) - mean3) * inv3 * gain[2] + shift[2]
    coarse = (v * jax.nn.sigmoid(v)).astype(BF16).reshape(CX + 2, CY + 2, CZ, C2)
    coarse_own = flat(coarse[1 : CX + 1, 1 : CY + 1])
    frame = (CY + 2) * CZ
    doubled = onehot(
        iota((2 * frame, frame), 1) == lax.shift_right_logical(iota((2 * frame, frame), 0), 1)
    )
    tall = s["tall"]
    for cx in range(CX + 2):
        tall[cx] = (
            dot(doubled, coarse[cx].reshape(frame, C2)).astype(BF16).reshape(CY + 2, Z, C2)
        )

    def expand(u):
        u = jnp.concatenate([u[(i + 1) // 2 : (i + 1) // 2 + 1] for i in range(XE)], 0)
        return jnp.concatenate([u[:, (j + 1) // 2 : (j + 1) // 2 + 1] for j in range(YE)], 1)

    gate_c = dot(flat(tall[...]), w_g).reshape(CX + 2, CY + 2, Z, LANES)
    mixed_in = flat(mix[...] + expand(gate_c))
    mix[...] = mixed_in.reshape(XE, YE, Z, LANES)
    mixed = mixed_in * jax.nn.sigmoid(mixed_in)
    att = jax.nn.sigmoid(jnp.sum(mixed * psi, axis=1, keepdims=True))
    attention = s["attention"]
    attention[...] = jnp.broadcast_to(att, (XE * YE * Z, LANES)).reshape(XE, YE, Z, LANES)
    pad_join = s["pad_join"]
    put_three(pad_join, flat(skip[...] * attention[...]), 0, C1 + C2)
    for half in range(2):
        piece = flat(tall[:, :, :, half * C1 : (half + 1) * C1].astype(F32))
        for c, part in enumerate(z_three(piece, Z)):
            lo = c * (C1 + C2) + C1 + half * C1
            pad_join[:, :, :, lo : lo + C1] = expand(part.reshape(CX + 2, CY + 2, Z, C1))
    clear_edges(pad_join, 1)

    raw4, low4 = s["raw4"], s["low4"]
    mine = conv(pad_join, w_ref, ROW_DEC1, (X, Y))
    raw4[1 : XE - 1, 1 : YE - 1] = mine.reshape(X, Y, Z, C1)
    low4[1 : XE - 1, 1 : YE - 1] = mine.astype(BF16).reshape(X, Y, Z, C1)
    ar_start(3, [col_sum(mine), col_sum(mine * mine)])
    halo_start(3, low4)
    sums = ar_wait(3)
    mean4, inv4 = stats(sums[0:2], voxels)
    halo_wait(3, low4)
    merge_frame(raw4, low4)
    v = (flat(raw4[...]) - mean4) * inv4 * gain[3] + shift[3]
    pad4 = s["pad4"]
    put_three(pad4, v * jax.nn.sigmoid(v), 0, C1)
    clear_edges(pad4, 1)

    raw5, low5 = s["raw5"], s["low5"]
    mine = conv(pad4, w_ref, ROW_DEC2, (X, Y))
    raw5[1 : XE - 1, 1 : YE - 1] = mine.reshape(X, Y, Z, C1)
    low5[1 : XE - 1, 1 : YE - 1] = mine.astype(BF16).reshape(X, Y, Z, C1)
    ar_start(4, [col_sum(mine), col_sum(mine * mine)])
    halo_start(4, low5)
    sums = ar_wait(4)
    mean5, inv5 = stats(sums[0:2], voxels)
    hat = (mine - mean5) * inv5
    v = hat * gain[4] + shift[4]
    sg = jax.nn.sigmoid(v)
    act = (v * sg).astype(BF16)

    logits = dot_nt(head_t, act) + bias_col
    real = iota((8, V), 0) < CLASSES
    logits = jnp.where(real, logits, -1e30)
    hot = iota((8, V), 0) == lab_ref[...]
    top = jnp.max(logits, axis=0, keepdims=True)
    log_total = top + jnp.log(jnp.sum(jnp.exp(logits - top), axis=0, keepdims=True))
    picked = jnp.sum(jnp.where(hot, logits, 0.0), axis=0, keepdims=True)
    loss = jnp.sum(valid * (log_total - picked), axis=1, keepdims=True)
    probs = jnp.exp(logits - log_total)
    g_logits = valid * (probs - jnp.where(hot, 1.0, 0.0)) / valid_count
    g_low = g_logits.astype(BF16)
    head_grad = dot(g_low, act)
    bias_grad = jnp.sum(g_low.astype(F32), axis=1, keepdims=True)
    bias_line = jnp.sum(
        jnp.where(iota((8, LANES), 0) == iota((8, LANES), 1), bias_grad, 0.0), axis=0, keepdims=True
    )
    dy = dot_tn(g_low, head_t) * silu_grad(v, sg)

    def norm_back(r, h, dy, hat, raw, mean, inv, gain_v, ext, count, names2, extra):
        dyf, dyl = s[names2[0]], s[names2[1]]
        ex, ey = ext[0] + 2, ext[1] + 2
        width = dy.shape[1]
        shaped = dy.reshape(ext + (width,))
        dyf[1 : ex - 1, 1 : ey - 1] = shaped
        dyl[1 : ex - 1, 1 : ey - 1] = shaped.astype(BF16)
        first, second = col_sum(dy), col_sum(dy * hat)
        rows = [first[:, i : i + LANES] for i in range(0, width, LANES)]
        rows += [second[:, i : i + LANES] for i in range(0, width, LANES)]
        ar_start(r, rows + extra)
        halo_start(h, dyl)
        return rows

    def norm_back_end(r, h, raw, mean, inv, gain_v, count, names2):
        dyf, dyl = s[names2[0]], s[names2[1]]
        sums = ar_wait(r)
        halo_wait(h, dyl)
        merge_frame(dyf, dyl)
        width = dyf.shape[3]
        k = width // LANES
        one = jnp.concatenate([sums[i : i + 1] for i in range(k)], 1)
        two = jnp.concatenate([sums[k + i : k + i + 1] for i in range(k)], 1)
        hat_all = (flat(raw[...]) - mean) * inv
        back = inv * gain_v * (flat(dyf[...]) - one / count - hat_all * (two / count))
        return sums, back

    grad_shift, grad_gain = {}, {}
    fine = (X, Y, Z)
    norm_back(5, 5, dy, hat, raw5, mean5, inv5, gain[4], fine, voxels, ("dy5", "dyl5"),
              [jnp.broadcast_to(loss, (1, LANES))])
    halo_wait(4, low5)
    merge_frame(raw5, low5)
    sums, back = norm_back_end(5, 5, raw5, mean5, inv5, gain[4], voxels, ("dy5", "dyl5"))
    grad_shift[4], grad_gain[4] = [sums[0:1]], [sums[1:2]]
    loss_row = sums[2:3]
    dpad = s["dpad5"]
    put_three(dpad, back, 0, C1)
    clear_edges(dpad, 1)
    grad_act = conv_back(dpad, w_ref, ROW_DEC2, C1, C1, (X, Y))
    hat = (flat(own(raw4)) - mean4) * inv4
    v = hat * gain[3] + shift[3]
    dy = grad_act * silu_grad(v, jax.nn.sigmoid(v))
    norm_back(6, 6, dy, hat, raw4, mean4, inv4, gain[3], fine, voxels, ("dy4", "dyl4"), [])
    conv_grad(pad4, flat(own(dpad)[:, :, :, C1 : 2 * C1]), ROW_DEC2, (X, Y))
    sums, back = norm_back_end(6, 6, raw4, mean4, inv4, gain[3], voxels, ("dy4", "dyl4"))
    grad_shift[3], grad_gain[3] = [sums[0:1]], [sums[1:2]]
    dpad = s["dpad4"]
    put_three(dpad, back, 0, C1)
    clear_edges(dpad, 1)
    low_raw4 = flat(own(dpad)[:, :, :, C1 : 2 * C1])
    grad_join = conv_back(dpad, w_ref, ROW_DEC1, C1 + C2, C1, (X, Y))

    grad_gated = grad_join[:, 0:C1]
    skip_own = flat(own(skip))
    att_own = flat(own(attention))
    mixed_own = flat(own(mix))
    sg = jax.nn.sigmoid(mixed_own)
    d_att = jnp.sum(grad_gated * skip_own, axis=1, keepdims=True)
    d_logit = d_att * att_own * (1.0 - att_own)
    psi_grad = col_sum(mixed_own * sg * d_logit)
    d_mixed = d_logit * psi * silu_grad(mixed_own, sg)
    low_fine = d_mixed.astype(BF16)
    low_gc = pool(d_mixed).astype(BF16)
    d_coarse = [
        pool(grad_join[:, C1 : 2 * C1]),
        pool(grad_join[:, 2 * C1 : 3 * C1]),
    ]
    d_coarse = jnp.concatenate(d_coarse, 1) + dot_nt(low_gc, w_g)
    d_coarse = d_coarse.astype(BF16).astype(F32)
    hat = (flat(own(raw3)) - mean3) * inv3
    v = hat * gain[2] + shift[2]
    dy = d_coarse * silu_grad(v, jax.nn.sigmoid(v))
    norm_back(7, 7, dy, hat, raw3, mean3, inv3, gain[2], (CX, CY, CZ), coarse_voxels, ("dy3", "dyl3"), [])
    side_start([head_grad[0:1], head_grad[1:2], head_grad[2:3], bias_line, psi_grad])
    d_skip = s["d_skip"]
    d_skip[...] = grad_gated * att_own + dot_nt(low_fine, w_x)
    conv_grad(pad_join, low_raw4, ROW_DEC1, (X, Y))
    g_ref[ROW_X : ROW_X + C1 // 2, :] = narrow_back(
        dot_tn(skip_own.astype(BF16), low_fine), C1 // 2
    )
    g_ref[ROW_G : ROW_G + C2 // 2, :] = narrow_back(dot_tn(coarse_own, low_gc), C2 // 2)
    red_start_one(wave_a)
    sums, back = norm_back_end(7, 7, raw3, mean3, inv3, gain[2], coarse_voxels, ("dy3", "dyl3"))
    grad_shift[2], grad_gain[2] = [sums[0:1], sums[1:2]], [sums[2:3], sums[3:4]]
    dpad = s["dpad3"]
    put_three(dpad, back[:, 0:C1], 0, C2)
    put_three(dpad, back[:, C1:C2], C1, C2)
    clear_edges(dpad, 1)
    low_raw3 = flat(own(dpad)[:, :, :, C2 : 2 * C2])
    d_pool = conv_back(dpad, wm, 0, C1, C2, (CX, CY))
    grad_skip = d_skip[...] + spread(d_pool) * 0.125
    hat = (flat(own(raw2)) - mean2) * inv2
    v = hat * gain[1] + shift[1]
    dy = grad_skip * silu_grad(v, jax.nn.sigmoid(v))
    norm_back(8, 8, dy, hat, raw2, mean2, inv2, gain[1], fine, voxels, ("dy2", "dyl2"), [])
    for ab in range(9):
        window = pad_mid[ab // 3 : ab // 3 + CX, ab % 3 : ab % 3 + CY].reshape(VC, 3 * C1)
        block = dot_tn(window, low_raw3).astype(BF16)
        for c in range(3):
            stacked = block[c * C1 : (c + 1) * C1]
            stacked = jnp.concatenate([stacked[:, 0:C1], stacked[:, C1:C2]], 0)
            lo = ROW_MID + (3 * ab + c) * C2
            g_ref[lo : lo + C2, :] = dot(shuffle, stacked).astype(BF16)
    red_end_one(wave_a)
    red_start_one(wave_b)
    sums, back = norm_back_end(8, 8, raw2, mean2, inv2, gain[1], voxels, ("dy2", "dyl2"))
    grad_shift[1], grad_gain[1] = [sums[0:1]], [sums[1:2]]
    dpad = s["dpad2"]
    put_three(dpad, back, 0, C1)
    clear_edges(dpad, 1)
    low_raw2 = flat(own(dpad)[:, :, :, C1 : 2 * C1])
    red_end_two(wave_a)
    red_end_one(wave_b)
    grad_act = conv_back(dpad, w_ref, ROW_ENC, C1, C1, (X, Y))
    hat1 = (flat(own(raw1)) - mean1) * inv1
    v = hat1 * gain[0] + shift[0]
    dy = grad_act * silu_grad(v, jax.nn.sigmoid(v))
    ar_start(9, [col_sum(dy), col_sum(dy * hat1)])
    conv_grad(pad1, low_raw2, ROW_ENC, (X, Y))
    red_start_one(wave_c)
    red_end_three(wave_a)
    red_end_two(wave_b)
    sums = ar_wait(9)
    grad_shift[0], grad_gain[0] = [sums[0:1]], [sums[1:2]]
    back = inv1 * gain[0] * (dy - sums[0:1] / voxels - hat1 * (sums[1:2] / voxels))
    low_raw1 = back.astype(BF16)
    in_rows = []
    for ab in range(9):
        a, b = ab // 3, ab % 3
        window = entry[a + 1 : a + 1 + X, b + 1 : b + 1 + Y].reshape(V, LANES)
        block = dot_tn(window, low_raw1)
        for c in range(3):
            in_rows.append(col_sum(block[c * Z : (c + 1) * Z]))
    in_rows = [jnp.zeros((ROW_IN, LANES), F32)] + in_rows
    in_slots, in_send, in_recv = s["in_slots"], s["in_send"], s["in_recv"]
    in_slots[me] = jnp.concatenate(in_rows, 0).astype(BF16)

    def in_copy():
        return pltpu.make_async_remote_copy(
            in_slots.at[me],
            in_slots.at[me],
            in_send,
            in_recv,
            device_id=(0, 0),
            device_id_type=MESH,
        )

    def in_whole():
        others_in = in_slots.at[pl.ds(0, total - 1)]
        return pltpu.make_async_remote_copy(
            others_in, others_in, in_send, in_recv, device_id=(w, n), device_id_type=MESH
        )

    @pl.when(me != 0)
    def _():
        in_copy().start()

    red_end_one(wave_c)
    red_end_last(wave_a)
    red_end_three(wave_b)
    red_end_two(wave_c)

    side_whole().wait_recv()
    small = jnp.sum(side[...], axis=0)
    flat_rows = []
    for r in range(CLASSES):
        row = None
        for j in range(CLASSES):
            part = lax.dot_general(
                small,
                select_head(j, r).astype(F32),
                (((1,), (1,)), ((), ())),
                preferred_element_type=F32,
                precision=lax.Precision.HIGHEST,
            )[j : j + 1]
            row = part if row is None else row + part
        flat_rows.append(row)
    later = []
    for group in (grad_gain, grad_shift):
        for layer in range(5):
            later += group[layer]
    later = [pltpu.roll(row, used_lanes, 1) for row in later]
    flat_rows.append(jnp.where(lane_id < used_lanes, small[3:4], later[0]))
    for q in range(1, 12):
        flat_rows.append(jnp.where(lane_id < used_lanes, later[q - 1], later[q]))
    flat_rows.append(jnp.where(lane_id < used_lanes, later[11], 0.0))
    tail_grad = jnp.concatenate(flat_rows, 0)
    psi_row = jnp.where(lane_id < GATE, small[4:5], 0.0)
    scalar_out[...] = jnp.concatenate(
        [loss_row, jnp.broadcast_to(valid_count, (1, LANES)), jnp.zeros((6, LANES), F32)], 0
    )

    red_end_three(wave_c)
    red_end_last(wave_b)
    red_end_last(wave_c)

    base = 16 * (begin - 1) - 16

    def put_row(row, block):
        at = row - base
        rows = block.shape[0]

        @pl.when((at >= 16) & (at + rows <= 16 + win_rows))
        def _():
            acc[pl.ds(pl.multiple_of(at, 16), rows), :] = block

    put_row(ROW_TAIL, tail_grad)
    put_row(ROW_PSI, jnp.concatenate([psi_row, jnp.zeros((15, LANES), F32)], 0))

    @pl.when(me == 0)
    def _():
        in_whole().wait_recv()
        at = 16 - 16 * (lay.begin[0] - 1)
        acc[at : at + 32] = acc[at : at + 32] + jnp.sum(in_slots[...].astype(F32), axis=0)

    grad_a = acc[pl.ds(16 + off_a, lay.rows), :]
    late = pltpu.roll(acc[pl.ds(16 + off_b + 1, lay.rows), :], LANES // 2, 1)
    early = pltpu.roll(acc[pl.ds(16 + off_b, lay.rows), :], LANES // 2, 1)
    grad_b = jnp.where(lane < LANES // 2, early, late)
    position = (
        me * lay.rows * LANES
        + iota((lay.rows, LANES), 0) * LANES
        + iota((lay.rows, LANES), 1)
    )
    gradient = jnp.where(position < SPLIT, grad_a, grad_b)
    gradient = jnp.where(position < USED, gradient, 0.0)
    params = param_ref[...]
    new_first = BETA_ONE * first_ref[...] + (1.0 - BETA_ONE) * gradient
    new_second = BETA_TWO * second_ref[...] + (1.0 - BETA_TWO) * gradient * gradient
    first_out[...] = new_first
    second_out[...] = new_second
    update = (
        new_first
        / (1.0 - BETA_ONE**STEP)
        / (jnp.sqrt(new_second / (1.0 - BETA_TWO**STEP)) + EPS_ADAM)
        + DECAY_RATE * params
    )
    param_out[...] = update
    limits = STARTS + (USED, total * lay.rows * LANES)
    squares = (params * params, update * update)
    lines = []
    for square in squares:
        for k in range(len(limits) - 1):
            member = (position >= limits[k]) & (position < limits[k + 1])
            lines.append(col_sum(jnp.where(member, square, 0.0)))
    lines = jnp.concatenate(lines, 0)
    lines = jnp.sum(lines, axis=1, keepdims=True)
    k = lines.shape[0]
    line = col_sum(jnp.where(iota((k, LANES), 0) == iota((k, LANES), 1), lines, 0.0))
    ar_start(10, [line])
    sums = ar_wait(10)[0:1]
    parts = len(limits) - 1
    roots = jnp.sqrt(sums)
    scale = jnp.zeros((lay.rows, LANES), F32)
    for k in range(parts):
        member = (position >= limits[k]) & (position < limits[k + 1])
        ratio = roots[:, k : k + 1] / roots[:, parts + k : parts + k + 1]
        scale = jnp.where(member, ratio, scale)
    param_out[...] = param_ref[...] - LEARN_RATE * scale * param_out[...]

    gather_end()
    red_finish()

    @pl.when(me != 0)
    def _():
        in_copy().wait_send()

    for r in range(N_AR):
        ar_whole(r).wait_send()
    side_whole().wait_send()
    for i in range(8):
        ct_copy(i).wait_send()
    for h, name in enumerate(
        ("low2", "pool_in", "low3", "low4", "low5", "dyl5", "dyl4", "dyl3", "dyl2")
    ):
        for i in range(8):
            halo_copy(h, s[name], i).wait_send()


def step_call(nw, nn, ext, ct, lab, val, params, first, second):
    X, Y, Z = ext
    XE, YE = X + 2, Y + 2
    CX, CY, CZ = X // 2, Y // 2, Z // 2
    total = nw * nn
    framed = (XE, YE, Z)
    small = (CX + 2, CY + 2, CZ)
    dma = pltpu.SemaphoreType.DMA
    rows = params.shape[0]
    lay = Layout(rows * LANES, total)
    nz, nx, ny, nc = grid_of(nw, nn)
    ox, oy = max(nx - 1, 1), max(ny - 1, 1)
    n_red = nz * (nx * ny * (nc - 1) + 2 * (nx - 1) * (ny - 1) + nx + ny) + 2 * nz + 8
    low = lambda *shape: pltpu.VMEM(shape, BF16)
    scratch = {
        "weights": low(lay.weight_rows, LANES),
        "grads": low(lay.grad_rows, LANES),
        "natural": pltpu.VMEM((rows + 112, LANES), F32),
        "fix": low(total, lay.fix, LANES),
        "gather_send": dma((PIECES,)),
        "gather_recv": dma((total, PIECES)),
        "red_c": low(nz, nx, ny, nc - 1, lay.window, LANES),
        "red_dx": low(nz, ox, oy, lay.window // 2, LANES),
        "red_dy": low(nz, ox, oy, lay.window // 2, LANES),
        "red_ex": low(nz, ox, lay.window, LANES),
        "red_ey": low(nz, oy, lay.window, LANES),
        "red_z": low(nz, lay.window, LANES),
        "red_send": dma((n_red,)),
        "red_recv": dma((n_red,)),
        "acc": pltpu.VMEM((lay.window + 48, LANES), F32),
        "in_slots": low(total, 32, LANES),
        "in_send": dma,
        "in_recv": dma,
        "slots": pltpu.VMEM((N_AR, total, 4, LANES), F32),
        "ar_send": dma((N_AR,)),
        "ar_recv": dma((N_AR,)),
        "side": pltpu.VMEM((total, 8, LANES), F32),
        "side_send": dma,
        "side_recv": dma,
        "halo_send": dma((N_HALO, 8)),
        "halo_recv": dma((N_HALO, 8)),
        "cts": pltpu.VMEM((9, X * Y, LANES), F32),
        "ct_send": dma((8,)),
        "ct_recv": dma((8,)),
        "pair": pltpu.VMEM((CY * Z, LANES), F32),
        "we": pltpu.VMEM((9 * LANES, LANES), BF16),
        "wm": pltpu.VMEM((27 * C1, C2), BF16),
        "entry": pltpu.VMEM((X + 4, Y + 4, Z, LANES), BF16),
        "raw1": pltpu.VMEM(framed + (C1,), F32),
        "pad1": pltpu.VMEM(framed + (3 * C1,), BF16),
        "raw2": pltpu.VMEM(framed + (C1,), F32),
        "low2": pltpu.VMEM(framed + (C1,), BF16),
        "pool_in": pltpu.VMEM(small + (C1,), BF16),
        "skip": pltpu.VMEM(framed + (C1,), F32),
        "mix": pltpu.VMEM(framed + (LANES,), F32),
        "attention": pltpu.VMEM(framed + (LANES,), F32),
        "pad_mid": pltpu.VMEM(small + (3 * C1,), BF16),
        "raw3": pltpu.VMEM(small + (C2,), F32),
        "low3": pltpu.VMEM(small + (C2,), BF16),
        "tall": pltpu.VMEM((CX + 2, CY + 2, Z, C2), BF16),
        "pad_join": pltpu.VMEM(framed + (3 * (C1 + C2),), BF16),
        "raw4": pltpu.VMEM(framed + (C1,), F32),
        "low4": pltpu.VMEM(framed + (C1,), BF16),
        "pad4": pltpu.VMEM(framed + (3 * C1,), BF16),
        "raw5": pltpu.VMEM(framed + (C1,), F32),
        "low5": pltpu.VMEM(framed + (C1,), BF16),
        "dy5": pltpu.VMEM(framed + (C1,), F32),
        "dyl5": pltpu.VMEM(framed + (C1,), BF16),
        "dpad5": pltpu.VMEM(framed + (3 * C1,), BF16),
        "dy4": pltpu.VMEM(framed + (C1,), F32),
        "dyl4": pltpu.VMEM(framed + (C1,), BF16),
        "dpad4": pltpu.VMEM(framed + (3 * C1,), BF16),
        "dy3": pltpu.VMEM(small + (C2,), F32),
        "dyl3": pltpu.VMEM(small + (C2,), BF16),
        "dpad3": pltpu.VMEM(small + (3 * C2,), BF16),
        "dy2": pltpu.VMEM(framed + (C1,), F32),
        "dyl2": pltpu.VMEM(framed + (C1,), BF16),
        "dpad2": pltpu.VMEM(framed + (3 * C1,), BF16),
        "d_skip": pltpu.VMEM((X * Y * Z, C1), F32),
    }
    cfg = {"nw": nw, "nn": nn, "ext": ext, "names": tuple(scratch), "lay": lay}
    vmem = pl.BlockSpec(memory_space=pltpu.VMEM)
    return pl.pallas_call(
        functools.partial(step_kernel, cfg),
        out_shape=(
            jax.ShapeDtypeStruct((rows, LANES), F32),
            jax.ShapeDtypeStruct((rows, LANES), F32),
            jax.ShapeDtypeStruct((rows, LANES), F32),
            jax.ShapeDtypeStruct((8, LANES), F32),
        ),
        in_specs=[vmem] * 6,
        out_specs=(vmem,) * 4,
        scratch_shapes=list(scratch.values()),
        compiler_params=pltpu.CompilerParams(
            collective_id=0, has_side_effects=True, vmem_limit_bytes=60 * 1024 * 1024
        ),
    )(ct, lab, val, params, first, second)


def on_device(params, first_moment, second_moment, ct_image, labels, valid_mask):
    ext = ct_image.shape
    ct = ct_image.astype(F32).reshape(-1, ext[2])
    ct = jnp.concatenate([ct, ct, ct, jnp.zeros((ct.shape[0], LANES - 3 * ext[2]), F32)], 1)
    new_params, new_first, new_second, scalars = step_call(
        lax.axis_size("wide"),
        lax.axis_size("narrow"),
        ext,
        ct,
        labels.reshape(1, -1),
        valid_mask.astype(F32).reshape(1, -1),
        params.reshape(-1, LANES),
        first_moment.reshape(-1, LANES),
        second_moment.reshape(-1, LANES),
    )
    return (
        new_params.reshape(-1),
        new_first.reshape(-1),
        new_second.reshape(-1),
        scalars[0, 0],
        scalars[1, 0],
    )


def solution(mesh):
    in_specs = (
        P(("wide", "narrow")),
        P(("wide", "narrow")),
        P(("wide", "narrow")),
        P("wide", "narrow", None),
        P("wide", "narrow", None),
        P("wide", "narrow", None),
    )
    out_specs = (P(("wide", "narrow")), P(("wide", "narrow")), P(("wide", "narrow")), P(), P())
    return jax.shard_map(
        on_device, mesh=mesh, in_specs=in_specs, out_specs=out_specs, check_vma=False
    )
```

```python
import functools
import types

import jax
import jax.numpy as jnp
from jax import lax
from jax.experimental import pallas as pl
from jax.experimental.pallas import tpu as pltpu
from jax.sharding import PartitionSpec as P

C1 = 128
C2 = 256
GATE = 64
CLASSES = 3
STEP = 10

EPS_NORM = 1e-05
BETA_ONE = 0.9
BETA_TWO = 0.999
EPS_ADAM = 1e-06
DECAY_RATE = 0.01
LEARN_RATE = 0.3

F32 = jnp.float32
BF16 = jnp.bfloat16
MESH = pl.DeviceIdType.MESH
LANES = 128
TILE = 16 * LANES

LENGTHS = (
    27 * C1,
    27 * C1 * C1,
    27 * C1 * C2,
    C1 * GATE,
    C2 * GATE,
    GATE,
    27 * (C1 + C2) * C1,
    27 * C1 * C1,
    (C1 + 1) * CLASSES,
    4 * C1 + C2,
    4 * C1 + C2,
)
STARTS = tuple(sum(LENGTHS[:i]) for i in range(len(LENGTHS)))
USED = sum(LENGTHS)

FRONT = 32 * LANES - STARTS[1]
SPLIT = STARTS[6]
ROW_IN = STARTS[0] + FRONT
ROW_IN = ROW_IN // LANES
ROW_ENC = (STARTS[1] + FRONT) // LANES
ROW_MID = (STARTS[2] + FRONT) // LANES
ROW_X = (STARTS[3] + FRONT) // LANES
ROW_G = (STARTS[4] + FRONT) // LANES
ROW_PSI = (STARTS[5] + FRONT) // LANES
ROWS_A = -(-(SPLIT + FRONT) // TILE) * 16
ROW_DEC1 = ROWS_A
ROW_DEC2 = ROW_DEC1 + (STARTS[7] - SPLIT) // LANES
ROW_TAIL = ROW_DEC1 + (STARTS[8] - SPLIT) // LANES

DIRS = tuple((dx, dy) for dx in (-1, 0, 1) for dy in (-1, 0, 1) if (dx, dy) != (0, 0))

N_AR = 11
N_HALO = 9
PIECES = 3


def grid_of(nw, nn):
    nx = max(k for k in range(1, nw + 1) if nw % k == 0 and k * k <= nw)
    ny = max(nn // 2, 1)
    return nw // nx, nx, ny, nn // ny


class Layout:
    def __init__(self, shard_len, total):
        self.rows = shard_len // LANES
        self.total = total
        self.turn = -(-SPLIT // shard_len)
        self.shift_a = FRONT // LANES
        self.shift_b = ROWS_A - SPLIT // LANES - 1
        begin = [self.first(p) for p in range(total + 1)]
        edge = []
        for p in range(1, total + 1):
            low = self.rows * p + (self.shift_b if p >= self.turn else self.shift_a)
            edge.append(low // 16)
        self.body = min(edge[p] - begin[p] for p in range(total))
        self.gap = max(begin[p + 1] - begin[p] - self.body for p in range(total))
        self.begin = begin
        self.half = -(-self.body // 2)
        self.fix = 16 * (1 + self.gap)
        self.window = 16 * (1 + self.body + self.gap)
        self.weight_rows = 16 * begin[total]
        self.grad_rows = max(16 * (begin[p] - 1) for p in range(total)) + self.window
        self.grad_rows = max(self.grad_rows, self.weight_rows)

    def first(self, p):
        late = (p + self.total - self.turn) // self.total
        return (self.rows * p + self.shift_a + 15 + (self.shift_b + 1 - self.shift_a) * late) // 16


def dot(a, b):
    return jnp.dot(a, b, preferred_element_type=F32)


def dot_nt(a, b):
    return lax.dot_general(a, b, (((1,), (1,)), ((), ())), preferred_element_type=F32)


def dot_tn(a, b):
    return lax.dot_general(a, b, (((0,), (0,)), ((), ())), preferred_element_type=F32)


def iota(shape, dim):
    return lax.broadcasted_iota(jnp.int32, shape, dim)


def onehot(cond):
    return jnp.where(cond, 1.0, 0.0).astype(BF16)


def silu_grad(v, s):
    return s * (1.0 + v * (1.0 - s))


def step_kernel(
    cfg,
    ct_ref,
    lab_ref,
    val_ref,
    param_ref,
    first_ref,
    second_ref,
    param_out,
    first_out,
    second_out,
    scalar_out,
    *scr,
):
    s = types.SimpleNamespace(**dict(zip(cfg.names, scr)))
    w_ref, g_ref = s.weights, s.grads
    lay = cfg.lay
    nw, nn = cfg.nw, cfg.nn
    total = nw * nn
    X, Y, Z = cfg.ext
    XE, YE = X + 2, Y + 2
    CX, CY, CZ = X // 2, Y // 2, Z // 2
    V = X * Y * Z
    VC = CX * CY * CZ
    voxels = float(V * total)
    coarse_voxels = voxels / 8.0
    w = lax.axis_index("wide")
    n = lax.axis_index("narrow")
    me = w * nn + n

    def dev(p):
        return (p // nn, lax.rem(p, nn))

    barrier = pltpu.get_barrier_semaphore()

    def greet(d, carry):
        pl.semaphore_signal(
            barrier, inc=1, device_id=dev(lax.rem(me + d, total)), device_id_type=MESH
        )
        return carry

    lax.fori_loop(1, total, greet, 0)

    nz, nx, ny, nc = grid_of(nw, nn)
    here = (w // nx, lax.rem(w, nx), n // nc, lax.rem(n, nc))
    sizes = (nz, nx, ny, nc)

    def place(r):
        z, x, y, c = [
            h if d == 0 else lax.rem(h + d % k, k) for h, d, k in zip(here, r, sizes)
        ]
        return z * nx + x, y * nc + c

    def number(zp, r):
        a, b = place((0,) + r)
        return (zp * nx + lax.rem(a, nx)) * nn + b

    natural = s.natural
    lead = 32
    natural[0:lead] = jnp.zeros((lead, LANES), F32)
    natural[lead : lead + lay.rows] = param_ref[...]
    rest = natural.shape[0] - lead - lay.rows
    natural[lead + lay.rows :] = jnp.zeros((rest, LANES), F32)
    begin = lay.first(me)
    off_a = lay.rows * me + lay.shift_a - 16 * (begin - 1)
    off_b = off_a + lay.shift_b - lay.shift_a
    lane = iota((1, LANES), 1)
    span = 16 * (1 + lay.body + lay.gap)
    row_at = iota((span, LANES), 0) + 16 * (begin - 1)
    as_a = natural[pl.ds(lead - off_a, span), :]
    late = pltpu.roll(natural[pl.ds(lead - off_b, span), :], LANES // 2, 1)
    early = pltpu.roll(natural[pl.ds(lead - off_b - 1, span), :], LANES // 2, 1)
    as_b = jnp.where(lane < LANES // 2, early, late)
    share = jnp.where(row_at < ROWS_A, as_a, as_b).astype(BF16)
    fix = s.fix
    body = 16 * lay.body

    def at_tile(t):
        return pl.multiple_of(16 * t, 16)

    w_ref[pl.ds(at_tile(begin), body), :] = share[16 : 16 + body]
    fix[me] = jnp.concatenate([share[0:16], share[16 + body : 16 + body + 16 * lay.gap]], 0)

    gather_send, gather_recv = s.gather_send, s.gather_recv
    sent = [0] * PIECES
    every = (0, 1, 2)

    def flat_id(zp, r):
        x, y, c = [d % k for d, k in zip(r, sizes[1:])]
        return ((zp * nx + x) * ny + y) * nc + c

    def piece_ref(p, piece):
        if piece == 2:
            return fix.at[p]
        lo = 0 if piece == 0 else lay.half
        size = lay.half if piece == 0 else lay.body - lay.half
        return w_ref.at[pl.ds(at_tile(lay.first(p) + lo), 16 * size)]

    def gather_copy(zp, r, d, piece):
        ref = piece_ref(number(zp, r), piece)
        there = tuple(a - b for a, b in zip(r, d[1:]))
        return pltpu.make_async_remote_copy(
            ref,
            ref,
            gather_send.at[piece],
            gather_recv.at[flat_id(zp, there), piece],
            device_id=place(d),
            device_id_type=MESH,
        )

    def gather_push(zp, r, dests, pieces):
        for piece in pieces:
            for d in dests:
                gather_copy(zp, r, d, piece).start()

    def gather_take(zp, r, piece):
        gather_copy(zp, r, (0, 0, 0, 0), piece).wait_recv()

    along_x = [(0, k, 0, 0) for k in range(1, nx)]
    along_y = [(0, 0, k, 0) for k in range(1, ny)]
    sibling = [(0, 0, 0, k) for k in range(1, nc)]
    mine_r = (0, 0, 0)
    for piece in every:
        split = [len(along_y), len(along_x), len(along_x) + len(along_y)][piece]
        sent[piece] = nz * (len(along_x) + len(along_y) + len(sibling))
        first_hop = [(nx - 1) * len(along_y), (ny - 1) * len(along_x), (nx - 1) * len(along_y)]
        sent[piece] += nz * (first_hop[piece] + (nx * ny - 1) * len(sibling))

    onward_send = s.onward_send

    def onward_copy(zp, up, piece):
        ref = piece_ref(number(zp, mine_r), piece)
        return pltpu.make_async_remote_copy(
            ref,
            ref,
            onward_send.at[zp, int(up), piece],
            gather_recv.at[flat_id(zp, mine_r), piece],
            device_id=place((1 if up else nz - 1, 0, 0, 0)),
            device_id_type=MESH,
        )

    def onward(zp, up, piece):
        @pl.when(here[0] < nz - 1 if up else here[0] > 0)
        def _():
            onward_copy(zp, up, piece).start()

    def gather_own():
        for piece in every:
            for up in (True, False):
                onward(here[0], up, piece)
            gather_push(here[0], mine_r, along_x + along_y + sibling, (piece,))

    def at_distance(d, step):
        if d == 0:
            step(here[0], None)
            return

        @pl.when(here[0] - d >= 0)
        def _():
            step(here[0] - d, True)

        @pl.when(here[0] + d < nz)
        def _():
            step(here[0] + d, False)

    def gather_one(zp, up):
        for piece in every:
            gather_take(zp, mine_r, piece)
            onward(zp, up, piece)
            gather_push(zp, mine_r, along_x + along_y + sibling, (piece,))

    def gather_two(zp, up):
        for piece in every:
            for kx in range(1, nx):
                gather_take(zp, (kx, 0, 0), piece)
                if piece != 1:
                    gather_push(zp, (kx, 0, 0), along_y, (piece,))
                gather_push(zp, (kx, 0, 0), sibling, (piece,))
            for ky in range(1, ny):
                gather_take(zp, (0, ky, 0), piece)
                if piece == 1:
                    gather_push(zp, (0, ky, 0), along_x, (piece,))
                gather_push(zp, (0, ky, 0), sibling, (piece,))

    def gather_three(zp, up):
        for piece in every:
            for kx in range(1, nx):
                for ky in range(1, ny):
                    gather_take(zp, (kx, ky, 0), piece)
                    gather_push(zp, (kx, ky, 0), sibling, (piece,))

    def gather_four(zp):
        for kx in range(nx):
            for ky in range(ny):
                for kc in range(1, nc):
                    for piece in every:
                        gather_take(zp, (kx, ky, kc), piece)
        low, high = zp * nx * nn, (zp + 1) * nx * nn
        if zp == 0:
            w_ref[16 * (lay.begin[0] - 1) : 16 * lay.begin[0]] = fix[0, 0:16]
        else:
            put_gap(low - 1)
        for p in range(low, high - (zp < nz - 1)):
            put_gap(p)

    def put_gap(p):
        tile = lay.begin[p] + lay.body
        for i in range(lay.begin[p + 1] - tile):
            part = fix[p, 16 * (1 + i) : 16 * (2 + i)]
            if tile + i == lay.begin[p + 1] - 1 and p + 1 < total:
                part = part + fix[p + 1, 0:16]
            w_ref[16 * (tile + i) : 16 * (tile + i + 1)] = part

    quick, quick_send, quick_recv = s.quick, s.quick_send, s.quick_recv
    shard_len = lay.rows * LANES
    quick_parts = []
    for row, size in ((0, 32), (ROW_TAIL, 16)):
        owner = 0 if row == 0 else STARTS[8] // shard_len
        at = row - 16 * (lay.begin[owner] - 1)
        quick_parts.append((owner, at, size))

    def quick_copy(k, p):
        lo, size = (0, 32) if k == 0 else (32, 16)
        ref = quick.at[pl.ds(lo, size)]
        return pltpu.make_async_remote_copy(
            ref,
            ref,
            quick_send.at[k],
            quick_recv.at[k],
            device_id=dev(p),
            device_id_type=MESH,
        )

    for k, (owner, at, size) in enumerate(quick_parts):

        @pl.when(me == owner)
        def _():
            lo = 0 if k == 0 else 32
            quick[lo : lo + size] = share[at : at + size]

    pl.semaphore_wait(barrier, total - 1)
    for k, (owner, at, size) in enumerate(quick_parts):

        @pl.when(me == owner)
        def _():
            def push(d, carry):
                quick_copy(k, lax.rem(me + d, total)).start()
                return carry

            lax.fori_loop(1, total, push, 0)

    def quick_wait():
        for k, (owner, at, size) in enumerate(quick_parts):

            @pl.when(me != owner)
            def _():
                quick_copy(k, me).wait_recv()

    def quick_end():
        for k, (owner, at, size) in enumerate(quick_parts):

            @pl.when(me == owner)
            def _():
                whole = w_ref.at[pl.ds(0, (total - 1) * size)]
                pltpu.make_async_remote_copy(
                    whole,
                    whole,
                    quick_send.at[k],
                    quick_recv.at[k],
                    device_id=(w, n),
                    device_id_type=MESH,
                ).wait_send()

    quarter = nz // 4
    quarters = [range(k * quarter, (k + 1) * quarter) for k in range(4)]

    def gather(step, k):
        if step is gather_four:
            for zp in quarters[k]:
                step(zp)
            return
        for d in quarters[k]:
            at_distance(d, step)

    def step(what, d):
        if quarter == 1:
            gather(what, d)

    gather_own()

    def gather_end():
        for piece, count in enumerate(sent):
            if piece == 2:
                ref = fix
                unit = 1
            else:
                ref = w_ref
                unit = 16 * (lay.half if piece == 0 else lay.body - lay.half)
            most = ref.shape[0] // unit
            while count:
                k = min(count, most)
                whole = ref.at[pl.ds(0, k * unit)]
                pltpu.make_async_remote_copy(
                    whole,
                    whole,
                    gather_send.at[piece],
                    gather_recv.at[0, piece],
                    device_id=(w, n),
                    device_id_type=MESH,
                ).wait_send()
                count -= k

    cc, dx_in, dy_in = s.red_c, s.red_dx, s.red_dy
    ex_in, ey_in, zz_in = s.red_ex, s.red_ey, s.red_z
    win_rows = lay.window
    mid_row = 16 * (-(-win_rows // 32))
    halves = (pl.ds(0, mid_row), pl.ds(mid_row, win_rows - mid_row))
    acc = s.acc
    sent_red = []

    def grad_window(zd, xd, ry, rc):
        y = lax.rem(here[2] + ry, ny) if ry else here[2]
        c = lax.rem(here[3] + rc, nc) if rc else here[3]
        p = (zd * nx + xd) * nn + y * nc + c
        return pl.ds(at_tile(lay.first(p) - 1), win_rows)

    def red_copy(step, at_send, at_recv, source, target, to):
        return pltpu.make_async_remote_copy(
            source,
            target,
            step[0].at[at_send],
            step[1].at[at_recv],
            device_id=to,
            device_id_type=MESH,
        )

    def in_place(zd, xd):
        return here[1] == xd

    def off_place(zd, xd):
        return here[1] != xd

    def red_go(cond, copy):
        if cond is None:
            copy.start()
        else:

            @pl.when(cond)
            def _():
                copy.start()

        sent_red.append((cond, copy))

    def others(size):
        return range(1, size)

    def copy_core(zd, xd, ry, k):
        return red_copy(
            (s.send_core, s.recv_core),
            (zd, xd, ry, k - 1),
            (zd, xd, ry, k - 1),
            g_ref.at[grad_window(zd, xd, ry, k)],
            cc.at[zd, xd, ry, k - 1],
            place((0, 0, 0, k)),
        )

    def copy_dx(zd, xd, ry, xs):
        return red_copy(
            (s.send_dx, s.recv_dx),
            (zd, xd, ry - 1),
            (zd, xs, ry - 1),
            cc.at[zd, xd, ry, 0, halves[0]],
            dx_in.at[zd, xs, ry - 1],
            (here[0] * nx + xd, n),
        )

    def copy_dy(zd, xd, ry):
        return red_copy(
            (s.send_dy, s.recv_dy),
            (zd, xd, ry - 1),
            (zd, xd, ny - ry - 1),
            cc.at[zd, xd, ry, 0, halves[1]],
            dy_in.at[zd, xd, ny - ry - 1],
            place((0, 0, ry, 0)),
        )

    def copy_ex(zd, xd, xs):
        return red_copy(
            (s.send_ex, s.recv_ex), (zd, xd), (zd, xs), cc.at[zd, xd, 0, 0], ex_in.at[zd, xs], (here[0] * nx + xd, n)
        )

    def copy_ey(zd, xd, ry):
        return red_copy(
            (s.send_ey, s.recv_ey),
            (zd, xd, ry - 1),
            (zd, ny - ry - 1),
            cc.at[zd, xd, ry, 0],
            ey_in.at[zd, ny - ry - 1],
            place((0, 0, ry, 0)),
        )

    def way_along_z(zd):
        if nz != 4:
            return [], [zs for zs in range(nz) if zs != zd], None, None
        lead = 2 if zd < 2 else 1
        far = 3 if zd < 2 else 0
        near = zd + 1 - 2 * (zd % 2)
        return [(far, lead)], [near, lead], far, lead

    def copy_z(zd, xd, zs, to, h):
        return red_copy(
            (s.send_z, s.recv_z),
            (zd, xd, h),
            (zd, zs, h),
            cc.at[zd, xd, 0, 0, halves[h]],
            zz_in.at[zd if nz == 4 else 0, zs, halves[h]],
            (to * nx + xd, n),
        )

    def red_one(units):
        for zd, xd in units:
            for ry in range(ny):
                for k in others(nc):
                    red_go(None, copy_core(zd, xd, ry, k))

    def red_two(units):
        for zd, xd in units:
            for ry in reversed(range(ny)):
                part = g_ref[grad_window(zd, xd, ry, 0), :]
                for k in others(nc):
                    copy_core(zd, xd, ry, k).wait_recv()
                    part = part + cc[zd, xd, ry, k - 1]
                cc[zd, xd, ry, 0] = part
                if ry:
                    red_go(off_place(zd, xd), copy_dx(zd, xd, ry, here[1]))
                    red_go(off_place(zd, xd), copy_dy(zd, xd, ry))

    def red_three(units):
        for zd, xd in units:

            @pl.when(in_place(zd, xd))
            def _():
                for ry in others(ny):
                    part = cc[zd, xd, ry, 0, halves[0]]
                    for xs in range(nx):
                        if xs != xd:
                            copy_dx(zd, xd, ry, xs).wait_recv()
                            part = part + dx_in[zd, xs, ry - 1]
                    cc[zd, xd, ry, 0, halves[0]] = part
                    copy_ey(zd, xd, ry).start()

            @pl.when(off_place(zd, xd))
            def _():
                part = cc[zd, xd, 0, 0, halves[1]]
                for sy in others(ny):
                    copy_dy(zd, xd, ny - sy).wait_recv()
                    part = part + dy_in[zd, xd, sy - 1]
                cc[zd, xd, 0, 0, halves[1]] = part
                copy_ex(zd, xd, here[1]).start()

            for ry in others(ny):
                sent_red.append((in_place(zd, xd), copy_ey(zd, xd, ry)))
            sent_red.append((off_place(zd, xd), copy_ex(zd, xd, here[1])))

    def red_four(units):
        for zd, xd in units:

            @pl.when(in_place(zd, xd))
            def _():
                part = cc[zd, xd, 0, 0].astype(F32)
                for xs in range(nx):
                    if xs != xd:
                        copy_ex(zd, xd, xs).wait_recv()
                        part = part + ex_in[zd, xs].astype(F32)
                for sy in others(ny):
                    copy_ey(zd, xd, ny - sy).wait_recv()
                    part = part + ey_in[zd, sy - 1].astype(F32)
                cc[zd, xd, 0, 0] = part.astype(BF16)
                hops, ends, far, lead = way_along_z(zd)
                for h in range(2):
                    for zs in range(nz):
                        if zs in (zd, lead):
                            continue

                        @pl.when(here[0] == zs)
                        def _():
                            copy_z(zd, xd, zs, lead if zs == far else zd, h).start()

            hops, ends, far, lead = way_along_z(zd)
            for zs in range(nz):
                if zs != zd:
                    for h in range(2):
                        to = lead if zs == far else zd
                        sent_red.append(
                            (in_place(zd, xd) & (here[0] == zs), copy_z(zd, xd, zs, to, h))
                        )

    def red_between(units):
        for zd, xd in units:
            hops, ends, far, lead = way_along_z(zd)
            if not hops:
                continue

            @pl.when(in_place(zd, xd) & (here[0] == lead))
            def _():
                for h in range(2):
                    copy_z(zd, xd, far, lead, h).wait_recv()
                    part = cc[zd, xd, 0, 0, halves[h]]
                    cc[zd, xd, 0, 0, halves[h]] = part + zz_in[zd, far, halves[h]]
                    copy_z(zd, xd, lead, zd, h).start()

    def red_five(units):
        for zd, xd in units:

            @pl.when(in_place(zd, xd) & (here[0] == zd))
            def _():
                part = cc[zd, xd, 0, 0].astype(F32)
                hops, ends, far, lead = way_along_z(zd)
                for zs in ends:
                    for h in range(2):
                        copy_z(zd, xd, zs, zd, h).wait_recv()
                    part = part + zz_in[zd if nz == 4 else 0, zs].astype(F32)
                acc[16 : 16 + win_rows] = part

    def red_finish():
        for cond, copy in sent_red:
            if cond is None:
                copy.wait_send()
            else:

                @pl.when(cond)
                def _():
                    copy.wait_send()

    slots, ar_send, ar_recv = s.slots, s.ar_send, s.ar_recv

    def to_all(copy):
        if total > 64:

            def push(d, carry):
                copy(dev(lax.rem(me + d, total))).start()
                return carry

            lax.fori_loop(1, total, push, 0)
            return
        upper = (2 * here[0]) // nz
        for i in range(nz):
            zp = (1 - upper) * (nz - 1 - i) + upper * i
            for rx in reversed(range(nx)):
                for ry in reversed(range(ny)):
                    for rc in reversed(range(nc)):
                        a, b = place((0, rx, ry, rc))
                        target = (zp * nx + lax.rem(a, nx), b)
                        if rx or ry or rc:
                            copy(target).start()
                        else:

                            @pl.when(zp != here[0])
                            def _():
                                copy(target).start()

    def ar_start(r, rows):
        rows = list(rows) + [jnp.zeros((1, LANES), F32)] * (4 - len(rows))
        slots[r, me] = jnp.concatenate(rows, 0)

        def copy(target):
            return pltpu.make_async_remote_copy(
                slots.at[r, me],
                slots.at[r, me],
                ar_send.at[r],
                ar_recv.at[r],
                device_id=target,
                device_id_type=MESH,
            )

        to_all(copy)

    def ar_whole(r):
        others = slots.at[r, pl.ds(0, total - 1)]
        return pltpu.make_async_remote_copy(
            others, others, ar_send.at[r], ar_recv.at[r], device_id=(w, n), device_id_type=MESH
        )

    def ar_wait(r):
        ar_whole(r).wait_recv()
        return jnp.sum(slots[r], axis=0)

    side, side_send, side_recv = s.side, s.side_send, s.side_recv

    def side_start(rows):
        rows = list(rows) + [jnp.zeros((1, LANES), F32)] * (8 - len(rows))
        side[me] = jnp.concatenate(rows, 0)

        def copy(target):
            return pltpu.make_async_remote_copy(
                side.at[me],
                side.at[me],
                side_send,
                side_recv,
                device_id=target,
                device_id_type=MESH,
            )

        to_all(copy)

    def side_whole():
        others = side.at[pl.ds(0, total - 1)]
        return pltpu.make_async_remote_copy(
            others, others, side_send, side_recv, device_id=(w, n), device_id_type=MESH
        )

    halo_send, halo_recv = s.halo_send, s.halo_recv

    def halo_copy(h, ref, i):
        dx, dy = DIRS[i]
        ex, ey = ref.shape[0] - 2, ref.shape[1] - 2

        def source(d, size):
            return pl.ds(1, size) if d == 0 else pl.ds(size if d > 0 else 1, 1)

        def target(d, size):
            return pl.ds(1, size) if d == 0 else pl.ds(0 if d > 0 else size + 1, 1)

        return pltpu.make_async_remote_copy(
            ref.at[source(dx, ex), source(dy, ey)],
            ref.at[target(dx, ex), target(dy, ey)],
            halo_send.at[h, i],
            halo_recv.at[h, i],
            device_id=(lax.rem(w + dx + nw, nw), lax.rem(n + dy + nn, nn)),
            device_id_type=MESH,
        )

    def halo_start(h, ref):
        for i in range(8):
            halo_copy(h, ref, i).start()

    def halo_wait(h, ref):
        for i in range(8):
            halo_copy(h, ref, i).wait_recv()

    def clear_edges(ref, depth):
        ex, ey = ref.shape[0], ref.shape[1]

        @pl.when(w == 0)
        def _():
            ref[0:depth] = jnp.zeros((depth,) + ref.shape[1:], ref.dtype)

        @pl.when(w == nw - 1)
        def _():
            ref[ex - depth : ex] = jnp.zeros((depth,) + ref.shape[1:], ref.dtype)

        @pl.when(n == 0)
        def _():
            ref[:, 0:depth] = jnp.zeros((ex, depth) + ref.shape[2:], ref.dtype)

        @pl.when(n == nn - 1)
        def _():
            ref[:, ey - depth : ey] = jnp.zeros((ex, depth) + ref.shape[2:], ref.dtype)

    def z_three(flat, length):
        rows = flat.shape[0]
        at = jnp.bitwise_and(iota(flat.shape, 0), length - 1)
        before = jnp.where(at == 0, 0.0, pltpu.roll(flat, 1, 0))
        after = jnp.where(at == length - 1, 0.0, pltpu.roll(flat, rows - 1, 0))
        return before.astype(BF16), flat.astype(BF16), after.astype(BF16)

    def put_three(ref, flat, base, stride):
        shape = ref.shape[:3] + (LANES,)
        for c, part in enumerate(z_three(flat, ref.shape[2])):
            lo = c * stride + base
            ref[:, :, :, lo : lo + LANES] = part.reshape(shape)

    def merge_frame(full, low):
        ex, ey = full.shape[0], full.shape[1]
        full[0] = low[0].astype(F32)
        full[ex - 1] = low[ex - 1].astype(F32)
        full[1 : ex - 1, 0] = low[1 : ex - 1, 0].astype(F32)
        full[1 : ex - 1, ey - 1] = low[1 : ex - 1, ey - 1].astype(F32)

    def conv(ref, weight, row0, ext):
        x, y = ext
        rows = x * y * ref.shape[2]
        depth = ref.shape[3]
        acc = None
        for ab in range(9):
            a, b = ab // 3, ab % 3
            window = ref[a : a + x, b : b + y].reshape(rows, depth)
            part = dot(window, weight[row0 + ab * depth : row0 + (ab + 1) * depth, :])
            acc = part if acc is None else acc + part
        return acc

    def conv_back(ref, weight, row0, cin, cout, ext):
        x, y = ext
        rows = x * y * ref.shape[2]
        acc = None
        for ab in range(9):
            a, b = ab // 3, ab % 3
            for c in range(3):
                window = ref[a : a + x, b : b + y, :, c * cout : (c + 1) * cout]
                tap = 26 - (3 * ab + c)
                part = dot_nt(
                    window.reshape(rows, cout),
                    weight[row0 + tap * cin : row0 + (tap + 1) * cin, :],
                )
                acc = part if acc is None else acc + part
        return acc

    def conv_grad(ref, low, row0, ext):
        x, y = ext
        rows = x * y * ref.shape[2]
        depth = ref.shape[3]
        for ab in range(9):
            a, b = ab // 3, ab % 3
            window = ref[a : a + x, b : b + y].reshape(rows, depth)
            g_ref[row0 + ab * depth : row0 + (ab + 1) * depth, :] = dot_tn(window, low).astype(BF16)

    def col_sum(v):
        return jnp.sum(v, axis=0, keepdims=True)

    def own(ref):
        return ref[1 : ref.shape[0] - 1, 1 : ref.shape[1] - 1]

    def flat(v):
        return v.reshape(-1, v.shape[-1])

    pair = s.pair

    def pool(v):
        v = v.reshape(X, Y, Z, LANES)
        v = v[0] + v[1]
        v = v.reshape(CY, 2, Z, LANES)
        v = v[:, 0] + v[:, 1]
        pair[0 : CY * Z] = v.reshape(CY * Z, LANES)
        return pair[pl.ds(0, VC, stride=2), :] + pair[pl.ds(1, VC, stride=2), :]

    def spread(v):
        pair[pl.ds(0, VC, stride=2), :] = v
        pair[pl.ds(1, VC, stride=2), :] = v
        u = pair[0 : CY * Z].reshape(CY, 1, Z, LANES)
        u = jnp.broadcast_to(u, (CY, 2, Z, LANES)).reshape(1, Y, Z, LANES)
        return jnp.broadcast_to(u, (X, Y, Z, LANES)).reshape(V, LANES)

    def stats(total_rows, count):
        half = total_rows.shape[0] // 2
        parts = [total_rows[i : i + 1] for i in range(2 * half)]
        mean = jnp.concatenate(parts[:half], 1) / count
        spread_v = jnp.concatenate(parts[half:], 1) / count - mean * mean
        return mean, lax.rsqrt(spread_v + EPS_NORM)

    def ready(zd, xd):
        p = (zd * nx + xd) * nn
        low = 16 * (lay.begin[p] - 1)
        return 3 if low < ROW_MID else 2 if low < ROW_PSI else 1 if low < ROW_DEC2 else 0

    units = [(zd, xd) for zd in range(nz) for xd in range(nx)]
    units_a, units_b, units_c, units_d = [
        [u for u in units if ready(*u) == k] for k in range(4)
    ]
    g_ref[0:32] = jnp.zeros((32, LANES), BF16)
    g_ref[ROW_PSI:ROWS_A] = jnp.zeros((ROWS_A - ROW_PSI, LANES), BF16)
    g_ref[ROW_TAIL:] = jnp.zeros((g_ref.shape[0] - ROW_TAIL, LANES), BF16)

    in_slots, in_send, in_recv = s.in_slots, s.in_send, s.in_recv

    def entry_grad(low):
        rows = [jnp.zeros((ROW_IN, LANES), F32)]
        for ab in range(9):
            a, b = ab // 3, ab % 3
            patch = entry[a + 1 : a + 1 + X, b + 1 : b + 1 + Y].reshape(V, LANES)
            block = dot_tn(patch, low)
            for c in range(3):
                rows.append(col_sum(block[c * Z : (c + 1) * Z]))
        return jnp.concatenate(rows, 0)

    def in_copy(k):
        return pltpu.make_async_remote_copy(
            in_slots.at[k, me],
            in_slots.at[k, me],
            in_send.at[k],
            in_recv.at[k],
            device_id=(0, 0),
            device_id_type=MESH,
        )

    def in_whole(k):
        others_in = in_slots.at[k, pl.ds(0, total - 1)]
        return pltpu.make_async_remote_copy(
            others_in, others_in, in_send.at[k], in_recv.at[k], device_id=(w, n), device_id_type=MESH
        )

    tap_at = iota((32, LANES), 0) == iota((32, LANES), 1) + ROW_IN

    def in_put(k, block):
        in_slots[k, me] = block.astype(in_slots.dtype)

        @pl.when(me != 0)
        def _():
            in_copy(k).start()

    cts, ct_send, ct_recv = s.cts, s.ct_send, s.ct_recv
    cts[4] = ct_ref[...]

    def ct_copy(i):
        dx, dy = DIRS[i]
        return pltpu.make_async_remote_copy(
            cts.at[4],
            cts.at[3 * (1 - dx) + 1 - dy],
            ct_send.at[i],
            ct_recv.at[i],
            device_id=(lax.rem(w + dx + nw, nw), lax.rem(n + dy + nn, nn)),
            device_id_type=MESH,
        )

    for i in range(8):
        ct_copy(i).start()

    step(gather_one, 1)

    quick_wait()
    tail = quick[32:48, :].astype(F32)
    used_rows = CLASSES * (C1 + 1) // LANES
    used_lanes = CLASSES * (C1 + 1) % LANES
    rolled = pltpu.roll(tail, LANES - used_lanes, 1)
    lane_id = iota((1, LANES), 1)

    def tail_row(q):
        r = used_rows + q
        return jnp.where(
            lane_id < LANES - used_lanes, rolled[r : r + 1], rolled[r + 1 : r + 2]
        )

    gains = [tail_row(q) for q in range(6)]
    shifts = [tail_row(6 + q) for q in range(6)]
    gain = [gains[0], gains[1], jnp.concatenate(gains[2:4], 1), gains[4], gains[5]]
    shift = [shifts[0], shifts[1], jnp.concatenate(shifts[2:4], 1), shifts[4], shifts[5]]

    def select_head(j, r):
        return onehot(
            LANES * r + iota((LANES, LANES), 0) == CLASSES * iota((LANES, LANES), 1) + j
        )

    tail_low = tail.astype(BF16)
    head_rows = []
    for j in range(CLASSES):
        row = None
        for r in range(CLASSES):
            part = dot(tail_low, select_head(j, r))[r : r + 1]
            row = part if row is None else row + part
        head_rows.append(row)
    head_t = jnp.concatenate(head_rows + [jnp.zeros((8 - CLASSES, LANES), F32)], 0).astype(BF16)
    bias_row = tail[used_rows : used_rows + 1]
    bias_col = jnp.sum(
        jnp.where(iota((8, LANES), 0) == iota((8, LANES), 1), bias_row, 0.0), axis=1, keepdims=True
    )
    bias_col = jnp.where(iota((8, 1), 0) < CLASSES, bias_col, 0.0)

    def pick_half(h, rows):
        return onehot(iota((2 * rows, rows), 0) == 2 * iota((2 * rows, rows), 1) + h)

    def widen(block, rows):
        block = block.astype(F32)
        lower = jnp.where(lane_id < GATE, block, 0.0).astype(BF16)
        upper = jnp.where(lane_id < GATE, pltpu.roll(block, GATE, 1), 0.0).astype(BF16)
        both = dot(pick_half(0, rows), lower) + dot(pick_half(1, rows), upper)
        return both.astype(BF16)

    def narrow_back(block, rows):
        low = block.astype(BF16)
        lower = dot_tn(pick_half(0, rows), low)
        upper = dot_tn(pick_half(1, rows), low)
        return (lower + pltpu.roll(upper, GATE, 1)).astype(BF16)

    front = quick[0:32, :].astype(F32)
    step(gather_two, 0)
    step(gather_one, 2)
    we = s.we
    for ab in range(9):
        taps = [
            jnp.broadcast_to(front[ROW_IN + 3 * ab + c : ROW_IN + 3 * ab + c + 1], (Z, LANES))
            for c in range(3)
        ]
        taps.append(jnp.zeros((LANES - 3 * Z, LANES), F32))
        we[ab * LANES : (ab + 1) * LANES] = jnp.concatenate(taps, 0).astype(BF16)

    shuffle = onehot(
        iota((C2, C2), 1)
        == jnp.bitwise_and(iota((C2, C2), 0), 1) * C1 + lax.shift_right_logical(iota((C2, C2), 0), 1)
    )
    valid = val_ref[...]
    count_row = jnp.broadcast_to(jnp.sum(valid, axis=1, keepdims=True), (1, LANES))

    for i in range(8):
        ct_copy(i).wait_recv()

    entry = s.entry
    zz, ll = iota((Z, LANES), 0), iota((Z, LANES), 1)
    band = jnp.where((jnp.bitwise_and(ll, Z - 1) == zz + ll // Z - 1) & (ll < 3 * Z), 1.0, 0.0)
    for ex in range(X + 4):
        bx = (ex - 2 + X) // X
        lx = ex - 2 - (bx - 1) * X
        for ey in range(Y + 4):
            by = (ey - 2 + Y) // Y
            ly = ey - 2 - (by - 1) * Y
            row = cts[3 * bx + by, lx * Y + ly : lx * Y + ly + 1]
            entry[ex, ey] = (jnp.broadcast_to(row, (Z, LANES)) * band).astype(BF16)
    clear_edges(entry, 2)
    step(gather_two, 1)
    step(gather_three, 0)
    step(gather_one, 3)
    raw1 = s.raw1
    raw1[...] = conv(entry, we, 0, (XE, YE)).reshape(XE, YE, Z, LANES)
    mine = flat(own(raw1))
    ar_start(0, [col_sum(mine), col_sum(mine * mine), count_row])
    if quarter == 1:
        step(gather_two, 2)
        step(gather_three, 1)
    else:
        for d in range(1, nz):
            at_distance(d, gather_one)
        for k in range(3):
            gather(gather_two, k)
        for k in range(2):
            gather(gather_three, k)
    sums = ar_wait(0)
    valid_count = sums[2:3, 0:1]
    mean1, inv1 = stats(sums[0:2], voxels)
    v = (flat(raw1[...]) - mean1) * inv1 * gain[0] + shift[0]
    pad1 = s.pad1
    put_three(pad1, v * jax.nn.sigmoid(v), 0, C1)
    clear_edges(pad1, 1)

    gather(gather_two, 3)
    gather(gather_three, 2)
    gather(gather_three, 3)
    gather(gather_four, 0)
    raw2, low2 = s.raw2, s.low2
    mine = conv(pad1, w_ref, ROW_ENC, (X, Y))
    raw2[1 : XE - 1, 1 : YE - 1] = mine.reshape(X, Y, Z, C1)
    low2[1 : XE - 1, 1 : YE - 1] = mine.astype(BF16).reshape(X, Y, Z, C1)
    ar_start(1, [col_sum(mine), col_sum(mine * mine)])
    halo_start(0, low2)
    sums = ar_wait(1)
    mean2, inv2 = stats(sums[0:2], voxels)
    v = (mine - mean2) * inv2 * gain[1] + shift[1]
    skip_own = v * jax.nn.sigmoid(v)

    gather(gather_four, 1)
    pool_in = s.pool_in
    pool_in[1 : CX + 1, 1 : CY + 1] = (pool(skip_own) * 0.125).astype(BF16).reshape(CX, CY, CZ, C1)
    halo_start(1, pool_in)
    wm = s.wm
    for tap in range(27):
        part = dot_tn(shuffle, w_ref[ROW_MID + C2 * tap : ROW_MID + C2 * (tap + 1), :]).astype(BF16)
        wm[tap * C1 : (tap + 1) * C1, 0:LANES] = part[0:LANES]
        wm[tap * C1 : (tap + 1) * C1, LANES:C2] = part[LANES:C2]

    psi = w_ref[ROW_PSI : ROW_PSI + 16, :].astype(F32)[0:1]
    psi = jnp.where(lane_id < GATE, psi, 0.0)
    w_x = widen(w_ref[ROW_X : ROW_X + C1 // 2, :], C1 // 2)
    w_g = widen(w_ref[ROW_G : ROW_G + C2 // 2, :], C2 // 2)
    halo_wait(0, low2)
    merge_frame(raw2, low2)
    v = (flat(raw2[...]) - mean2) * inv2 * gain[1] + shift[1]
    skip = s.skip
    skip_all = v * jax.nn.sigmoid(v)
    skip[...] = skip_all.reshape(XE, YE, Z, C1)
    mix = s.mix
    mix[...] = dot(skip_all.astype(BF16), w_x).reshape(XE, YE, Z, LANES)
    halo_wait(1, pool_in)
    clear_edges(pool_in, 1)
    pad_mid = s.pad_mid
    put_three(pad_mid, flat(pool_in[...].astype(F32)), 0, C1)
    raw3, low3 = s.raw3, s.low3
    mine = conv(pad_mid, wm, 0, (CX, CY))
    raw3[1 : CX + 1, 1 : CY + 1] = mine.reshape(CX, CY, CZ, C2)
    low3[1 : CX + 1, 1 : CY + 1] = mine.astype(BF16).reshape(CX, CY, CZ, C2)
    sum_v, square_v = col_sum(mine), col_sum(mine * mine)
    ar_start(
        2, [sum_v[:, 0:C1], sum_v[:, C1:C2], square_v[:, 0:C1], square_v[:, C1:C2]]
    )
    halo_start(2, low3)
    in_put(
        0,
        entry_grad(((flat(own(raw1)) - mean1) * inv1).astype(BF16))
        + jnp.where(
            iota((32, LANES), 0) == 0,
            col_sum(jnp.where(tap_at, entry_grad(jnp.ones((V, LANES), BF16)), 0.0)),
            0.0,
        ),
    )
    sums = ar_wait(2)
    mean3, inv3 = stats(sums, coarse_voxels)
    halo_wait(2, low3)
    merge_frame(raw3, low3)
    v = (flat(raw3[...]) - mean3) * inv3 * gain[2] + shift[2]
    coarse = (v * jax.nn.sigmoid(v)).astype(BF16).reshape(CX + 2, CY + 2, CZ, C2)
    coarse_own = flat(coarse[1 : CX + 1, 1 : CY + 1])
    frame = (CY + 2) * CZ
    doubled = onehot(
        iota((2 * frame, frame), 1) == lax.shift_right_logical(iota((2 * frame, frame), 0), 1)
    )
    tall = s.tall
    for cx in range(CX + 2):
        tall[cx] = (
            dot(doubled, coarse[cx].reshape(frame, C2)).astype(BF16).reshape(CY + 2, Z, C2)
        )

    def expand(u):
        u = jnp.concatenate([u[(i + 1) // 2 : (i + 1) // 2 + 1] for i in range(XE)], 0)
        return jnp.concatenate([u[:, (j + 1) // 2 : (j + 1) // 2 + 1] for j in range(YE)], 1)

    gate_c = dot(flat(tall[...]), w_g).reshape(CX + 2, CY + 2, Z, LANES)
    mixed_in = flat(mix[...] + expand(gate_c))
    mix[...] = mixed_in.reshape(XE, YE, Z, LANES)
    mixed = mixed_in * jax.nn.sigmoid(mixed_in)
    att = jax.nn.sigmoid(jnp.sum(mixed * psi, axis=1, keepdims=True))
    attention = s.attention
    attention[...] = jnp.broadcast_to(att, (XE * YE * Z, LANES)).reshape(XE, YE, Z, LANES)
    pad_join = s.pad_join
    put_three(pad_join, flat(skip[...] * attention[...]), 0, C1 + C2)
    for half in range(2):
        piece = flat(tall[:, :, :, half * C1 : (half + 1) * C1].astype(F32))
        for c, part in enumerate(z_three(piece, Z)):
            lo = c * (C1 + C2) + C1 + half * C1
            pad_join[:, :, :, lo : lo + C1] = expand(part.reshape(CX + 2, CY + 2, Z, C1))
    clear_edges(pad_join, 1)

    gather(gather_four, 2)
    gather(gather_four, 3)
    raw4, low4 = s.raw4, s.low4
    mine = conv(pad_join, w_ref, ROW_DEC1, (X, Y))
    raw4[1 : XE - 1, 1 : YE - 1] = mine.reshape(X, Y, Z, C1)
    low4[1 : XE - 1, 1 : YE - 1] = mine.astype(BF16).reshape(X, Y, Z, C1)
    ar_start(3, [col_sum(mine), col_sum(mine * mine)])
    halo_start(3, low4)
    sums = ar_wait(3)
    mean4, inv4 = stats(sums[0:2], voxels)
    halo_wait(3, low4)
    merge_frame(raw4, low4)
    v = (flat(raw4[...]) - mean4) * inv4 * gain[3] + shift[3]
    pad4 = s.pad4
    put_three(pad4, v * jax.nn.sigmoid(v), 0, C1)
    clear_edges(pad4, 1)

    raw5, low5 = s.raw5, s.low5
    mine = conv(pad4, w_ref, ROW_DEC2, (X, Y))
    raw5[1 : XE - 1, 1 : YE - 1] = mine.reshape(X, Y, Z, C1)
    low5[1 : XE - 1, 1 : YE - 1] = mine.astype(BF16).reshape(X, Y, Z, C1)
    ar_start(4, [col_sum(mine), col_sum(mine * mine)])
    halo_start(4, low5)
    sums = ar_wait(4)
    mean5, inv5 = stats(sums[0:2], voxels)
    hat = (mine - mean5) * inv5
    v = hat * gain[4] + shift[4]
    sg = jax.nn.sigmoid(v)
    act = (v * sg).astype(BF16)

    logits = dot_nt(head_t, act) + bias_col
    real = iota((8, V), 0) < CLASSES
    logits = jnp.where(real, logits, -1e30)
    hot = iota((8, V), 0) == lab_ref[...]
    top = jnp.max(logits, axis=0, keepdims=True)
    log_total = top + jnp.log(jnp.sum(jnp.exp(logits - top), axis=0, keepdims=True))
    picked = jnp.sum(jnp.where(hot, logits, 0.0), axis=0, keepdims=True)
    loss = jnp.sum(valid * (log_total - picked), axis=1, keepdims=True)
    probs = jnp.exp(logits - log_total)
    g_logits = valid * (probs - jnp.where(hot, 1.0, 0.0)) / valid_count
    g_low = g_logits.astype(BF16)
    head_grad = dot(g_low, act)
    bias_grad = jnp.sum(g_low.astype(F32), axis=1, keepdims=True)
    bias_line = jnp.sum(
        jnp.where(iota((8, LANES), 0) == iota((8, LANES), 1), bias_grad, 0.0), axis=0, keepdims=True
    )
    dy = dot_tn(g_low, head_t) * silu_grad(v, sg)

    def norm_back(r, h, dy, hat, raw, mean, inv, gain_v, ext, count, names2, extra):
        dyf, dyl = names2
        ex, ey = ext[0] + 2, ext[1] + 2
        width = dy.shape[1]
        shaped = dy.reshape(ext + (width,))
        dyf[1 : ex - 1, 1 : ey - 1] = shaped
        dyl[1 : ex - 1, 1 : ey - 1] = shaped.astype(BF16)
        first, second = col_sum(dy), col_sum(dy * hat)
        rows = [first[:, i : i + LANES] for i in range(0, width, LANES)]
        rows += [second[:, i : i + LANES] for i in range(0, width, LANES)]
        ar_start(r, rows + extra)
        halo_start(h, dyl)
        return rows

    def norm_back_end(r, h, raw, mean, inv, gain_v, count, names2):
        dyf, dyl = names2
        sums = ar_wait(r)
        halo_wait(h, dyl)
        merge_frame(dyf, dyl)
        width = dyf.shape[3]
        k = width // LANES
        one = jnp.concatenate([sums[i : i + 1] for i in range(k)], 1)
        two = jnp.concatenate([sums[k + i : k + i + 1] for i in range(k)], 1)
        hat_all = (flat(raw[...]) - mean) * inv
        back = inv * gain_v * (flat(dyf[...]) - one / count - hat_all * (two / count))
        return sums, back

    grad_shift, grad_gain = {}, {}
    fine = (X, Y, Z)
    norm_back(5, 5, dy, hat, raw5, mean5, inv5, gain[4], fine, voxels, (s.dy5, s.dyl5),
              [jnp.broadcast_to(loss, (1, LANES))])
    halo_wait(4, low5)
    merge_frame(raw5, low5)
    sums, back = norm_back_end(5, 5, raw5, mean5, inv5, gain[4], voxels, (s.dy5, s.dyl5))
    grad_shift[4], grad_gain[4] = [sums[0:1]], [sums[1:2]]
    loss_row = sums[2:3]
    dpad = s.dpad5
    put_three(dpad, back, 0, C1)
    clear_edges(dpad, 1)
    grad_act = conv_back(dpad, w_ref, ROW_DEC2, C1, C1, (X, Y))
    hat = (flat(own(raw4)) - mean4) * inv4
    v = hat * gain[3] + shift[3]
    dy = grad_act * silu_grad(v, jax.nn.sigmoid(v))
    norm_back(6, 6, dy, hat, raw4, mean4, inv4, gain[3], fine, voxels, (s.dy4, s.dyl4), [])
    conv_grad(pad4, flat(own(dpad)[:, :, :, C1 : 2 * C1]), ROW_DEC2, (X, Y))
    red_one(units_a)
    red_two(units_a)
    sums, back = norm_back_end(6, 6, raw4, mean4, inv4, gain[3], voxels, (s.dy4, s.dyl4))
    grad_shift[3], grad_gain[3] = [sums[0:1]], [sums[1:2]]
    dpad = s.dpad4
    put_three(dpad, back, 0, C1)
    clear_edges(dpad, 1)
    low_raw4 = flat(own(dpad)[:, :, :, C1 : 2 * C1])
    grad_join = conv_back(dpad, w_ref, ROW_DEC1, C1 + C2, C1, (X, Y))

    grad_gated = grad_join[:, 0:C1]
    skip_own = flat(own(skip))
    att_own = flat(own(attention))
    mixed_own = flat(own(mix))
    sg = jax.nn.sigmoid(mixed_own)
    d_att = jnp.sum(grad_gated * skip_own, axis=1, keepdims=True)
    d_logit = d_att * att_own * (1.0 - att_own)
    psi_grad = col_sum(mixed_own * sg * d_logit)
    d_mixed = d_logit * psi * silu_grad(mixed_own, sg)
    low_fine = d_mixed.astype(BF16)
    low_gc = pool(d_mixed).astype(BF16)
    d_coarse = [
        pool(grad_join[:, C1 : 2 * C1]),
        pool(grad_join[:, 2 * C1 : 3 * C1]),
    ]
    d_coarse = jnp.concatenate(d_coarse, 1) + dot_nt(low_gc, w_g)
    d_coarse = d_coarse.astype(BF16).astype(F32)
    hat = (flat(own(raw3)) - mean3) * inv3
    v = hat * gain[2] + shift[2]
    dy = d_coarse * silu_grad(v, jax.nn.sigmoid(v))
    norm_back(7, 7, dy, hat, raw3, mean3, inv3, gain[2], (CX, CY, CZ), coarse_voxels, (s.dy3, s.dyl3), [])
    side_start([head_grad[0:1], head_grad[1:2], head_grad[2:3], bias_line, psi_grad])
    red_three(units_a)
    d_skip = s.d_skip
    d_skip[...] = grad_gated * att_own + dot_nt(low_fine, w_x)
    conv_grad(pad_join, low_raw4, ROW_DEC1, (X, Y))
    g_ref[ROW_X : ROW_X + C1 // 2, :] = narrow_back(
        dot_tn(skip_own.astype(BF16), low_fine), C1 // 2
    )
    g_ref[ROW_G : ROW_G + C2 // 2, :] = narrow_back(dot_tn(coarse_own, low_gc), C2 // 2)
    red_one(units_b)
    sums, back = norm_back_end(7, 7, raw3, mean3, inv3, gain[2], coarse_voxels, (s.dy3, s.dyl3))
    grad_shift[2], grad_gain[2] = [sums[0:1], sums[1:2]], [sums[2:3], sums[3:4]]
    dpad = s.dpad3
    put_three(dpad, back[:, 0:C1], 0, C2)
    put_three(dpad, back[:, C1:C2], C1, C2)
    clear_edges(dpad, 1)
    low_raw3 = flat(own(dpad)[:, :, :, C2 : 2 * C2])
    d_pool = conv_back(dpad, wm, 0, C1, C2, (CX, CY))
    grad_skip = d_skip[...] + spread(d_pool) * 0.125
    hat = (flat(own(raw2)) - mean2) * inv2
    v = hat * gain[1] + shift[1]
    dy = grad_skip * silu_grad(v, jax.nn.sigmoid(v))
    norm_back(8, 8, dy, hat, raw2, mean2, inv2, gain[1], fine, voxels, (s.dy2, s.dyl2), [])
    red_two(units_b)
    for ab in range(9):
        window = pad_mid[ab // 3 : ab // 3 + CX, ab % 3 : ab % 3 + CY].reshape(VC, 3 * C1)
        block = dot_tn(window, low_raw3).astype(BF16)
        for c in range(3):
            stacked = block[c * C1 : (c + 1) * C1]
            stacked = jnp.concatenate([stacked[:, 0:C1], stacked[:, C1:C2]], 0)
            lo = ROW_MID + (3 * ab + c) * C2
            g_ref[lo : lo + C2, :] = dot(shuffle, stacked).astype(BF16)
    red_one(units_c)
    red_four(units_a)
    red_two(units_c)
    sums, back = norm_back_end(8, 8, raw2, mean2, inv2, gain[1], voxels, (s.dy2, s.dyl2))
    grad_shift[1], grad_gain[1] = [sums[0:1]], [sums[1:2]]
    dpad = s.dpad2
    put_three(dpad, back, 0, C1)
    clear_edges(dpad, 1)
    low_raw2 = flat(own(dpad)[:, :, :, C1 : 2 * C1])
    conv_grad(pad1, low_raw2, ROW_ENC, (X, Y))
    red_one(units_d)
    red_between(units_a)
    red_three(units_b)
    grad_act = conv_back(dpad, w_ref, ROW_ENC, C1, C1, (X, Y))
    hat1 = (flat(own(raw1)) - mean1) * inv1
    v = hat1 * gain[0] + shift[0]
    dy = grad_act * silu_grad(v, jax.nn.sigmoid(v))
    ar_start(9, [col_sum(dy), col_sum(dy * hat1)])
    low_raw1 = dy.astype(BF16)
    in_put(1, entry_grad(low_raw1))
    red_two(units_d)
    red_three(units_c)
    red_three(units_d)
    red_four(units_b)
    red_four(units_c)
    red_four(units_d)
    red_between(units_b)
    red_between(units_c)
    red_between(units_d)

    sums = ar_wait(9)
    grad_shift[0], grad_gain[0] = [sums[0:1]], [sums[1:2]]
    side_whole().wait_recv()
    small = jnp.sum(side[...], axis=0)
    flat_rows = []
    for r in range(CLASSES):
        row = None
        for j in range(CLASSES):
            part = lax.dot_general(
                small,
                select_head(j, r).astype(F32),
                (((1,), (1,)), ((), ())),
                preferred_element_type=F32,
                precision=lax.Precision.HIGHEST,
            )[j : j + 1]
            row = part if row is None else row + part
        flat_rows.append(row)
    later = []
    for group in (grad_gain, grad_shift):
        for layer in range(5):
            later += group[layer]
    later = [pltpu.roll(row, used_lanes, 1) for row in later]
    flat_rows.append(jnp.where(lane_id < used_lanes, small[3:4], later[0]))
    for q in range(1, 12):
        flat_rows.append(jnp.where(lane_id < used_lanes, later[q - 1], later[q]))
    flat_rows.append(jnp.where(lane_id < used_lanes, later[11], 0.0))
    tail_grad = jnp.concatenate(flat_rows, 0)
    psi_row = jnp.where(lane_id < GATE, small[4:5], 0.0)
    scalar_out[...] = jnp.concatenate(
        [loss_row, jnp.broadcast_to(valid_count, (1, LANES)), jnp.zeros((6, LANES), F32)], 0
    )


    red_five(units)
    base = 16 * (begin - 1) - 16

    def put_row(row, block):
        at = row - base
        rows = block.shape[0]

        @pl.when((at >= 16) & (at + rows <= 16 + win_rows))
        def _():
            acc[pl.ds(pl.multiple_of(at, 16), rows), :] = block

    put_row(ROW_TAIL, tail_grad)
    put_row(ROW_PSI, jnp.concatenate([psi_row, jnp.zeros((15, LANES), F32)], 0))

    @pl.when(me == 0)
    def _():
        for k in range(2):
            in_whole(k).wait_recv()
        with_hat, with_dy = [jnp.sum(in_slots[k].astype(F32), axis=0) for k in range(2)]
        with_one = jnp.sum(jnp.where(tap_at, with_hat[0:1], 0.0), axis=1, keepdims=True)
        with_hat = jnp.where(iota((32, LANES), 0) < ROW_IN, 0.0, with_hat)
        entry_total = with_dy - with_one * (grad_shift[0][0] / voxels)
        entry_total = entry_total - with_hat * (grad_gain[0][0] / voxels)
        at = 16 - 16 * (lay.begin[0] - 1)
        acc[at : at + 32] = acc[at : at + 32] + entry_total * (inv1 * gain[0])

    grad_a = acc[pl.ds(16 + off_a, lay.rows), :]
    late = pltpu.roll(acc[pl.ds(16 + off_b + 1, lay.rows), :], LANES // 2, 1)
    early = pltpu.roll(acc[pl.ds(16 + off_b, lay.rows), :], LANES // 2, 1)
    grad_b = jnp.where(lane < LANES // 2, early, late)
    position = (
        me * lay.rows * LANES
        + iota((lay.rows, LANES), 0) * LANES
        + iota((lay.rows, LANES), 1)
    )
    gradient = jnp.where(position < SPLIT, grad_a, grad_b)
    gradient = jnp.where(position < USED, gradient, 0.0)
    params = param_ref[...]
    new_first = BETA_ONE * first_ref[...] + (1.0 - BETA_ONE) * gradient
    new_second = BETA_TWO * second_ref[...] + (1.0 - BETA_TWO) * gradient * gradient
    first_out[...] = new_first
    second_out[...] = new_second
    update = (
        new_first
        / (1.0 - BETA_ONE**STEP)
        / (jnp.sqrt(new_second / (1.0 - BETA_TWO**STEP)) + EPS_ADAM)
        + DECAY_RATE * params
    )
    param_out[...] = update
    limits = STARTS + (USED, total * lay.rows * LANES)
    squares = (params * params, update * update)
    lines = []
    for square in squares:
        for k in range(len(limits) - 1):
            member = (position >= limits[k]) & (position < limits[k + 1])
            lines.append(col_sum(jnp.where(member, square, 0.0)))
    lines = jnp.concatenate(lines, 0)
    lines = jnp.sum(lines, axis=1, keepdims=True)
    k = lines.shape[0]
    line = col_sum(jnp.where(iota((k, LANES), 0) == iota((k, LANES), 1), lines, 0.0))
    ar_start(10, [line])
    sums = ar_wait(10)[0:1]
    parts = len(limits) - 1
    roots = jnp.sqrt(sums)
    scale = jnp.zeros((lay.rows, LANES), F32)
    for k in range(parts):
        member = (position >= limits[k]) & (position < limits[k + 1])
        ratio = roots[:, k : k + 1] / roots[:, parts + k : parts + k + 1]
        scale = jnp.where(member, ratio, scale)
    param_out[...] = param_ref[...] - LEARN_RATE * scale * param_out[...]

    gather_end()
    quick_end()
    for zp in range(nz):

        @pl.when((here[0] >= zp) & (here[0] < nz - 1))
        def _():
            for piece in every:
                onward_copy(zp, True, piece).wait_send()

        @pl.when((here[0] <= zp) & (here[0] > 0))
        def _():
            for piece in every:
                onward_copy(zp, False, piece).wait_send()

    red_finish()

    @pl.when(me != 0)
    def _():
        for k in range(2):
            in_copy(k).wait_send()

    for r in range(N_AR):
        ar_whole(r).wait_send()
    side_whole().wait_send()
    for i in range(8):
        ct_copy(i).wait_send()
    for h, framed in enumerate(
        (s.low2, s.pool_in, s.low3, s.low4, s.low5, s.dyl5, s.dyl4, s.dyl3, s.dyl2)
    ):
        for i in range(8):
            halo_copy(h, framed, i).wait_send()


def step_call(nw, nn, ext, ct, lab, val, params, first, second):
    X, Y, Z = ext
    XE, YE = X + 2, Y + 2
    CX, CY, CZ = X // 2, Y // 2, Z // 2
    total = nw * nn
    framed = (XE, YE, Z)
    small = (CX + 2, CY + 2, CZ)
    dma = pltpu.SemaphoreType.DMA
    rows = params.shape[0]
    lay = Layout(rows * LANES, total)
    nz, nx, ny, nc = grid_of(nw, nn)
    oy = max(ny - 1, 1)
    half = 16 * (-(-lay.window // 32))
    low = lambda *shape: pltpu.VMEM(shape, BF16)
    scratch = dict(
        weights=low(lay.weight_rows, LANES),
        grads=low(lay.grad_rows, LANES),
        natural=pltpu.VMEM((rows + 112, LANES), F32),
        fix=low(total, lay.fix, LANES),
        quick=low(48, LANES),
        quick_send=dma((2,)),
        quick_recv=dma((2,)),
        onward_send=dma((nz, 2, PIECES)),
        gather_send=dma((PIECES,)),
        gather_recv=dma((total, PIECES)),
        red_c=low(nz, nx, ny, nc - 1, lay.window, LANES),
        red_dx=low(nz, nx, oy, half, LANES),
        red_dy=low(nz, nx, oy, lay.window - half, LANES),
        red_ex=low(nz, nx, lay.window, LANES),
        red_ey=low(nz, oy, lay.window, LANES),
        red_z=low(nz if nz == 4 else 1, nz, lay.window, LANES),
        send_core=dma((nz, nx, ny, nc - 1)),
        recv_core=dma((nz, nx, ny, nc - 1)),
        send_dx=dma((nz, nx, oy)),
        recv_dx=dma((nz, nx, oy)),
        send_dy=dma((nz, nx, oy)),
        recv_dy=dma((nz, nx, oy)),
        send_ex=dma((nz, nx)),
        recv_ex=dma((nz, nx)),
        send_ey=dma((nz, nx, oy)),
        recv_ey=dma((nz, oy)),
        send_z=dma((nz, nx, 2)),
        recv_z=dma((nz, nz, 2)),
        acc=pltpu.VMEM((lay.window + 48, LANES), F32),
        in_slots=pltpu.VMEM((2, total, 32, LANES), F32 if total <= 64 else BF16),
        in_send=dma((2,)),
        in_recv=dma((2,)),
        slots=pltpu.VMEM((N_AR, total, 4, LANES), F32),
        ar_send=dma((N_AR,)),
        ar_recv=dma((N_AR,)),
        side=pltpu.VMEM((total, 8, LANES), F32),
        side_send=dma,
        side_recv=dma,
        halo_send=dma((N_HALO, 8)),
        halo_recv=dma((N_HALO, 8)),
        cts=pltpu.VMEM((9, X * Y, LANES), F32),
        ct_send=dma((8,)),
        ct_recv=dma((8,)),
        pair=pltpu.VMEM((CY * Z, LANES), F32),
        we=pltpu.VMEM((9 * LANES, LANES), BF16),
        wm=pltpu.VMEM((27 * C1, C2), BF16),
        entry=pltpu.VMEM((X + 4, Y + 4, Z, LANES), BF16),
        raw1=pltpu.VMEM(framed + (C1,), F32),
        pad1=pltpu.VMEM(framed + (3 * C1,), BF16),
        raw2=pltpu.VMEM(framed + (C1,), F32),
        low2=pltpu.VMEM(framed + (C1,), BF16),
        pool_in=pltpu.VMEM(small + (C1,), BF16),
        skip=pltpu.VMEM(framed + (C1,), F32),
        mix=pltpu.VMEM(framed + (LANES,), F32),
        attention=pltpu.VMEM(framed + (LANES,), F32),
        pad_mid=pltpu.VMEM(small + (3 * C1,), BF16),
        raw3=pltpu.VMEM(small + (C2,), F32),
        low3=pltpu.VMEM(small + (C2,), BF16),
        tall=pltpu.VMEM((CX + 2, CY + 2, Z, C2), BF16),
        pad_join=pltpu.VMEM(framed + (3 * (C1 + C2),), BF16),
        raw4=pltpu.VMEM(framed + (C1,), F32),
        low4=pltpu.VMEM(framed + (C1,), BF16),
        pad4=pltpu.VMEM(framed + (3 * C1,), BF16),
        raw5=pltpu.VMEM(framed + (C1,), F32),
        low5=pltpu.VMEM(framed + (C1,), BF16),
        dy5=pltpu.VMEM(framed + (C1,), F32),
        dyl5=pltpu.VMEM(framed + (C1,), BF16),
        dpad5=pltpu.VMEM(framed + (3 * C1,), BF16),
        dy4=pltpu.VMEM(framed + (C1,), F32),
        dyl4=pltpu.VMEM(framed + (C1,), BF16),
        dpad4=pltpu.VMEM(framed + (3 * C1,), BF16),
        dy3=pltpu.VMEM(small + (C2,), F32),
        dyl3=pltpu.VMEM(small + (C2,), BF16),
        dpad3=pltpu.VMEM(small + (3 * C2,), BF16),
        dy2=pltpu.VMEM(framed + (C1,), F32),
        dyl2=pltpu.VMEM(framed + (C1,), BF16),
        dpad2=pltpu.VMEM(framed + (3 * C1,), BF16),
        d_skip=pltpu.VMEM((X * Y * Z, C1), F32),
    )
    cfg = types.SimpleNamespace(nw=nw, nn=nn, ext=ext, names=tuple(scratch), lay=lay)
    vmem = pl.BlockSpec(memory_space=pltpu.VMEM)
    return pl.pallas_call(
        functools.partial(step_kernel, cfg),
        out_shape=(
            jax.ShapeDtypeStruct((rows, LANES), F32),
            jax.ShapeDtypeStruct((rows, LANES), F32),
            jax.ShapeDtypeStruct((rows, LANES), F32),
            jax.ShapeDtypeStruct((8, LANES), F32),
        ),
        in_specs=[vmem] * 6,
        out_specs=(vmem,) * 4,
        scratch_shapes=list(scratch.values()),
        compiler_params=pltpu.CompilerParams(
            collective_id=0, has_side_effects=True, vmem_limit_bytes=62 * 1024 * 1024
        ),
    )(ct, lab, val, params, first, second)


def on_device(params, first_moment, second_moment, ct_image, labels, valid_mask):
    ext = ct_image.shape
    ct = ct_image.astype(F32).reshape(-1, ext[2])
    ct = jnp.concatenate([ct, ct, ct, jnp.zeros((ct.shape[0], LANES - 3 * ext[2]), F32)], 1)
    new_params, new_first, new_second, scalars = step_call(
        lax.axis_size("wide"),
        lax.axis_size("narrow"),
        ext,
        ct,
        labels.reshape(1, -1),
        valid_mask.astype(F32).reshape(1, -1),
        params.reshape(-1, LANES),
        first_moment.reshape(-1, LANES),
        second_moment.reshape(-1, LANES),
    )
    return (
        new_params.reshape(-1),
        new_first.reshape(-1),
        new_second.reshape(-1),
        scalars[0, 0],
        scalars[1, 0],
    )


def solution(mesh):
    in_specs = (
        P(("wide", "narrow")),
        P(("wide", "narrow")),
        P(("wide", "narrow")),
        P("wide", "narrow", None),
        P("wide", "narrow", None),
        P("wide", "narrow", None),
    )
    out_specs = (P(("wide", "narrow")), P(("wide", "narrow")), P(("wide", "narrow")), P(), P())
    return jax.shard_map(
        on_device, mesh=mesh, in_specs=in_specs, out_specs=out_specs, check_vma=False
    )
```

```python
import functools
import types

import jax
import jax.numpy as jnp
from jax import lax
from jax.experimental import pallas as pl
from jax.experimental.pallas import tpu as pltpu
from jax.sharding import PartitionSpec as P

C1 = 128
C2 = 256
GATE = 64
CLASSES = 3
STEP = 10

EPS_NORM = 1e-05
BETA_ONE = 0.9
BETA_TWO = 0.999
EPS_ADAM = 1e-06
DECAY_RATE = 0.01
LEARN_RATE = 0.3

F32 = jnp.float32
BF16 = jnp.bfloat16
MESH = pl.DeviceIdType.MESH
LANES = 128
TILE = 16 * LANES

LENGTHS = (
    27 * C1,
    27 * C1 * C1,
    27 * C1 * C2,
    C1 * GATE,
    C2 * GATE,
    GATE,
    27 * (C1 + C2) * C1,
    27 * C1 * C1,
    (C1 + 1) * CLASSES,
    4 * C1 + C2,
    4 * C1 + C2,
)
STARTS = tuple(sum(LENGTHS[:i]) for i in range(len(LENGTHS)))
USED = sum(LENGTHS)

FRONT = 32 * LANES - STARTS[1]
SPLIT = STARTS[6]
ROW_IN = STARTS[0] + FRONT
ROW_IN = ROW_IN // LANES
ROW_ENC = (STARTS[1] + FRONT) // LANES
ROW_MID = (STARTS[2] + FRONT) // LANES
ROW_X = (STARTS[3] + FRONT) // LANES
ROW_G = (STARTS[4] + FRONT) // LANES
ROW_PSI = (STARTS[5] + FRONT) // LANES
ROWS_A = -(-(SPLIT + FRONT) // TILE) * 16
ROW_DEC1 = ROWS_A
ROW_DEC2 = ROW_DEC1 + (STARTS[7] - SPLIT) // LANES
ROW_TAIL = ROW_DEC1 + (STARTS[8] - SPLIT) // LANES

DIRS = tuple((dx, dy) for dx in (-1, 0, 1) for dy in (-1, 0, 1) if (dx, dy) != (0, 0))

N_AR = 11
N_HALO = 9
PIECES = 3


def grid_of(nw, nn):
    nx = max(k for k in range(1, nw + 1) if nw % k == 0 and k * k <= nw)
    ny = max(nn // 2, 1)
    return nw // nx, nx, ny, nn // ny


class Layout:
    def __init__(self, shard_len, total):
        self.rows = shard_len // LANES
        self.total = total
        self.turn = -(-SPLIT // shard_len)
        self.shift_a = FRONT // LANES
        self.shift_b = ROWS_A - SPLIT // LANES - 1
        begin = [self.first(p) for p in range(total + 1)]
        edge = []
        for p in range(1, total + 1):
            low = self.rows * p + (self.shift_b if p >= self.turn else self.shift_a)
            edge.append(low // 16)
        self.body = min(edge[p] - begin[p] for p in range(total))
        self.gap = max(begin[p + 1] - begin[p] - self.body for p in range(total))
        self.begin = begin
        self.half = -(-self.body // 2)
        self.fix = 16 * (1 + self.gap)
        self.window = 16 * (1 + self.body + self.gap)
        self.weight_rows = 16 * begin[total]
        self.grad_rows = max(16 * (begin[p] - 1) for p in range(total)) + self.window
        self.grad_rows = max(self.grad_rows, self.weight_rows)

    def first(self, p):
        late = (p + self.total - self.turn) // self.total
        return (self.rows * p + self.shift_a + 15 + (self.shift_b + 1 - self.shift_a) * late) // 16


def dot(a, b):
    return jnp.dot(a, b, preferred_element_type=F32)


def dot_nt(a, b):
    return lax.dot_general(a, b, (((1,), (1,)), ((), ())), preferred_element_type=F32)


def dot_tn(a, b):
    return lax.dot_general(a, b, (((0,), (0,)), ((), ())), preferred_element_type=F32)


def iota(shape, dim):
    return lax.broadcasted_iota(jnp.int32, shape, dim)


def onehot(cond):
    return jnp.where(cond, 1.0, 0.0).astype(BF16)


def silu_grad(v, s):
    return s * (1.0 + v * (1.0 - s))


def step_kernel(
    cfg,
    ct_ref,
    marks_ref,
    param_ref,
    first_ref,
    second_ref,
    param_out,
    first_out,
    second_out,
    scalar_out,
    *scr,
):
    s = types.SimpleNamespace(turn2=None, turn4=None, turn5=None)
    s.__dict__.update(zip(cfg.names, scr))
    w_ref, g_ref = s.weights, s.grads
    lay = cfg.lay
    nw, nn = cfg.nw, cfg.nn
    total = nw * nn
    X, Y, Z = cfg.ext
    XE, YE = X + 2, Y + 2
    CX, CY, CZ = X // 2, Y // 2, Z // 2
    V = X * Y * Z
    VC = CX * CY * CZ
    voxels = float(V * total)
    coarse_voxels = voxels / 8.0
    w = lax.axis_index("wide")
    n = lax.axis_index("narrow")
    me = w * nn + n

    def dev(p):
        return (p // nn, lax.rem(p, nn))

    barrier = pltpu.get_barrier_semaphore()

    def greet(d, carry):
        pl.semaphore_signal(
            barrier, inc=1, device_id=dev(lax.rem(me + d, total)), device_id_type=MESH
        )
        return carry

    lax.fori_loop(1, total, greet, 0)

    nz, nx, ny, nc = grid_of(nw, nn)
    here = (w // nx, lax.rem(w, nx), n // nc, lax.rem(n, nc))
    sizes = (nz, nx, ny, nc)

    def place(r):
        z, x, y, c = [
            h if d == 0 else lax.rem(h + d % k, k) for h, d, k in zip(here, r, sizes)
        ]
        return z * nx + x, y * nc + c

    def number(zp, r):
        a, b = place((0,) + r)
        return (zp * nx + lax.rem(a, nx)) * nn + b

    natural = s.natural
    lead = 32
    natural[0:lead] = jnp.zeros((lead, LANES), F32)
    natural[lead : lead + lay.rows] = param_ref[...]
    rest = natural.shape[0] - lead - lay.rows
    natural[lead + lay.rows :] = jnp.zeros((rest, LANES), F32)
    begin = lay.first(me)
    off_a = lay.rows * me + lay.shift_a - 16 * (begin - 1)
    off_b = off_a + lay.shift_b - lay.shift_a
    lane = iota((1, LANES), 1)
    span = 16 * (1 + lay.body + lay.gap)
    row_at = iota((span, LANES), 0) + 16 * (begin - 1)
    as_a = natural[pl.ds(lead - off_a, span), :]
    late = pltpu.roll(natural[pl.ds(lead - off_b, span), :], LANES // 2, 1)
    early = pltpu.roll(natural[pl.ds(lead - off_b - 1, span), :], LANES // 2, 1)
    as_b = jnp.where(lane < LANES // 2, early, late)
    share = jnp.where(row_at < ROWS_A, as_a, as_b).astype(BF16)
    fix = s.fix
    body = 16 * lay.body

    def at_tile(t):
        return pl.multiple_of(16 * t, 16)

    w_ref[pl.ds(at_tile(begin), body), :] = share[16 : 16 + body]
    fix[me] = jnp.concatenate([share[0:16], share[16 + body : 16 + body + 16 * lay.gap]], 0)

    gather_send, gather_recv = s.gather_send, s.gather_recv
    sent = [0] * PIECES
    every = (0, 1, 2)

    def flat_id(zp, r):
        x, y, c = [d % k for d, k in zip(r, sizes[1:])]
        return ((zp * nx + x) * ny + y) * nc + c

    def piece_ref(p, piece):
        if piece == 2:
            return fix.at[p]
        lo = 0 if piece == 0 else lay.half
        size = lay.half if piece == 0 else lay.body - lay.half
        return w_ref.at[pl.ds(at_tile(lay.first(p) + lo), 16 * size)]

    def gather_copy(zp, r, d, piece):
        ref = piece_ref(number(zp, r), piece)
        there = tuple(a - b for a, b in zip(r, d[1:]))
        return pltpu.make_async_remote_copy(
            ref,
            ref,
            gather_send.at[piece],
            gather_recv.at[flat_id(zp, there), piece],
            device_id=place(d),
            device_id_type=MESH,
        )

    def gather_push(zp, r, dests, pieces):
        for piece in pieces:
            for d in dests:
                gather_copy(zp, r, d, piece).start()

    def gather_take(zp, r, piece):
        gather_copy(zp, r, (0, 0, 0, 0), piece).wait_recv()

    along_x = [(0, k, 0, 0) for k in range(1, nx)]
    along_y = [(0, 0, k, 0) for k in range(1, ny)]
    sibling = [(0, 0, 0, k) for k in range(1, nc)]
    mine_r = (0, 0, 0)
    for piece in every:
        split = [len(along_y), len(along_x), len(along_x) + len(along_y)][piece]
        sent[piece] = nz * (len(along_x) + len(along_y) + len(sibling))
        first_hop = [(nx - 1) * len(along_y), (ny - 1) * len(along_x), (nx - 1) * len(along_y)]
        sent[piece] += nz * (first_hop[piece] + (nx * ny - 1) * len(sibling))

    onward_send = s.onward_send

    def onward_copy(zp, up, piece):
        ref = piece_ref(number(zp, mine_r), piece)
        return pltpu.make_async_remote_copy(
            ref,
            ref,
            onward_send.at[zp, int(up), piece],
            gather_recv.at[flat_id(zp, mine_r), piece],
            device_id=place((1 if up else nz - 1, 0, 0, 0)),
            device_id_type=MESH,
        )

    def onward(zp, up, piece):
        @pl.when(here[0] < nz - 1 if up else here[0] > 0)
        def _():
            onward_copy(zp, up, piece).start()

    def gather_own():
        for piece in every:
            for up in (True, False):
                onward(here[0], up, piece)
            gather_push(here[0], mine_r, along_x + along_y + sibling, (piece,))

    def at_distance(d, step):
        if d == 0:
            step(here[0], None)
            return

        @pl.when(here[0] - d >= 0)
        def _():
            step(here[0] - d, True)

        @pl.when(here[0] + d < nz)
        def _():
            step(here[0] + d, False)

    def gather_one(zp, up):
        for piece in every:
            gather_take(zp, mine_r, piece)
            onward(zp, up, piece)
            gather_push(zp, mine_r, along_x + along_y + sibling, (piece,))

    def gather_two(zp, up):
        for piece in every:
            for kx in range(1, nx):
                gather_take(zp, (kx, 0, 0), piece)
                if piece != 1:
                    gather_push(zp, (kx, 0, 0), along_y, (piece,))
                gather_push(zp, (kx, 0, 0), sibling, (piece,))
            for ky in range(1, ny):
                gather_take(zp, (0, ky, 0), piece)
                if piece == 1:
                    gather_push(zp, (0, ky, 0), along_x, (piece,))
                gather_push(zp, (0, ky, 0), sibling, (piece,))

    def gather_three(zp, up):
        for piece in every:
            for kx in range(1, nx):
                for ky in range(1, ny):
                    gather_take(zp, (kx, ky, 0), piece)
                    gather_push(zp, (kx, ky, 0), sibling, (piece,))

    def gather_four(zp):
        for kx in range(nx):
            for ky in range(ny):
                for kc in range(1, nc):
                    for piece in every:
                        gather_take(zp, (kx, ky, kc), piece)
        low, high = zp * nx * nn, (zp + 1) * nx * nn
        if zp == 0:
            w_ref[16 * (lay.begin[0] - 1) : 16 * lay.begin[0]] = fix[0, 0:16]
        else:
            put_gap(low - 1)
        for p in range(low, high - (zp < nz - 1)):
            put_gap(p)

    def put_gap(p):
        tile = lay.begin[p] + lay.body
        for i in range(lay.begin[p + 1] - tile):
            part = fix[p, 16 * (1 + i) : 16 * (2 + i)]
            if tile + i == lay.begin[p + 1] - 1 and p + 1 < total:
                part = part + fix[p + 1, 0:16]
            w_ref[16 * (tile + i) : 16 * (tile + i + 1)] = part

    quick, quick_send, quick_recv = s.quick, s.quick_send, s.quick_recv
    shard_len = lay.rows * LANES
    quick_parts = []
    for row, size in ((0, 32), (ROW_TAIL, 16)):
        owner = 0 if row == 0 else STARTS[8] // shard_len
        at = row - 16 * (lay.begin[owner] - 1)
        quick_parts.append((owner, at, size))

    def quick_copy(k, p):
        lo, size = (0, 32) if k == 0 else (32, 16)
        ref = quick.at[pl.ds(lo, size)]
        return pltpu.make_async_remote_copy(
            ref,
            ref,
            quick_send.at[k],
            quick_recv.at[k],
            device_id=dev(p),
            device_id_type=MESH,
        )

    for k, (owner, at, size) in enumerate(quick_parts):

        @pl.when(me == owner)
        def _():
            lo = 0 if k == 0 else 32
            quick[lo : lo + size] = share[at : at + size]

    pl.semaphore_wait(barrier, total - 1)
    for k, (owner, at, size) in enumerate(quick_parts):

        @pl.when(me == owner)
        def _():
            def push(d, carry):
                quick_copy(k, lax.rem(me + d, total)).start()
                return carry

            lax.fori_loop(1, total, push, 0)

    def quick_wait():
        for k, (owner, at, size) in enumerate(quick_parts):

            @pl.when(me != owner)
            def _():
                quick_copy(k, me).wait_recv()

    def quick_end():
        for k, (owner, at, size) in enumerate(quick_parts):

            @pl.when(me == owner)
            def _():
                whole = w_ref.at[pl.ds(0, (total - 1) * size)]
                pltpu.make_async_remote_copy(
                    whole,
                    whole,
                    quick_send.at[k],
                    quick_recv.at[k],
                    device_id=(w, n),
                    device_id_type=MESH,
                ).wait_send()

    quarter = nz // 4
    quarters = [range(k * quarter, (k + 1) * quarter) for k in range(4)]

    def gather(step, k):
        if step is gather_four:
            for zp in quarters[k]:
                step(zp)
            return
        for d in quarters[k]:
            at_distance(d, step)

    def step(what, d):
        if quarter == 1:
            gather(what, d)

    gather_own()

    def gather_end():
        for piece, count in enumerate(sent):
            if piece == 2:
                ref = fix
                unit = 1
            else:
                ref = w_ref
                unit = 16 * (lay.half if piece == 0 else lay.body - lay.half)
            most = ref.shape[0] // unit
            while count:
                k = min(count, most)
                whole = ref.at[pl.ds(0, k * unit)]
                pltpu.make_async_remote_copy(
                    whole,
                    whole,
                    gather_send.at[piece],
                    gather_recv.at[0, piece],
                    device_id=(w, n),
                    device_id_type=MESH,
                ).wait_send()
                count -= k

    cc, dx_in, dy_in = s.red_c, s.red_dx, s.red_dy
    ex_in, ey_in, zz_in = s.red_ex, s.red_ey, s.red_z
    win_rows = lay.window
    mid_row = 16 * (-(-win_rows // 32))
    halves = (pl.ds(0, mid_row), pl.ds(mid_row, win_rows - mid_row))
    acc = s.acc
    sent_red = []

    def grad_window(zd, xd, ry, rc):
        y = lax.rem(here[2] + ry, ny) if ry else here[2]
        c = lax.rem(here[3] + rc, nc) if rc else here[3]
        p = (zd * nx + xd) * nn + y * nc + c
        return pl.ds(at_tile(lay.first(p) - 1), win_rows)

    def red_copy(step, at_send, at_recv, source, target, to):
        return pltpu.make_async_remote_copy(
            source,
            target,
            step[0].at[at_send],
            step[1].at[at_recv],
            device_id=to,
            device_id_type=MESH,
        )

    def in_place(zd, xd):
        return here[1] == xd

    def off_place(zd, xd):
        return here[1] != xd

    def red_go(cond, copy):
        if cond is None:
            copy.start()
        else:

            @pl.when(cond)
            def _():
                copy.start()

        sent_red.append((cond, copy))

    def others(size):
        return range(1, size)

    def copy_core(zd, xd, ry, k):
        return red_copy(
            (s.send_core, s.recv_core),
            (zd, xd, ry, k - 1),
            (zd, xd, ry, k - 1),
            g_ref.at[grad_window(zd, xd, ry, k)],
            cc.at[zd, xd, ry, k - 1],
            place((0, 0, 0, k)),
        )

    def copy_dx(zd, xd, ry, xs):
        return red_copy(
            (s.send_dx, s.recv_dx),
            (zd, xd, ry - 1),
            (zd, xs, ry - 1),
            cc.at[zd, xd, ry, 0, halves[0]],
            dx_in.at[zd, xs, ry - 1],
            (here[0] * nx + xd, n),
        )

    def copy_dy(zd, xd, ry):
        return red_copy(
            (s.send_dy, s.recv_dy),
            (zd, xd, ry - 1),
            (zd, xd, ny - ry - 1),
            cc.at[zd, xd, ry, 0, halves[1]],
            dy_in.at[zd, xd, ny - ry - 1],
            place((0, 0, ry, 0)),
        )

    def copy_ex(zd, xd, xs):
        return red_copy(
            (s.send_ex, s.recv_ex), (zd, xd), (zd, xs), cc.at[zd, xd, 0, 0], ex_in.at[zd, xs], (here[0] * nx + xd, n)
        )

    def copy_ey(zd, xd, ry):
        return red_copy(
            (s.send_ey, s.recv_ey),
            (zd, xd, ry - 1),
            (zd, ny - ry - 1),
            cc.at[zd, xd, ry, 0],
            ey_in.at[zd, ny - ry - 1],
            place((0, 0, ry, 0)),
        )

    def way_along_z(zd):
        if nz != 4:
            return [], [zs for zs in range(nz) if zs != zd], None, None
        lead = 2 if zd < 2 else 1
        far = 3 if zd < 2 else 0
        near = zd + 1 - 2 * (zd % 2)
        return [(far, lead)], [near, lead], far, lead

    def copy_z(zd, xd, zs, to, h):
        return red_copy(
            (s.send_z, s.recv_z),
            (zd, xd, h),
            (zd, zs, h),
            cc.at[zd, xd, 0, 0, halves[h]],
            zz_in.at[zd if nz == 4 else 0, zs, halves[h]],
            (to * nx + xd, n),
        )

    def red_one(units):
        for zd, xd in units:
            for ry in range(ny):
                for k in others(nc):
                    red_go(None, copy_core(zd, xd, ry, k))

    def red_two(units):
        for zd, xd in units:
            for ry in reversed(range(ny)):
                part = g_ref[grad_window(zd, xd, ry, 0), :]
                for k in others(nc):
                    copy_core(zd, xd, ry, k).wait_recv()
                    part = part + cc[zd, xd, ry, k - 1]
                cc[zd, xd, ry, 0] = part
                if ry:
                    red_go(off_place(zd, xd), copy_dx(zd, xd, ry, here[1]))
                    red_go(off_place(zd, xd), copy_dy(zd, xd, ry))

    def red_three(units):
        for zd, xd in units:

            @pl.when(in_place(zd, xd))
            def _():
                for ry in others(ny):
                    part = cc[zd, xd, ry, 0, halves[0]]
                    for xs in range(nx):
                        if xs != xd:
                            copy_dx(zd, xd, ry, xs).wait_recv()
                            part = part + dx_in[zd, xs, ry - 1]
                    cc[zd, xd, ry, 0, halves[0]] = part
                    copy_ey(zd, xd, ry).start()

            @pl.when(off_place(zd, xd))
            def _():
                part = cc[zd, xd, 0, 0, halves[1]]
                for sy in others(ny):
                    copy_dy(zd, xd, ny - sy).wait_recv()
                    part = part + dy_in[zd, xd, sy - 1]
                cc[zd, xd, 0, 0, halves[1]] = part
                copy_ex(zd, xd, here[1]).start()

            for ry in others(ny):
                sent_red.append((in_place(zd, xd), copy_ey(zd, xd, ry)))
            sent_red.append((off_place(zd, xd), copy_ex(zd, xd, here[1])))

    def red_four(units):
        for zd, xd in units:

            @pl.when(in_place(zd, xd))
            def _():
                part = cc[zd, xd, 0, 0].astype(F32)
                for xs in range(nx):
                    if xs != xd:
                        copy_ex(zd, xd, xs).wait_recv()
                        part = part + ex_in[zd, xs].astype(F32)
                for sy in others(ny):
                    copy_ey(zd, xd, ny - sy).wait_recv()
                    part = part + ey_in[zd, sy - 1].astype(F32)
                cc[zd, xd, 0, 0] = part.astype(BF16)
                hops, ends, far, lead = way_along_z(zd)
                for h in range(2):
                    for zs in range(nz):
                        if zs in (zd, lead):
                            continue

                        @pl.when(here[0] == zs)
                        def _():
                            copy_z(zd, xd, zs, lead if zs == far else zd, h).start()

            hops, ends, far, lead = way_along_z(zd)
            for zs in range(nz):
                if zs != zd:
                    for h in range(2):
                        to = lead if zs == far else zd
                        sent_red.append(
                            (in_place(zd, xd) & (here[0] == zs), copy_z(zd, xd, zs, to, h))
                        )

    def red_between(units):
        for zd, xd in units:
            hops, ends, far, lead = way_along_z(zd)
            if not hops:
                continue

            @pl.when(in_place(zd, xd) & (here[0] == lead))
            def _():
                for h in range(2):
                    copy_z(zd, xd, far, lead, h).wait_recv()
                    part = cc[zd, xd, 0, 0, halves[h]]
                    cc[zd, xd, 0, 0, halves[h]] = part + zz_in[zd, far, halves[h]]
                    copy_z(zd, xd, lead, zd, h).start()

    def red_five(units):
        for zd, xd in units:

            @pl.when(in_place(zd, xd) & (here[0] == zd))
            def _():
                part = cc[zd, xd, 0, 0].astype(F32)
                hops, ends, far, lead = way_along_z(zd)
                for zs in ends:
                    for h in range(2):
                        copy_z(zd, xd, zs, zd, h).wait_recv()
                    part = part + zz_in[zd if nz == 4 else 0, zs].astype(F32)
                acc[16 : 16 + win_rows] = part

    def red_finish():
        for cond, copy in sent_red:
            if cond is None:
                copy.wait_send()
            else:

                @pl.when(cond)
                def _():
                    copy.wait_send()

    slots, ar_send, ar_recv = s.slots, s.ar_send, s.ar_recv

    def to_all(copy):
        if total > 64:

            def push(d, carry):
                copy(dev(lax.rem(me + d, total))).start()
                return carry

            lax.fori_loop(1, total, push, 0)
            return
        upper = (2 * here[0]) // nz
        for i in range(nz):
            zp = (1 - upper) * (nz - 1 - i) + upper * i
            for rx in reversed(range(nx)):
                for ry in reversed(range(ny)):
                    for rc in reversed(range(nc)):
                        a, b = place((0, rx, ry, rc))
                        target = (zp * nx + lax.rem(a, nx), b)
                        if rx or ry or rc:
                            copy(target).start()
                        else:

                            @pl.when(zp != here[0])
                            def _():
                                copy(target).start()

    def ar_start(r, rows):
        rows = list(rows) + [jnp.zeros((1, LANES), F32)] * (4 - len(rows))
        slots[r, me] = jnp.concatenate(rows, 0)

        def copy(target):
            return pltpu.make_async_remote_copy(
                slots.at[r, me],
                slots.at[r, me],
                ar_send.at[r],
                ar_recv.at[r],
                device_id=target,
                device_id_type=MESH,
            )

        to_all(copy)

    def ar_whole(r):
        others = slots.at[r, pl.ds(0, total - 1)]
        return pltpu.make_async_remote_copy(
            others, others, ar_send.at[r], ar_recv.at[r], device_id=(w, n), device_id_type=MESH
        )

    def ar_wait(r):
        ar_whole(r).wait_recv()
        return jnp.sum(slots[r], axis=0)

    side, side_send, side_recv = s.side, s.side_send, s.side_recv

    def side_start(rows):
        rows = list(rows) + [jnp.zeros((1, LANES), F32)] * (8 - len(rows))
        side[me] = jnp.concatenate(rows, 0)

        def copy(target):
            return pltpu.make_async_remote_copy(
                side.at[me],
                side.at[me],
                side_send,
                side_recv,
                device_id=target,
                device_id_type=MESH,
            )

        to_all(copy)

    def side_whole():
        others = side.at[pl.ds(0, total - 1)]
        return pltpu.make_async_remote_copy(
            others, others, side_send, side_recv, device_id=(w, n), device_id_type=MESH
        )

    halo_send, halo_recv = s.halo_send, s.halo_recv

    def halo_copy(h, ref, i):
        dx, dy = DIRS[i]
        ex, ey = ref.shape[0] - 2, ref.shape[1] - 2

        def source(d, size):
            return pl.ds(1, size) if d == 0 else pl.ds(size if d > 0 else 1, 1)

        def target(d, size):
            return pl.ds(1, size) if d == 0 else pl.ds(0 if d > 0 else size + 1, 1)

        return pltpu.make_async_remote_copy(
            ref.at[source(dx, ex), source(dy, ey)],
            ref.at[target(dx, ex), target(dy, ey)],
            halo_send.at[h, i],
            halo_recv.at[h, i],
            device_id=(lax.rem(w + dx + nw, nw), lax.rem(n + dy + nn, nn)),
            device_id_type=MESH,
        )

    def halo_start(h, ref):
        for i in range(8):
            halo_copy(h, ref, i).start()

    def halo_wait(h, ref):
        for i in range(8):
            halo_copy(h, ref, i).wait_recv()

    def clear_edges(ref, depth):
        ex, ey = ref.shape[0], ref.shape[1]

        @pl.when(w == 0)
        def _():
            ref[0:depth] = jnp.zeros((depth,) + ref.shape[1:], ref.dtype)

        @pl.when(w == nw - 1)
        def _():
            ref[ex - depth : ex] = jnp.zeros((depth,) + ref.shape[1:], ref.dtype)

        @pl.when(n == 0)
        def _():
            ref[:, 0:depth] = jnp.zeros((ex, depth) + ref.shape[2:], ref.dtype)

        @pl.when(n == nn - 1)
        def _():
            ref[:, ey - depth : ey] = jnp.zeros((ex, depth) + ref.shape[2:], ref.dtype)

    def z_three(flat, length):
        rows = flat.shape[0]
        at = jnp.bitwise_and(iota(flat.shape, 0), length - 1)
        before = jnp.where(at == 0, 0.0, pltpu.roll(flat, 1, 0))
        after = jnp.where(at == length - 1, 0.0, pltpu.roll(flat, rows - 1, 0))
        return before.astype(BF16), flat.astype(BF16), after.astype(BF16)

    def put_three(ref, flat, base, stride):
        shape = ref.shape[:3] + (LANES,)
        for c, part in enumerate(z_three(flat, ref.shape[2])):
            lo = c * stride + base
            ref[:, :, :, lo : lo + LANES] = part.reshape(shape)

    def merge_frame(full, low):
        ex, ey = full.shape[0], full.shape[1]
        full[0] = low[0].astype(F32)
        full[ex - 1] = low[ex - 1].astype(F32)
        full[1 : ex - 1, 0] = low[1 : ex - 1, 0].astype(F32)
        full[1 : ex - 1, ey - 1] = low[1 : ex - 1, ey - 1].astype(F32)

    def conv(ref, weight, row0, ext):
        x, y = ext
        rows = x * y * ref.shape[2]
        depth = ref.shape[3]
        acc = None
        for ab in range(9):
            a, b = ab // 3, ab % 3
            window = ref[a : a + x, b : b + y].reshape(rows, depth)
            part = dot(window, weight[row0 + ab * depth : row0 + (ab + 1) * depth, :])
            acc = part if acc is None else acc + part
        return acc

    def conv_back(ref, weight, row0, cin, cout, ext):
        x, y = ext
        rows = x * y * ref.shape[2]
        acc = None
        for ab in range(9):
            a, b = ab // 3, ab % 3
            for c in range(3):
                window = ref[a : a + x, b : b + y, :, c * cout : (c + 1) * cout]
                tap = 26 - (3 * ab + c)
                part = dot_nt(
                    window.reshape(rows, cout),
                    weight[row0 + tap * cin : row0 + (tap + 1) * cin, :],
                )
                acc = part if acc is None else acc + part
        return acc

    def turn(turned, row0, cin):
        if turned is None:
            return
        for tap in range(27):
            block = w_ref[row0 + (26 - tap) * cin : row0 + (27 - tap) * cin, :]
            turned[tap * C1 : (tap + 1) * C1, :] = block.T

    def conv_in(ref, turned, row0, cin):
        if turned is None:
            return conv_back(ref, w_ref, row0, cin, C1, (X, Y))
        return conv(ref, turned, 0, (X, Y))

    def conv_grad(ref, low, row0, ext):
        x, y = ext
        rows = x * y * ref.shape[2]
        depth = ref.shape[3]
        for ab in range(9):
            a, b = ab // 3, ab % 3
            window = ref[a : a + x, b : b + y].reshape(rows, depth)
            g_ref[row0 + ab * depth : row0 + (ab + 1) * depth, :] = dot_tn(window, low).astype(BF16)

    def col_sum(v):
        return jnp.sum(v, axis=0, keepdims=True)

    def own(ref):
        return ref[1 : ref.shape[0] - 1, 1 : ref.shape[1] - 1]

    def flat(v):
        return v.reshape(-1, v.shape[-1])

    pair = s.pair

    def pool(v):
        v = v.reshape(X, Y, Z, LANES)
        v = v[0] + v[1]
        v = v.reshape(CY, 2, Z, LANES)
        v = v[:, 0] + v[:, 1]
        pair[0 : CY * Z] = v.reshape(CY * Z, LANES)
        return pair[pl.ds(0, VC, stride=2), :] + pair[pl.ds(1, VC, stride=2), :]

    def spread(v):
        pair[pl.ds(0, VC, stride=2), :] = v
        pair[pl.ds(1, VC, stride=2), :] = v
        u = pair[0 : CY * Z].reshape(CY, 1, Z, LANES)
        u = jnp.broadcast_to(u, (CY, 2, Z, LANES)).reshape(1, Y, Z, LANES)
        return jnp.broadcast_to(u, (X, Y, Z, LANES)).reshape(V, LANES)

    def stats(total_rows, count):
        half = total_rows.shape[0] // 2
        parts = [total_rows[i : i + 1] for i in range(2 * half)]
        mean = jnp.concatenate(parts[:half], 1) / count
        spread_v = jnp.concatenate(parts[half:], 1) / count - mean * mean
        return mean, lax.rsqrt(spread_v + EPS_NORM)

    def ready(zd, xd):
        p = (zd * nx + xd) * nn
        low = 16 * (lay.begin[p] - 1)
        return 3 if low < ROW_MID else 2 if low < ROW_PSI else 1 if low < ROW_DEC2 else 0

    units = [(zd, xd) for zd in range(nz) for xd in range(nx)]
    units_a, units_b, units_c, units_d = [
        [u for u in units if ready(*u) == k] for k in range(4)
    ]
    g_ref[0:32] = jnp.zeros((32, LANES), BF16)
    g_ref[ROW_PSI:ROWS_A] = jnp.zeros((ROWS_A - ROW_PSI, LANES), BF16)
    g_ref[ROW_TAIL:] = jnp.zeros((g_ref.shape[0] - ROW_TAIL, LANES), BF16)

    in_slots, in_send, in_recv = s.in_slots, s.in_send, s.in_recv

    def entry_grad(low):
        rows = [jnp.zeros((ROW_IN, LANES), F32)]
        for ab in range(9):
            a, b = ab // 3, ab % 3
            patch = entry[a + 1 : a + 1 + X, b + 1 : b + 1 + Y].reshape(V, LANES)
            block = dot_tn(patch, low)
            for c in range(3):
                rows.append(col_sum(block[c * Z : (c + 1) * Z]))
        return jnp.concatenate(rows, 0)

    def in_copy(k):
        return pltpu.make_async_remote_copy(
            in_slots.at[k, me],
            in_slots.at[k, me],
            in_send.at[k],
            in_recv.at[k],
            device_id=(0, 0),
            device_id_type=MESH,
        )

    def in_whole(k):
        others_in = in_slots.at[k, pl.ds(0, total - 1)]
        return pltpu.make_async_remote_copy(
            others_in, others_in, in_send.at[k], in_recv.at[k], device_id=(w, n), device_id_type=MESH
        )

    tap_at = iota((32, LANES), 0) == iota((32, LANES), 1) + ROW_IN

    def in_put(k, block):
        in_slots[k, me] = block.astype(in_slots.dtype)

        @pl.when(me != 0)
        def _():
            in_copy(k).start()

    cts, ct_send, ct_recv = s.cts, s.ct_send, s.ct_recv
    ct_rows = [ct_ref[...]] * 3 + [jnp.zeros((X * Y, LANES - 3 * Z), F32)]
    cts[4] = jnp.concatenate(ct_rows, 1)

    def ct_copy(i):
        dx, dy = DIRS[i]
        return pltpu.make_async_remote_copy(
            cts.at[4],
            cts.at[3 * (1 - dx) + 1 - dy],
            ct_send.at[i],
            ct_recv.at[i],
            device_id=(lax.rem(w + dx + nw, nw), lax.rem(n + dy + nn, nn)),
            device_id_type=MESH,
        )

    for i in range(8):
        ct_copy(i).start()

    step(gather_one, 1)

    quick_wait()
    tail = quick[32:48, :].astype(F32)
    used_rows = CLASSES * (C1 + 1) // LANES
    used_lanes = CLASSES * (C1 + 1) % LANES
    rolled = pltpu.roll(tail, LANES - used_lanes, 1)
    lane_id = iota((1, LANES), 1)

    def tail_row(q):
        r = used_rows + q
        return jnp.where(
            lane_id < LANES - used_lanes, rolled[r : r + 1], rolled[r + 1 : r + 2]
        )

    gains = [tail_row(q) for q in range(6)]
    shifts = [tail_row(6 + q) for q in range(6)]
    gain = [gains[0], gains[1], jnp.concatenate(gains[2:4], 1), gains[4], gains[5]]
    shift = [shifts[0], shifts[1], jnp.concatenate(shifts[2:4], 1), shifts[4], shifts[5]]

    def select_head(j, r):
        return onehot(
            LANES * r + iota((LANES, LANES), 0) == CLASSES * iota((LANES, LANES), 1) + j
        )

    tail_low = tail.astype(BF16)
    head_rows = []
    for j in range(CLASSES):
        row = None
        for r in range(CLASSES):
            part = dot(tail_low, select_head(j, r))[r : r + 1]
            row = part if row is None else row + part
        head_rows.append(row)
    head_t = jnp.concatenate(head_rows + [jnp.zeros((8 - CLASSES, LANES), F32)], 0).astype(BF16)
    bias_row = tail[used_rows : used_rows + 1]
    bias_col = jnp.sum(
        jnp.where(iota((8, LANES), 0) == iota((8, LANES), 1), bias_row, 0.0), axis=1, keepdims=True
    )
    bias_col = jnp.where(iota((8, 1), 0) < CLASSES, bias_col, 0.0)

    def pick_half(h, rows):
        return onehot(iota((2 * rows, rows), 0) == 2 * iota((2 * rows, rows), 1) + h)

    def widen(block, rows):
        block = block.astype(F32)
        lower = jnp.where(lane_id < GATE, block, 0.0).astype(BF16)
        upper = jnp.where(lane_id < GATE, pltpu.roll(block, GATE, 1), 0.0).astype(BF16)
        both = dot(pick_half(0, rows), lower) + dot(pick_half(1, rows), upper)
        return both.astype(BF16)

    def narrow_back(block, rows):
        low = block.astype(BF16)
        lower = dot_tn(pick_half(0, rows), low)
        upper = dot_tn(pick_half(1, rows), low)
        return (lower + pltpu.roll(upper, GATE, 1)).astype(BF16)

    front = quick[0:32, :].astype(F32)
    step(gather_two, 0)
    step(gather_one, 2)
    we = s.we
    for ab in range(9):
        taps = [
            jnp.broadcast_to(front[ROW_IN + 3 * ab + c : ROW_IN + 3 * ab + c + 1], (Z, LANES))
            for c in range(3)
        ]
        taps.append(jnp.zeros((LANES - 3 * Z, LANES), F32))
        we[ab * LANES : (ab + 1) * LANES] = jnp.concatenate(taps, 0).astype(BF16)

    shuffle = onehot(
        iota((C2, C2), 1)
        == jnp.bitwise_and(iota((C2, C2), 0), 1) * C1 + lax.shift_right_logical(iota((C2, C2), 0), 1)
    )
    valid = marks_ref[1:2].astype(F32)
    count_row = jnp.broadcast_to(jnp.sum(valid, axis=1, keepdims=True), (1, LANES))

    for i in range(8):
        ct_copy(i).wait_recv()

    entry = s.entry
    zz, ll = iota((Z, LANES), 0), iota((Z, LANES), 1)
    band = jnp.where((jnp.bitwise_and(ll, Z - 1) == zz + ll // Z - 1) & (ll < 3 * Z), 1.0, 0.0)
    for ex in range(X + 4):
        bx = (ex - 2 + X) // X
        lx = ex - 2 - (bx - 1) * X
        for ey in range(Y + 4):
            by = (ey - 2 + Y) // Y
            ly = ey - 2 - (by - 1) * Y
            row = cts[3 * bx + by, lx * Y + ly : lx * Y + ly + 1]
            entry[ex, ey] = (jnp.broadcast_to(row, (Z, LANES)) * band).astype(BF16)
    clear_edges(entry, 2)
    step(gather_two, 1)
    step(gather_three, 0)
    step(gather_one, 3)
    raw1 = s.raw1
    raw1[...] = conv(entry, we, 0, (XE, YE)).reshape(XE, YE, Z, LANES)
    mine = flat(own(raw1))
    ar_start(0, [col_sum(mine), col_sum(mine * mine), count_row])
    if quarter == 1:
        step(gather_two, 2)
        step(gather_three, 1)
    else:
        for d in range(1, nz):
            at_distance(d, gather_one)
        for k in range(3):
            gather(gather_two, k)
        for k in range(2):
            gather(gather_three, k)
    sums = ar_wait(0)
    valid_count = sums[2:3, 0:1]
    mean1, inv1 = stats(sums[0:2], voxels)
    v = (flat(raw1[...]) - mean1) * inv1 * gain[0] + shift[0]
    pad1 = s.pad1
    put_three(pad1, v * jax.nn.sigmoid(v), 0, C1)
    clear_edges(pad1, 1)

    gather(gather_two, 3)
    gather(gather_three, 2)
    gather(gather_three, 3)
    gather(gather_four, 0)
    raw2, low2 = s.raw2, s.low2
    mine = conv(pad1, w_ref, ROW_ENC, (X, Y))
    raw2[1 : XE - 1, 1 : YE - 1] = mine.reshape(X, Y, Z, C1)
    low2[1 : XE - 1, 1 : YE - 1] = mine.astype(BF16).reshape(X, Y, Z, C1)
    ar_start(1, [col_sum(mine), col_sum(mine * mine)])
    halo_start(0, low2)
    turn(s.turn2, ROW_ENC, C1)
    sums = ar_wait(1)
    mean2, inv2 = stats(sums[0:2], voxels)
    v = (mine - mean2) * inv2 * gain[1] + shift[1]
    skip_own = v * jax.nn.sigmoid(v)

    gather(gather_four, 1)
    pool_in = s.pool_in
    pool_in[1 : CX + 1, 1 : CY + 1] = (pool(skip_own) * 0.125).astype(BF16).reshape(CX, CY, CZ, C1)
    halo_start(1, pool_in)
    wm = s.wm
    for tap in range(27):
        part = dot_tn(shuffle, w_ref[ROW_MID + C2 * tap : ROW_MID + C2 * (tap + 1), :]).astype(BF16)
        wm[tap * C1 : (tap + 1) * C1, 0:LANES] = part[0:LANES]
        wm[tap * C1 : (tap + 1) * C1, LANES:C2] = part[LANES:C2]

    psi = w_ref[ROW_PSI : ROW_PSI + 16, :].astype(F32)[0:1]
    psi = jnp.where(lane_id < GATE, psi, 0.0)
    w_x = widen(w_ref[ROW_X : ROW_X + C1 // 2, :], C1 // 2)
    w_g = widen(w_ref[ROW_G : ROW_G + C2 // 2, :], C2 // 2)
    halo_wait(0, low2)
    merge_frame(raw2, low2)
    v = (flat(raw2[...]) - mean2) * inv2 * gain[1] + shift[1]
    skip = s.skip
    skip_all = v * jax.nn.sigmoid(v)
    skip[...] = skip_all.reshape(XE, YE, Z, C1)
    mix = s.mix
    mix[...] = dot(skip_all.astype(BF16), w_x).reshape(XE, YE, Z, LANES)
    halo_wait(1, pool_in)
    clear_edges(pool_in, 1)
    pad_mid = s.pad_mid
    put_three(pad_mid, flat(pool_in[...].astype(F32)), 0, C1)
    raw3, low3 = s.raw3, s.low3
    mine = conv(pad_mid, wm, 0, (CX, CY))
    raw3[1 : CX + 1, 1 : CY + 1] = mine.reshape(CX, CY, CZ, C2)
    low3[1 : CX + 1, 1 : CY + 1] = mine.astype(BF16).reshape(CX, CY, CZ, C2)
    sum_v, square_v = col_sum(mine), col_sum(mine * mine)
    ar_start(
        2, [sum_v[:, 0:C1], sum_v[:, C1:C2], square_v[:, 0:C1], square_v[:, C1:C2]]
    )
    halo_start(2, low3)
    in_put(
        0,
        entry_grad(((flat(own(raw1)) - mean1) * inv1).astype(BF16))
        + jnp.where(
            iota((32, LANES), 0) == 0,
            col_sum(jnp.where(tap_at, entry_grad(jnp.ones((V, LANES), BF16)), 0.0)),
            0.0,
        ),
    )
    sums = ar_wait(2)
    mean3, inv3 = stats(sums, coarse_voxels)
    halo_wait(2, low3)
    merge_frame(raw3, low3)
    v = (flat(raw3[...]) - mean3) * inv3 * gain[2] + shift[2]
    coarse = (v * jax.nn.sigmoid(v)).astype(BF16).reshape(CX + 2, CY + 2, CZ, C2)
    coarse_own = flat(coarse[1 : CX + 1, 1 : CY + 1])
    frame = (CY + 2) * CZ
    doubled = onehot(
        iota((2 * frame, frame), 1) == lax.shift_right_logical(iota((2 * frame, frame), 0), 1)
    )
    tall = s.tall
    for cx in range(CX + 2):
        tall[cx] = (
            dot(doubled, coarse[cx].reshape(frame, C2)).astype(BF16).reshape(CY + 2, Z, C2)
        )

    def expand(u):
        u = jnp.concatenate([u[(i + 1) // 2 : (i + 1) // 2 + 1] for i in range(XE)], 0)
        return jnp.concatenate([u[:, (j + 1) // 2 : (j + 1) // 2 + 1] for j in range(YE)], 1)

    gate_c = dot(flat(tall[...]), w_g).reshape(CX + 2, CY + 2, Z, LANES)
    mixed_in = flat(mix[...] + expand(gate_c))
    mix[...] = mixed_in.reshape(XE, YE, Z, LANES)
    mixed = mixed_in * jax.nn.sigmoid(mixed_in)
    att = jax.nn.sigmoid(jnp.sum(mixed * psi, axis=1, keepdims=True))
    attention = s.attention
    attention[...] = jnp.broadcast_to(att, (XE * YE * Z, LANES)).reshape(XE, YE, Z, LANES)
    pad_join = s.pad_join
    put_three(pad_join, flat(skip[...] * attention[...]), 0, C1 + C2)
    for half in range(2):
        piece = flat(tall[:, :, :, half * C1 : (half + 1) * C1].astype(F32))
        for c, part in enumerate(z_three(piece, Z)):
            lo = c * (C1 + C2) + C1 + half * C1
            pad_join[:, :, :, lo : lo + C1] = expand(part.reshape(CX + 2, CY + 2, Z, C1))
    clear_edges(pad_join, 1)

    gather(gather_four, 2)
    gather(gather_four, 3)
    raw4, low4 = s.raw4, s.low4
    mine = conv(pad_join, w_ref, ROW_DEC1, (X, Y))
    raw4[1 : XE - 1, 1 : YE - 1] = mine.reshape(X, Y, Z, C1)
    low4[1 : XE - 1, 1 : YE - 1] = mine.astype(BF16).reshape(X, Y, Z, C1)
    ar_start(3, [col_sum(mine), col_sum(mine * mine)])
    halo_start(3, low4)
    turn(s.turn5, ROW_DEC2, C1)
    sums = ar_wait(3)
    mean4, inv4 = stats(sums[0:2], voxels)
    halo_wait(3, low4)
    merge_frame(raw4, low4)
    v = (flat(raw4[...]) - mean4) * inv4 * gain[3] + shift[3]
    pad4 = s.pad4
    put_three(pad4, v * jax.nn.sigmoid(v), 0, C1)
    clear_edges(pad4, 1)

    raw5, low5 = s.raw5, s.low5
    mine = conv(pad4, w_ref, ROW_DEC2, (X, Y))
    raw5[1 : XE - 1, 1 : YE - 1] = mine.reshape(X, Y, Z, C1)
    low5[1 : XE - 1, 1 : YE - 1] = mine.astype(BF16).reshape(X, Y, Z, C1)
    ar_start(4, [col_sum(mine), col_sum(mine * mine)])
    halo_start(4, low5)
    turn(s.turn4, ROW_DEC1, C1 + C2)
    sums = ar_wait(4)
    mean5, inv5 = stats(sums[0:2], voxels)
    hat = (mine - mean5) * inv5
    v = hat * gain[4] + shift[4]
    sg = jax.nn.sigmoid(v)
    act = (v * sg).astype(BF16)

    logits = dot_nt(head_t, act) + bias_col
    real = iota((8, V), 0) < CLASSES
    logits = jnp.where(real, logits, -1e30)
    hot = iota((8, V), 0) == marks_ref[0:1]
    top = jnp.max(logits, axis=0, keepdims=True)
    log_total = top + jnp.log(jnp.sum(jnp.exp(logits - top), axis=0, keepdims=True))
    picked = jnp.sum(jnp.where(hot, logits, 0.0), axis=0, keepdims=True)
    loss = jnp.sum(valid * (log_total - picked), axis=1, keepdims=True)
    probs = jnp.exp(logits - log_total)
    g_logits = valid * (probs - jnp.where(hot, 1.0, 0.0)) / valid_count
    g_low = g_logits.astype(BF16)
    head_grad = dot(g_low, act)
    bias_grad = jnp.sum(g_low.astype(F32), axis=1, keepdims=True)
    bias_line = jnp.sum(
        jnp.where(iota((8, LANES), 0) == iota((8, LANES), 1), bias_grad, 0.0), axis=0, keepdims=True
    )
    dy = dot_tn(g_low, head_t) * silu_grad(v, sg)

    def norm_back(r, h, dy, hat, raw, mean, inv, gain_v, ext, count, names2, extra):
        dyf, dyl = names2
        ex, ey = ext[0] + 2, ext[1] + 2
        width = dy.shape[1]
        shaped = dy.reshape(ext + (width,))
        dyf[1 : ex - 1, 1 : ey - 1] = shaped
        dyl[1 : ex - 1, 1 : ey - 1] = shaped.astype(BF16)
        first, second = col_sum(dy), col_sum(dy * hat)
        rows = [first[:, i : i + LANES] for i in range(0, width, LANES)]
        rows += [second[:, i : i + LANES] for i in range(0, width, LANES)]
        ar_start(r, rows + extra)
        halo_start(h, dyl)
        return rows

    def norm_back_end(r, h, raw, mean, inv, gain_v, count, names2):
        dyf, dyl = names2
        sums = ar_wait(r)
        halo_wait(h, dyl)
        merge_frame(dyf, dyl)
        width = dyf.shape[3]
        k = width // LANES
        one = jnp.concatenate([sums[i : i + 1] for i in range(k)], 1)
        two = jnp.concatenate([sums[k + i : k + i + 1] for i in range(k)], 1)
        hat_all = (flat(raw[...]) - mean) * inv
        back = inv * gain_v * (flat(dyf[...]) - one / count - hat_all * (two / count))
        return sums, back

    grad_shift, grad_gain = {}, {}
    fine = (X, Y, Z)
    norm_back(5, 5, dy, hat, raw5, mean5, inv5, gain[4], fine, voxels, (s.dy5, s.dyl5),
              [jnp.broadcast_to(loss, (1, LANES))])
    halo_wait(4, low5)
    merge_frame(raw5, low5)
    sums, back = norm_back_end(5, 5, raw5, mean5, inv5, gain[4], voxels, (s.dy5, s.dyl5))
    grad_shift[4], grad_gain[4] = [sums[0:1]], [sums[1:2]]
    loss_row = sums[2:3]
    dpad = s.dpad5
    put_three(dpad, back, 0, C1)
    clear_edges(dpad, 1)
    grad_act = conv_in(dpad, s.turn5, ROW_DEC2, C1)
    hat = (flat(own(raw4)) - mean4) * inv4
    v = hat * gain[3] + shift[3]
    dy = grad_act * silu_grad(v, jax.nn.sigmoid(v))
    norm_back(6, 6, dy, hat, raw4, mean4, inv4, gain[3], fine, voxels, (s.dy4, s.dyl4), [])
    conv_grad(pad4, flat(own(dpad)[:, :, :, C1 : 2 * C1]), ROW_DEC2, (X, Y))
    red_one(units_a)
    red_two(units_a)
    sums, back = norm_back_end(6, 6, raw4, mean4, inv4, gain[3], voxels, (s.dy4, s.dyl4))
    grad_shift[3], grad_gain[3] = [sums[0:1]], [sums[1:2]]
    dpad = s.dpad4
    put_three(dpad, back, 0, C1)
    clear_edges(dpad, 1)
    low_raw4 = flat(own(dpad)[:, :, :, C1 : 2 * C1])
    grad_join = conv_in(dpad, s.turn4, ROW_DEC1, C1 + C2)

    grad_gated = grad_join[:, 0:C1]
    skip_own = flat(own(skip))
    att_own = flat(own(attention))
    mixed_own = flat(own(mix))
    sg = jax.nn.sigmoid(mixed_own)
    d_att = jnp.sum(grad_gated * skip_own, axis=1, keepdims=True)
    d_logit = d_att * att_own * (1.0 - att_own)
    psi_grad = col_sum(mixed_own * sg * d_logit)
    d_mixed = d_logit * psi * silu_grad(mixed_own, sg)
    low_fine = d_mixed.astype(BF16)
    low_gc = pool(d_mixed).astype(BF16)
    d_coarse = [
        pool(grad_join[:, C1 : 2 * C1]),
        pool(grad_join[:, 2 * C1 : 3 * C1]),
    ]
    d_coarse = jnp.concatenate(d_coarse, 1) + dot_nt(low_gc, w_g)
    d_coarse = d_coarse.astype(BF16).astype(F32)
    hat = (flat(own(raw3)) - mean3) * inv3
    v = hat * gain[2] + shift[2]
    dy = d_coarse * silu_grad(v, jax.nn.sigmoid(v))
    norm_back(7, 7, dy, hat, raw3, mean3, inv3, gain[2], (CX, CY, CZ), coarse_voxels, (s.dy3, s.dyl3), [])
    side_start([head_grad[0:1], head_grad[1:2], head_grad[2:3], bias_line, psi_grad])
    red_three(units_a)
    d_skip = s.d_skip
    d_skip[...] = grad_gated * att_own + dot_nt(low_fine, w_x)
    conv_grad(pad_join, low_raw4, ROW_DEC1, (X, Y))
    g_ref[ROW_X : ROW_X + C1 // 2, :] = narrow_back(
        dot_tn(skip_own.astype(BF16), low_fine), C1 // 2
    )
    g_ref[ROW_G : ROW_G + C2 // 2, :] = narrow_back(dot_tn(coarse_own, low_gc), C2 // 2)
    red_one(units_b)
    sums, back = norm_back_end(7, 7, raw3, mean3, inv3, gain[2], coarse_voxels, (s.dy3, s.dyl3))
    grad_shift[2], grad_gain[2] = [sums[0:1], sums[1:2]], [sums[2:3], sums[3:4]]
    dpad = s.dpad3
    put_three(dpad, back[:, 0:C1], 0, C2)
    put_three(dpad, back[:, C1:C2], C1, C2)
    clear_edges(dpad, 1)
    low_raw3 = flat(own(dpad)[:, :, :, C2 : 2 * C2])
    d_pool = conv_back(dpad, wm, 0, C1, C2, (CX, CY))
    grad_skip = d_skip[...] + spread(d_pool) * 0.125
    hat = (flat(own(raw2)) - mean2) * inv2
    v = hat * gain[1] + shift[1]
    dy = grad_skip * silu_grad(v, jax.nn.sigmoid(v))
    norm_back(8, 8, dy, hat, raw2, mean2, inv2, gain[1], fine, voxels, (s.dy2, s.dyl2), [])
    red_two(units_b)
    for ab in range(9):
        window = pad_mid[ab // 3 : ab // 3 + CX, ab % 3 : ab % 3 + CY].reshape(VC, 3 * C1)
        block = dot_tn(window, low_raw3).astype(BF16)
        for c in range(3):
            stacked = block[c * C1 : (c + 1) * C1]
            stacked = jnp.concatenate([stacked[:, 0:C1], stacked[:, C1:C2]], 0)
            lo = ROW_MID + (3 * ab + c) * C2
            g_ref[lo : lo + C2, :] = dot(shuffle, stacked).astype(BF16)
    red_one(units_c)
    red_four(units_a)
    red_two(units_c)
    sums, back = norm_back_end(8, 8, raw2, mean2, inv2, gain[1], voxels, (s.dy2, s.dyl2))
    grad_shift[1], grad_gain[1] = [sums[0:1]], [sums[1:2]]
    dpad = s.dpad2
    put_three(dpad, back, 0, C1)
    clear_edges(dpad, 1)
    low_raw2 = flat(own(dpad)[:, :, :, C1 : 2 * C1])
    conv_grad(pad1, low_raw2, ROW_ENC, (X, Y))
    red_one(units_d)
    red_between(units_a)
    red_three(units_b)
    grad_act = conv_in(dpad, s.turn2, ROW_ENC, C1)
    hat1 = (flat(own(raw1)) - mean1) * inv1
    v = hat1 * gain[0] + shift[0]
    dy = grad_act * silu_grad(v, jax.nn.sigmoid(v))
    low_raw1 = dy.astype(BF16)
    red_two(units_d)
    red_three(units_c)
    ar_start(9, [col_sum(dy), col_sum(dy * hat1)])
    entry_block = entry_grad(low_raw1)
    red_three(units_d)
    red_four(units_b)
    red_four(units_c)
    in_put(1, entry_block)
    red_four(units_d)
    red_between(units_b)
    red_between(units_c)
    red_between(units_d)

    sums = ar_wait(9)
    grad_shift[0], grad_gain[0] = [sums[0:1]], [sums[1:2]]
    side_whole().wait_recv()
    small = jnp.sum(side[...], axis=0)
    flat_rows = []
    for r in range(CLASSES):
        row = None
        for j in range(CLASSES):
            part = lax.dot_general(
                small,
                select_head(j, r).astype(F32),
                (((1,), (1,)), ((), ())),
                preferred_element_type=F32,
                precision=lax.Precision.HIGHEST,
            )[j : j + 1]
            row = part if row is None else row + part
        flat_rows.append(row)
    later = []
    for group in (grad_gain, grad_shift):
        for layer in range(5):
            later += group[layer]
    later = [pltpu.roll(row, used_lanes, 1) for row in later]
    flat_rows.append(jnp.where(lane_id < used_lanes, small[3:4], later[0]))
    for q in range(1, 12):
        flat_rows.append(jnp.where(lane_id < used_lanes, later[q - 1], later[q]))
    flat_rows.append(jnp.where(lane_id < used_lanes, later[11], 0.0))
    tail_grad = jnp.concatenate(flat_rows, 0)
    psi_row = jnp.where(lane_id < GATE, small[4:5], 0.0)
    scalar_out[...] = jnp.concatenate(
        [loss_row, jnp.broadcast_to(valid_count, (1, LANES)), jnp.zeros((6, LANES), F32)], 0
    )


    position = (
        me * lay.rows * LANES
        + iota((lay.rows, LANES), 0) * LANES
        + iota((lay.rows, LANES), 1)
    )
    limits = STARTS + (USED, total * lay.rows * LANES)

    def segment_lines(square):
        rows = []
        for k in range(len(limits) - 1):
            member = (position >= limits[k]) & (position < limits[k + 1])
            rows.append(col_sum(jnp.where(member, square, 0.0)))
        return rows

    weight_lines = segment_lines(param_ref[...] * param_ref[...])
    red_five(units)
    base = 16 * (begin - 1) - 16

    def put_row(row, block):
        at = row - base
        rows = block.shape[0]

        @pl.when((at >= 16) & (at + rows <= 16 + win_rows))
        def _():
            acc[pl.ds(pl.multiple_of(at, 16), rows), :] = block

    put_row(ROW_TAIL, tail_grad)
    put_row(ROW_PSI, jnp.concatenate([psi_row, jnp.zeros((15, LANES), F32)], 0))

    @pl.when(me == 0)
    def _():
        for k in range(2):
            in_whole(k).wait_recv()
        with_hat, with_dy = [jnp.sum(in_slots[k].astype(F32), axis=0) for k in range(2)]
        with_one = jnp.sum(jnp.where(tap_at, with_hat[0:1], 0.0), axis=1, keepdims=True)
        with_hat = jnp.where(iota((32, LANES), 0) < ROW_IN, 0.0, with_hat)
        entry_total = with_dy - with_one * (grad_shift[0][0] / voxels)
        entry_total = entry_total - with_hat * (grad_gain[0][0] / voxels)
        at = 16 - 16 * (lay.begin[0] - 1)
        acc[at : at + 32] = acc[at : at + 32] + entry_total * (inv1 * gain[0])

    grad_a = acc[pl.ds(16 + off_a, lay.rows), :]
    late = pltpu.roll(acc[pl.ds(16 + off_b + 1, lay.rows), :], LANES // 2, 1)
    early = pltpu.roll(acc[pl.ds(16 + off_b, lay.rows), :], LANES // 2, 1)
    grad_b = jnp.where(lane < LANES // 2, early, late)
    gradient = jnp.where(position < SPLIT, grad_a, grad_b)
    gradient = jnp.where(position < USED, gradient, 0.0)
    params = param_ref[...]
    new_first = BETA_ONE * first_ref[...] + (1.0 - BETA_ONE) * gradient
    new_second = BETA_TWO * second_ref[...] + (1.0 - BETA_TWO) * gradient * gradient
    first_out[...] = new_first
    second_out[...] = new_second
    update = (
        new_first
        / (1.0 - BETA_ONE**STEP)
        / (jnp.sqrt(new_second / (1.0 - BETA_TWO**STEP)) + EPS_ADAM)
        + DECAY_RATE * params
    )
    param_out[...] = update
    lines = weight_lines + segment_lines(update * update)
    lines = jnp.concatenate(lines, 0)
    lines = jnp.sum(lines, axis=1, keepdims=True)
    k = lines.shape[0]
    line = col_sum(jnp.where(iota((k, LANES), 0) == iota((k, LANES), 1), lines, 0.0))
    ar_start(10, [line])
    sums = ar_wait(10)[0:1]
    parts = len(limits) - 1
    roots = jnp.sqrt(sums)
    scale = jnp.zeros((lay.rows, LANES), F32)
    for k in range(parts):
        member = (position >= limits[k]) & (position < limits[k + 1])
        ratio = roots[:, k : k + 1] / roots[:, parts + k : parts + k + 1]
        scale = jnp.where(member, ratio, scale)
    param_out[...] = param_ref[...] - LEARN_RATE * scale * param_out[...]

    gather_end()
    quick_end()
    for zp in range(nz):

        @pl.when((here[0] >= zp) & (here[0] < nz - 1))
        def _():
            for piece in every:
                onward_copy(zp, True, piece).wait_send()

        @pl.when((here[0] <= zp) & (here[0] > 0))
        def _():
            for piece in every:
                onward_copy(zp, False, piece).wait_send()

    red_finish()

    @pl.when(me != 0)
    def _():
        for k in range(2):
            in_copy(k).wait_send()

    for r in range(N_AR):
        ar_whole(r).wait_send()
    side_whole().wait_send()
    for i in range(8):
        ct_copy(i).wait_send()
    for h, framed in enumerate(
        (s.low2, s.pool_in, s.low3, s.low4, s.low5, s.dyl5, s.dyl4, s.dyl3, s.dyl2)
    ):
        for i in range(8):
            halo_copy(h, framed, i).wait_send()


def step_call(nw, nn, ext, ct, marks, params, first, second):
    X, Y, Z = ext
    XE, YE = X + 2, Y + 2
    CX, CY, CZ = X // 2, Y // 2, Z // 2
    total = nw * nn
    framed = (XE, YE, Z)
    small = (CX + 2, CY + 2, CZ)
    dma = pltpu.SemaphoreType.DMA
    rows = params.shape[0]
    lay = Layout(rows * LANES, total)
    nz, nx, ny, nc = grid_of(nw, nn)
    oy = max(ny - 1, 1)
    half = 16 * (-(-lay.window // 32))
    low = lambda *shape: pltpu.VMEM(shape, BF16)
    scratch = dict(
        weights=low(lay.weight_rows, LANES),
        grads=low(lay.grad_rows, LANES),
        natural=pltpu.VMEM((rows + 112, LANES), F32),
        fix=low(total, lay.fix, LANES),
        quick=low(48, LANES),
        quick_send=dma((2,)),
        quick_recv=dma((2,)),
        onward_send=dma((nz, 2, PIECES)),
        gather_send=dma((PIECES,)),
        gather_recv=dma((total, PIECES)),
        red_c=low(nz, nx, ny, nc - 1, lay.window, LANES),
        red_dx=low(nz, nx, oy, half, LANES),
        red_dy=low(nz, nx, oy, lay.window - half, LANES),
        red_ex=low(nz, nx, lay.window, LANES),
        red_ey=low(nz, oy, lay.window, LANES),
        red_z=low(nz if nz == 4 else 1, nz, lay.window, LANES),
        send_core=dma((nz, nx, ny, nc - 1)),
        recv_core=dma((nz, nx, ny, nc - 1)),
        send_dx=dma((nz, nx, oy)),
        recv_dx=dma((nz, nx, oy)),
        send_dy=dma((nz, nx, oy)),
        recv_dy=dma((nz, nx, oy)),
        send_ex=dma((nz, nx)),
        recv_ex=dma((nz, nx)),
        send_ey=dma((nz, nx, oy)),
        recv_ey=dma((nz, oy)),
        send_z=dma((nz, nx, 2)),
        recv_z=dma((nz, nz, 2)),
        acc=pltpu.VMEM((lay.window + 48, LANES), F32),
        in_slots=pltpu.VMEM((2, total, 32, LANES), F32 if total <= 64 else BF16),
        in_send=dma((2,)),
        in_recv=dma((2,)),
        slots=pltpu.VMEM((N_AR, total, 4, LANES), F32),
        ar_send=dma((N_AR,)),
        ar_recv=dma((N_AR,)),
        side=pltpu.VMEM((total, 8, LANES), F32),
        side_send=dma,
        side_recv=dma,
        halo_send=dma((N_HALO, 8)),
        halo_recv=dma((N_HALO, 8)),
        cts=pltpu.VMEM((9, X * Y, LANES), F32),
        ct_send=dma((8,)),
        ct_recv=dma((8,)),
        pair=pltpu.VMEM((CY * Z, LANES), F32),
        we=pltpu.VMEM((9 * LANES, LANES), BF16),
        wm=pltpu.VMEM((27 * C1, C2), BF16),
        entry=pltpu.VMEM((X + 4, Y + 4, Z, LANES), BF16),
        raw1=pltpu.VMEM(framed + (C1,), F32),
        pad1=pltpu.VMEM(framed + (3 * C1,), BF16),
        raw2=pltpu.VMEM(framed + (C1,), F32),
        low2=pltpu.VMEM(framed + (C1,), BF16),
        pool_in=pltpu.VMEM(small + (C1,), BF16),
        skip=pltpu.VMEM(framed + (C1,), F32),
        mix=pltpu.VMEM(framed + (LANES,), F32),
        attention=pltpu.VMEM(framed + (LANES,), F32),
        pad_mid=pltpu.VMEM(small + (3 * C1,), BF16),
        raw3=pltpu.VMEM(small + (C2,), F32),
        low3=pltpu.VMEM(small + (C2,), BF16),
        tall=pltpu.VMEM((CX + 2, CY + 2, Z, C2), BF16),
        pad_join=pltpu.VMEM(framed + (3 * (C1 + C2),), BF16),
        raw4=pltpu.VMEM(framed + (C1,), F32),
        low4=pltpu.VMEM(framed + (C1,), BF16),
        pad4=pltpu.VMEM(framed + (3 * C1,), BF16),
        raw5=pltpu.VMEM(framed + (C1,), F32),
        low5=pltpu.VMEM(framed + (C1,), BF16),
        dy5=pltpu.VMEM(framed + (C1,), F32),
        dyl5=pltpu.VMEM(framed + (C1,), BF16),
        dpad5=pltpu.VMEM(framed + (3 * C1,), BF16),
        dy4=pltpu.VMEM(framed + (C1,), F32),
        dyl4=pltpu.VMEM(framed + (C1,), BF16),
        dpad4=pltpu.VMEM(framed + (3 * C1,), BF16),
        dy3=pltpu.VMEM(small + (C2,), F32),
        dyl3=pltpu.VMEM(small + (C2,), BF16),
        dpad3=pltpu.VMEM(small + (3 * C2,), BF16),
        dy2=pltpu.VMEM(framed + (C1,), F32),
        dyl2=pltpu.VMEM(framed + (C1,), BF16),
        dpad2=pltpu.VMEM(framed + (3 * C1,), BF16),
        d_skip=pltpu.VMEM((X * Y * Z, C1), F32),
    )
    if total <= 64:
        scratch.update(
            turn2=low(27 * C1, C1), turn4=low(27 * C1, C1 + C2), turn5=low(27 * C1, C1)
        )
    cfg = types.SimpleNamespace(nw=nw, nn=nn, ext=ext, names=tuple(scratch), lay=lay)
    vmem = pl.BlockSpec(memory_space=pltpu.VMEM)
    return pl.pallas_call(
        functools.partial(step_kernel, cfg),
        out_shape=(
            jax.ShapeDtypeStruct((rows, LANES), F32),
            jax.ShapeDtypeStruct((rows, LANES), F32),
            jax.ShapeDtypeStruct((rows, LANES), F32),
            jax.ShapeDtypeStruct((8, LANES), F32),
        ),
        in_specs=[vmem] * 5,
        out_specs=(vmem,) * 4,
        scratch_shapes=list(scratch.values()),
        compiler_params=pltpu.CompilerParams(
            collective_id=0, has_side_effects=True, vmem_limit_bytes=62 * 1024 * 1024
        ),
    )(ct, marks, params, first, second)


def on_device(params, first_moment, second_moment, ct_image, labels, valid_mask):
    ext = ct_image.shape
    ct = ct_image.astype(F32).reshape(-1, ext[2])
    new_params, new_first, new_second, scalars = step_call(
        lax.axis_size("wide"),
        lax.axis_size("narrow"),
        ext,
        ct,
        jnp.stack([labels.reshape(-1), valid_mask.reshape(-1)]),
        params.reshape(-1, LANES),
        first_moment.reshape(-1, LANES),
        second_moment.reshape(-1, LANES),
    )
    return (
        new_params.reshape(-1),
        new_first.reshape(-1),
        new_second.reshape(-1),
        scalars[0, 0],
        scalars[1, 0],
    )


def solution(mesh):
    in_specs = (
        P(("wide", "narrow")),
        P(("wide", "narrow")),
        P(("wide", "narrow")),
        P("wide", "narrow", None),
        P("wide", "narrow", None),
        P("wide", "narrow", None),
    )
    out_specs = (P(("wide", "narrow")), P(("wide", "narrow")), P(("wide", "narrow")), P(), P())
    return jax.shard_map(
        on_device, mesh=mesh, in_specs=in_specs, out_specs=out_specs, check_vma=False
    )
```

```python
import functools
import types

import jax
import jax.numpy as jnp
from jax import lax
from jax.experimental import pallas as pl
from jax.experimental.pallas import tpu as pltpu
from jax.sharding import PartitionSpec as P

C1 = 128
C2 = 256
GATE = 64
CLASSES = 3
STEP = 10

EPS_NORM = 1e-05
BETA_ONE = 0.9
BETA_TWO = 0.999
EPS_ADAM = 1e-06
DECAY_RATE = 0.01
LEARN_RATE = 0.3

F32 = jnp.float32
BF16 = jnp.bfloat16
MESH = pl.DeviceIdType.MESH
LANES = 128
TILE = 16 * LANES

LENGTHS = (
    27 * C1,
    27 * C1 * C1,
    27 * C1 * C2,
    C1 * GATE,
    C2 * GATE,
    GATE,
    27 * (C1 + C2) * C1,
    27 * C1 * C1,
    (C1 + 1) * CLASSES,
    4 * C1 + C2,
    4 * C1 + C2,
)
STARTS = tuple(sum(LENGTHS[:i]) for i in range(len(LENGTHS)))
USED = sum(LENGTHS)

FRONT = 32 * LANES - STARTS[1]
SPLIT = STARTS[6]
ROW_IN = STARTS[0] + FRONT
ROW_IN = ROW_IN // LANES
ROW_ENC = (STARTS[1] + FRONT) // LANES
ROW_MID = (STARTS[2] + FRONT) // LANES
ROW_X = (STARTS[3] + FRONT) // LANES
ROW_G = (STARTS[4] + FRONT) // LANES
ROW_PSI = (STARTS[5] + FRONT) // LANES
ROWS_A = -(-(SPLIT + FRONT) // TILE) * 16
ROW_DEC1 = ROWS_A
ROW_DEC2 = ROW_DEC1 + (STARTS[7] - SPLIT) // LANES
ROW_TAIL = ROW_DEC1 + (STARTS[8] - SPLIT) // LANES

DIRS = tuple((dx, dy) for dx in (-1, 0, 1) for dy in (-1, 0, 1) if (dx, dy) != (0, 0))

N_AR = 11
N_HALO = 9
PIECES = 3


def grid_of(nw, nn):
    nx = max(k for k in range(1, nw + 1) if nw % k == 0 and k * k <= nw)
    ny = max(nn // 2, 1)
    return nw // nx, nx, ny, nn // ny


class Layout:
    def __init__(self, shard_len, total):
        self.rows = shard_len // LANES
        self.total = total
        self.turn = -(-SPLIT // shard_len)
        self.shift_a = FRONT // LANES
        self.shift_b = ROWS_A - SPLIT // LANES - 1
        begin = [self.first(p) for p in range(total + 1)]
        edge = []
        for p in range(1, total + 1):
            low = self.rows * p + (self.shift_b if p >= self.turn else self.shift_a)
            edge.append(low // 16)
        self.body = min(edge[p] - begin[p] for p in range(total))
        self.gap = max(begin[p + 1] - begin[p] - self.body for p in range(total))
        self.begin = begin
        self.half = -(-self.body // 2)
        self.fix = 16 * (1 + self.gap)
        self.window = 16 * (1 + self.body + self.gap)
        self.weight_rows = 16 * begin[total]
        self.grad_rows = max(16 * (begin[p] - 1) for p in range(total)) + self.window
        self.grad_rows = max(self.grad_rows, self.weight_rows)

    def first(self, p):
        late = (p + self.total - self.turn) // self.total
        return (self.rows * p + self.shift_a + 15 + (self.shift_b + 1 - self.shift_a) * late) // 16


def dot(a, b):
    return jnp.dot(a, b, preferred_element_type=F32)


def dot_nt(a, b):
    return lax.dot_general(a, b, (((1,), (1,)), ((), ())), preferred_element_type=F32)


def dot_tn(a, b):
    return lax.dot_general(a, b, (((0,), (0,)), ((), ())), preferred_element_type=F32)


def iota(shape, dim):
    return lax.broadcasted_iota(jnp.int32, shape, dim)


def onehot(cond):
    return jnp.where(cond, 1.0, 0.0).astype(BF16)


def silu_grad(v, s):
    return s * (1.0 + v * (1.0 - s))


def step_kernel(
    cfg,
    ct_ref,
    marks_ref,
    param_ref,
    first_ref,
    second_ref,
    param_out,
    first_out,
    second_out,
    scalar_out,
    *scr,
):
    s = types.SimpleNamespace(turn2=None, turn4=None, turn5=None)
    s.__dict__.update(zip(cfg.names, scr))
    w_ref, g_ref = s.weights, s.grads
    lay = cfg.lay
    nw, nn = cfg.nw, cfg.nn
    total = nw * nn
    X, Y, Z = cfg.ext
    XE, YE = X + 2, Y + 2
    CX, CY, CZ = X // 2, Y // 2, Z // 2
    V = X * Y * Z
    VC = CX * CY * CZ
    voxels = float(V * total)
    coarse_voxels = voxels / 8.0
    w = lax.axis_index("wide")
    n = lax.axis_index("narrow")
    me = w * nn + n

    def dev(p):
        return (p // nn, lax.rem(p, nn))

    barrier = pltpu.get_barrier_semaphore()

    def greet(d, carry):
        pl.semaphore_signal(
            barrier, inc=1, device_id=dev(lax.rem(me + d, total)), device_id_type=MESH
        )
        return carry

    lax.fori_loop(1, total, greet, 0)

    nz, nx, ny, nc = grid_of(nw, nn)
    here = (w // nx, lax.rem(w, nx), n // nc, lax.rem(n, nc))
    sizes = (nz, nx, ny, nc)

    def place(r):
        z, x, y, c = [
            h if d == 0 else lax.rem(h + d % k, k) for h, d, k in zip(here, r, sizes)
        ]
        return z * nx + x, y * nc + c

    def number(zp, r):
        a, b = place((0,) + r)
        return (zp * nx + lax.rem(a, nx)) * nn + b

    natural = s.natural
    lead = 32
    natural[0:lead] = jnp.zeros((lead, LANES), F32)
    natural[lead : lead + lay.rows] = param_ref[...]
    rest = natural.shape[0] - lead - lay.rows
    natural[lead + lay.rows :] = jnp.zeros((rest, LANES), F32)
    begin = lay.first(me)
    off_a = lay.rows * me + lay.shift_a - 16 * (begin - 1)
    off_b = off_a + lay.shift_b - lay.shift_a
    lane = iota((1, LANES), 1)
    span = 16 * (1 + lay.body + lay.gap)
    row_at = iota((span, LANES), 0) + 16 * (begin - 1)
    as_a = natural[pl.ds(lead - off_a, span), :]
    late = pltpu.roll(natural[pl.ds(lead - off_b, span), :], LANES // 2, 1)
    early = pltpu.roll(natural[pl.ds(lead - off_b - 1, span), :], LANES // 2, 1)
    as_b = jnp.where(lane < LANES // 2, early, late)
    share = jnp.where(row_at < ROWS_A, as_a, as_b).astype(BF16)
    fix = s.fix
    body = 16 * lay.body

    def at_tile(t):
        return pl.multiple_of(16 * t, 16)

    w_ref[pl.ds(at_tile(begin), body), :] = share[16 : 16 + body]
    fix[me] = jnp.concatenate([share[0:16], share[16 + body : 16 + body + 16 * lay.gap]], 0)

    gather_send, gather_recv = s.gather_send, s.gather_recv
    sent = [0] * PIECES
    every = (0, 1, 2)

    def flat_id(zp, r):
        x, y, c = [d % k for d, k in zip(r, sizes[1:])]
        return ((zp * nx + x) * ny + y) * nc + c

    def piece_ref(p, piece):
        if piece == 2:
            return fix.at[p]
        lo = 0 if piece == 0 else lay.half
        size = lay.half if piece == 0 else lay.body - lay.half
        return w_ref.at[pl.ds(at_tile(lay.first(p) + lo), 16 * size)]

    def gather_copy(zp, r, d, piece):
        ref = piece_ref(number(zp, r), piece)
        there = tuple(a - b for a, b in zip(r, d[1:]))
        return pltpu.make_async_remote_copy(
            ref,
            ref,
            gather_send.at[piece],
            gather_recv.at[flat_id(zp, there), piece],
            device_id=place(d),
            device_id_type=MESH,
        )

    def gather_push(zp, r, dests, pieces):
        for piece in pieces:
            for d in dests:
                gather_copy(zp, r, d, piece).start()

    def gather_take(zp, r, piece):
        gather_copy(zp, r, (0, 0, 0, 0), piece).wait_recv()

    along_x = [(0, k, 0, 0) for k in range(1, nx)]
    along_y = [(0, 0, k, 0) for k in range(1, ny)]
    sibling = [(0, 0, 0, k) for k in range(1, nc)]
    mine_r = (0, 0, 0)
    for piece in every:
        split = [len(along_y), len(along_x), len(along_x) + len(along_y)][piece]
        sent[piece] = nz * (len(along_x) + len(along_y) + len(sibling))
        first_hop = [(nx - 1) * len(along_y), (ny - 1) * len(along_x), (nx - 1) * len(along_y)]
        sent[piece] += nz * (first_hop[piece] + (nx * ny - 1) * len(sibling))

    onward_send = s.onward_send

    def onward_copy(zp, up, piece):
        ref = piece_ref(number(zp, mine_r), piece)
        return pltpu.make_async_remote_copy(
            ref,
            ref,
            onward_send.at[zp, int(up), piece],
            gather_recv.at[flat_id(zp, mine_r), piece],
            device_id=place((1 if up else nz - 1, 0, 0, 0)),
            device_id_type=MESH,
        )

    def onward(zp, up, piece):
        @pl.when(here[0] < nz - 1 if up else here[0] > 0)
        def _():
            onward_copy(zp, up, piece).start()

    def gather_own():
        for piece in every:
            for up in (True, False):
                onward(here[0], up, piece)
            gather_push(here[0], mine_r, along_x + along_y + sibling, (piece,))

    def at_distance(d, step):
        if d == 0:
            step(here[0], None)
            return

        @pl.when(here[0] - d >= 0)
        def _():
            step(here[0] - d, True)

        @pl.when(here[0] + d < nz)
        def _():
            step(here[0] + d, False)

    def gather_one(zp, up):
        for piece in every:
            gather_take(zp, mine_r, piece)
            onward(zp, up, piece)
            gather_push(zp, mine_r, along_x + along_y + sibling, (piece,))

    def gather_two(zp, up):
        for piece in every:
            for kx in range(1, nx):
                gather_take(zp, (kx, 0, 0), piece)
                if piece != 1:
                    gather_push(zp, (kx, 0, 0), along_y, (piece,))
                gather_push(zp, (kx, 0, 0), sibling, (piece,))
            for ky in range(1, ny):
                gather_take(zp, (0, ky, 0), piece)
                if piece == 1:
                    gather_push(zp, (0, ky, 0), along_x, (piece,))
                gather_push(zp, (0, ky, 0), sibling, (piece,))

    def gather_three(zp, up):
        for piece in every:
            for kx in range(1, nx):
                for ky in range(1, ny):
                    gather_take(zp, (kx, ky, 0), piece)
                    gather_push(zp, (kx, ky, 0), sibling, (piece,))

    def gather_four(zp):
        for kx in range(nx):
            for ky in range(ny):
                for kc in range(1, nc):
                    for piece in every:
                        gather_take(zp, (kx, ky, kc), piece)
        low, high = zp * nx * nn, (zp + 1) * nx * nn
        if zp == 0:
            w_ref[16 * (lay.begin[0] - 1) : 16 * lay.begin[0]] = fix[0, 0:16]
        else:
            put_gap(low - 1)
        for p in range(low, high - (zp < nz - 1)):
            put_gap(p)

    def put_gap(p):
        tile = lay.begin[p] + lay.body
        for i in range(lay.begin[p + 1] - tile):
            part = fix[p, 16 * (1 + i) : 16 * (2 + i)]
            if tile + i == lay.begin[p + 1] - 1 and p + 1 < total:
                part = part + fix[p + 1, 0:16]
            w_ref[16 * (tile + i) : 16 * (tile + i + 1)] = part

    quick, quick_send, quick_recv = s.quick, s.quick_send, s.quick_recv
    shard_len = lay.rows * LANES
    quick_parts = []
    for row, size in ((0, 32), (ROW_TAIL, 16)):
        owner = 0 if row == 0 else STARTS[8] // shard_len
        at = row - 16 * (lay.begin[owner] - 1)
        quick_parts.append((owner, at, size))

    def quick_copy(k, p):
        lo, size = (0, 32) if k == 0 else (32, 16)
        ref = quick.at[pl.ds(lo, size)]
        return pltpu.make_async_remote_copy(
            ref,
            ref,
            quick_send.at[k],
            quick_recv.at[k],
            device_id=dev(p),
            device_id_type=MESH,
        )

    for k, (owner, at, size) in enumerate(quick_parts):

        @pl.when(me == owner)
        def _():
            lo = 0 if k == 0 else 32
            quick[lo : lo + size] = share[at : at + size]

    pl.semaphore_wait(barrier, total - 1)
    for k, (owner, at, size) in enumerate(quick_parts):

        @pl.when(me == owner)
        def _():
            def push(d, carry):
                quick_copy(k, lax.rem(me + d, total)).start()
                return carry

            lax.fori_loop(1, total, push, 0)

    def quick_wait():
        for k, (owner, at, size) in enumerate(quick_parts):

            @pl.when(me != owner)
            def _():
                quick_copy(k, me).wait_recv()

    def quick_end():
        for k, (owner, at, size) in enumerate(quick_parts):

            @pl.when(me == owner)
            def _():
                whole = w_ref.at[pl.ds(0, (total - 1) * size)]
                pltpu.make_async_remote_copy(
                    whole,
                    whole,
                    quick_send.at[k],
                    quick_recv.at[k],
                    device_id=(w, n),
                    device_id_type=MESH,
                ).wait_send()

    quarter = nz // 4
    quarters = [range(k * quarter, (k + 1) * quarter) for k in range(4)]

    def gather(step, k):
        if step is gather_four:
            for zp in quarters[k]:
                step(zp)
            return
        for d in quarters[k]:
            at_distance(d, step)

    def step(what, d):
        if quarter == 1:
            gather(what, d)

    gather_own()

    def gather_end():
        for piece, count in enumerate(sent):
            if piece == 2:
                ref = fix
                unit = 1
            else:
                ref = w_ref
                unit = 16 * (lay.half if piece == 0 else lay.body - lay.half)
            most = ref.shape[0] // unit
            while count:
                k = min(count, most)
                whole = ref.at[pl.ds(0, k * unit)]
                pltpu.make_async_remote_copy(
                    whole,
                    whole,
                    gather_send.at[piece],
                    gather_recv.at[0, piece],
                    device_id=(w, n),
                    device_id_type=MESH,
                ).wait_send()
                count -= k

    cc, dx_in, dy_in = s.red_c, s.red_dx, s.red_dy
    ex_in, ey_in, zz_in = s.red_ex, s.red_ey, s.red_z
    win_rows = lay.window
    mid_row = 16 * (-(-win_rows // 32))
    halves = (pl.ds(0, mid_row), pl.ds(mid_row, win_rows - mid_row))
    acc = s.acc
    sent_red = []

    def grad_window(zd, xd, ry, rc):
        y = lax.rem(here[2] + ry, ny) if ry else here[2]
        c = lax.rem(here[3] + rc, nc) if rc else here[3]
        p = (zd * nx + xd) * nn + y * nc + c
        return pl.ds(at_tile(lay.first(p) - 1), win_rows)

    def red_copy(step, at_send, at_recv, source, target, to):
        return pltpu.make_async_remote_copy(
            source,
            target,
            step[0].at[at_send],
            step[1].at[at_recv],
            device_id=to,
            device_id_type=MESH,
        )

    def in_place(zd, xd):
        return here[1] == xd

    def off_place(zd, xd):
        return here[1] != xd

    def red_go(cond, copy):
        if cond is None:
            copy.start()
        else:

            @pl.when(cond)
            def _():
                copy.start()

        sent_red.append((cond, copy))

    def others(size):
        return range(1, size)

    def copy_core(zd, xd, ry, k):
        return red_copy(
            (s.send_core, s.recv_core),
            (zd, xd, ry, k - 1),
            (zd, xd, ry, k - 1),
            g_ref.at[grad_window(zd, xd, ry, k)],
            cc.at[zd, xd, ry, k - 1],
            place((0, 0, 0, k)),
        )

    def copy_dx(zd, xd, ry, xs):
        return red_copy(
            (s.send_dx, s.recv_dx),
            (zd, xd, ry - 1),
            (zd, xs, ry - 1),
            cc.at[zd, xd, ry, 0, halves[0]],
            dx_in.at[zd, xs, ry - 1],
            (here[0] * nx + xd, n),
        )

    def copy_dy(zd, xd, ry):
        return red_copy(
            (s.send_dy, s.recv_dy),
            (zd, xd, ry - 1),
            (zd, xd, ny - ry - 1),
            cc.at[zd, xd, ry, 0, halves[1]],
            dy_in.at[zd, xd, ny - ry - 1],
            place((0, 0, ry, 0)),
        )

    def copy_ex(zd, xd, xs):
        return red_copy(
            (s.send_ex, s.recv_ex), (zd, xd), (zd, xs), cc.at[zd, xd, 0, 0], ex_in.at[zd, xs], (here[0] * nx + xd, n)
        )

    def copy_ey(zd, xd, ry):
        return red_copy(
            (s.send_ey, s.recv_ey),
            (zd, xd, ry - 1),
            (zd, ny - ry - 1),
            cc.at[zd, xd, ry, 0],
            ey_in.at[zd, ny - ry - 1],
            place((0, 0, ry, 0)),
        )

    def way_along_z(zd):
        if nz != 4:
            return [], [zs for zs in range(nz) if zs != zd], None, None
        lead = 2 if zd < 2 else 1
        far = 3 if zd < 2 else 0
        near = zd + 1 - 2 * (zd % 2)
        return [(far, lead)], [near, lead], far, lead

    def copy_z(zd, xd, zs, to, h):
        return red_copy(
            (s.send_z, s.recv_z),
            (zd, xd, h),
            (zd, zs, h),
            cc.at[zd, xd, 0, 0, halves[h]],
            zz_in.at[zd if nz == 4 else 0, zs, halves[h]],
            (to * nx + xd, n),
        )

    def red_one(units):
        for zd, xd in units:
            for ry in range(ny):
                for k in others(nc):
                    red_go(None, copy_core(zd, xd, ry, k))

    def red_two(units):
        for zd, xd in units:
            for ry in reversed(range(ny)):
                part = g_ref[grad_window(zd, xd, ry, 0), :]
                for k in others(nc):
                    copy_core(zd, xd, ry, k).wait_recv()
                    part = part + cc[zd, xd, ry, k - 1]
                cc[zd, xd, ry, 0] = part
                if ry:
                    red_go(off_place(zd, xd), copy_dx(zd, xd, ry, here[1]))
                    red_go(off_place(zd, xd), copy_dy(zd, xd, ry))

    def red_three(units):
        for zd, xd in units:

            @pl.when(in_place(zd, xd))
            def _():
                for ry in others(ny):
                    part = cc[zd, xd, ry, 0, halves[0]]
                    for xs in range(nx):
                        if xs != xd:
                            copy_dx(zd, xd, ry, xs).wait_recv()
                            part = part + dx_in[zd, xs, ry - 1]
                    cc[zd, xd, ry, 0, halves[0]] = part
                    copy_ey(zd, xd, ry).start()

            @pl.when(off_place(zd, xd))
            def _():
                part = cc[zd, xd, 0, 0, halves[1]]
                for sy in others(ny):
                    copy_dy(zd, xd, ny - sy).wait_recv()
                    part = part + dy_in[zd, xd, sy - 1]
                cc[zd, xd, 0, 0, halves[1]] = part
                copy_ex(zd, xd, here[1]).start()

            for ry in others(ny):
                sent_red.append((in_place(zd, xd), copy_ey(zd, xd, ry)))
            sent_red.append((off_place(zd, xd), copy_ex(zd, xd, here[1])))

    def red_four(units):
        for zd, xd in units:

            @pl.when(in_place(zd, xd))
            def _():
                part = cc[zd, xd, 0, 0].astype(F32)
                for xs in range(nx):
                    if xs != xd:
                        copy_ex(zd, xd, xs).wait_recv()
                        part = part + ex_in[zd, xs].astype(F32)
                for sy in others(ny):
                    copy_ey(zd, xd, ny - sy).wait_recv()
                    part = part + ey_in[zd, sy - 1].astype(F32)
                cc[zd, xd, 0, 0] = part.astype(BF16)
                hops, ends, far, lead = way_along_z(zd)
                for h in range(2):
                    for zs in range(nz):
                        if zs in (zd, lead):
                            continue

                        @pl.when(here[0] == zs)
                        def _():
                            copy_z(zd, xd, zs, lead if zs == far else zd, h).start()

            hops, ends, far, lead = way_along_z(zd)
            for zs in range(nz):
                if zs != zd:
                    for h in range(2):
                        to = lead if zs == far else zd
                        sent_red.append(
                            (in_place(zd, xd) & (here[0] == zs), copy_z(zd, xd, zs, to, h))
                        )

    def red_between(units):
        for zd, xd in units:
            hops, ends, far, lead = way_along_z(zd)
            if not hops:
                continue

            @pl.when(in_place(zd, xd) & (here[0] == lead))
            def _():
                for h in range(2):
                    copy_z(zd, xd, far, lead, h).wait_recv()
                    part = cc[zd, xd, 0, 0, halves[h]]
                    cc[zd, xd, 0, 0, halves[h]] = part + zz_in[zd, far, halves[h]]
                    copy_z(zd, xd, lead, zd, h).start()

    def red_five(units):
        for zd, xd in units:

            @pl.when(in_place(zd, xd) & (here[0] == zd))
            def _():
                part = cc[zd, xd, 0, 0].astype(F32)
                hops, ends, far, lead = way_along_z(zd)
                for zs in ends:
                    for h in range(2):
                        copy_z(zd, xd, zs, zd, h).wait_recv()
                    part = part + zz_in[zd if nz == 4 else 0, zs].astype(F32)
                acc[16 : 16 + win_rows] = part

    def red_finish():
        for cond, copy in sent_red:
            if cond is None:
                copy.wait_send()
            else:

                @pl.when(cond)
                def _():
                    copy.wait_send()

    slots, ar_send, ar_recv = s.slots, s.ar_send, s.ar_recv

    def to_all(copy):
        if total > 64:

            def push(d, carry):
                copy(dev(lax.rem(me + d, total))).start()
                return carry

            lax.fori_loop(1, total, push, 0)
            return
        upper = (2 * here[0]) // nz
        for i in range(nz):
            zp = (1 - upper) * (nz - 1 - i) + upper * i
            for rx in reversed(range(nx)):
                for ry in reversed(range(ny)):
                    for rc in reversed(range(nc)):
                        a, b = place((0, rx, ry, rc))
                        target = (zp * nx + lax.rem(a, nx), b)
                        if rx or ry or rc:
                            copy(target).start()
                        else:

                            @pl.when(zp != here[0])
                            def _():
                                copy(target).start()

    def ar_start(r, rows):
        rows = list(rows) + [jnp.zeros((1, LANES), F32)] * (4 - len(rows))
        slots[r, me] = jnp.concatenate(rows, 0)

        def copy(target):
            return pltpu.make_async_remote_copy(
                slots.at[r, me],
                slots.at[r, me],
                ar_send.at[r],
                ar_recv.at[r],
                device_id=target,
                device_id_type=MESH,
            )

        to_all(copy)

    def ar_whole(r):
        others = slots.at[r, pl.ds(0, total - 1)]
        return pltpu.make_async_remote_copy(
            others, others, ar_send.at[r], ar_recv.at[r], device_id=(w, n), device_id_type=MESH
        )

    def ar_wait(r):
        ar_whole(r).wait_recv()
        return jnp.sum(slots[r], axis=0)

    side, side_send, side_recv = s.side, s.side_send, s.side_recv

    def side_start(rows):
        rows = list(rows) + [jnp.zeros((1, LANES), F32)] * (8 - len(rows))
        side[me] = jnp.concatenate(rows, 0)

        def copy(target):
            return pltpu.make_async_remote_copy(
                side.at[me],
                side.at[me],
                side_send,
                side_recv,
                device_id=target,
                device_id_type=MESH,
            )

        to_all(copy)

    def side_whole():
        others = side.at[pl.ds(0, total - 1)]
        return pltpu.make_async_remote_copy(
            others, others, side_send, side_recv, device_id=(w, n), device_id_type=MESH
        )

    halo_send, halo_recv = s.halo_send, s.halo_recv

    def halo_copy(h, ref, i):
        dx, dy = DIRS[i]
        ex, ey = ref.shape[0] - 2, ref.shape[1] - 2

        def source(d, size):
            return pl.ds(1, size) if d == 0 else pl.ds(size if d > 0 else 1, 1)

        def target(d, size):
            return pl.ds(1, size) if d == 0 else pl.ds(0 if d > 0 else size + 1, 1)

        return pltpu.make_async_remote_copy(
            ref.at[source(dx, ex), source(dy, ey)],
            ref.at[target(dx, ex), target(dy, ey)],
            halo_send.at[h, i],
            halo_recv.at[h, i],
            device_id=(lax.rem(w + dx + nw, nw), lax.rem(n + dy + nn, nn)),
            device_id_type=MESH,
        )

    def halo_start(h, ref):
        for i in range(8):
            halo_copy(h, ref, i).start()

    def halo_wait(h, ref):
        for i in range(8):
            halo_copy(h, ref, i).wait_recv()

    def clear_edges(ref, depth):
        ex, ey = ref.shape[0], ref.shape[1]

        @pl.when(w == 0)
        def _():
            ref[0:depth] = jnp.zeros((depth,) + ref.shape[1:], ref.dtype)

        @pl.when(w == nw - 1)
        def _():
            ref[ex - depth : ex] = jnp.zeros((depth,) + ref.shape[1:], ref.dtype)

        @pl.when(n == 0)
        def _():
            ref[:, 0:depth] = jnp.zeros((ex, depth) + ref.shape[2:], ref.dtype)

        @pl.when(n == nn - 1)
        def _():
            ref[:, ey - depth : ey] = jnp.zeros((ex, depth) + ref.shape[2:], ref.dtype)

    def z_three(flat, length):
        rows = flat.shape[0]
        at = jnp.bitwise_and(iota(flat.shape, 0), length - 1)
        before = jnp.where(at == 0, 0.0, pltpu.roll(flat, 1, 0))
        after = jnp.where(at == length - 1, 0.0, pltpu.roll(flat, rows - 1, 0))
        return before.astype(BF16), flat.astype(BF16), after.astype(BF16)

    def put_three(ref, flat, base, stride):
        shape = ref.shape[:3] + (LANES,)
        for c, part in enumerate(z_three(flat, ref.shape[2])):
            lo = c * stride + base
            ref[:, :, :, lo : lo + LANES] = part.reshape(shape)

    def merge_frame(full, low):
        ex, ey = full.shape[0], full.shape[1]
        full[0] = low[0].astype(F32)
        full[ex - 1] = low[ex - 1].astype(F32)
        full[1 : ex - 1, 0] = low[1 : ex - 1, 0].astype(F32)
        full[1 : ex - 1, ey - 1] = low[1 : ex - 1, ey - 1].astype(F32)

    def conv(ref, weight, row0, ext):
        x, y = ext
        rows = x * y * ref.shape[2]
        depth = ref.shape[3]
        acc = None
        for ab in range(9):
            a, b = ab // 3, ab % 3
            window = ref[a : a + x, b : b + y].reshape(rows, depth)
            part = dot(window, weight[row0 + ab * depth : row0 + (ab + 1) * depth, :])
            acc = part if acc is None else acc + part
        return acc

    def conv_back(ref, weight, row0, cin, cout, ext):
        x, y = ext
        rows = x * y * ref.shape[2]
        acc = None
        for ab in range(9):
            a, b = ab // 3, ab % 3
            for c in range(3):
                window = ref[a : a + x, b : b + y, :, c * cout : (c + 1) * cout]
                tap = 26 - (3 * ab + c)
                part = dot_nt(
                    window.reshape(rows, cout),
                    weight[row0 + tap * cin : row0 + (tap + 1) * cin, :],
                )
                acc = part if acc is None else acc + part
        return acc

    def turn(turned, row0, cin):
        if turned is None:
            return
        for tap in range(27):
            block = w_ref[row0 + (26 - tap) * cin : row0 + (27 - tap) * cin, :]
            turned[tap * C1 : (tap + 1) * C1, :] = block.T

    def conv_in(ref, turned, row0, cin):
        if turned is None:
            return conv_back(ref, w_ref, row0, cin, C1, (X, Y))
        return conv(ref, turned, 0, (X, Y))

    def conv_grad(ref, low, row0, ext):
        x, y = ext
        rows = x * y * ref.shape[2]
        depth = ref.shape[3]
        for ab in range(9):
            a, b = ab // 3, ab % 3
            window = ref[a : a + x, b : b + y].reshape(rows, depth)
            g_ref[row0 + ab * depth : row0 + (ab + 1) * depth, :] = dot_tn(window, low).astype(BF16)

    def col_sum(v):
        return jnp.sum(v, axis=0, keepdims=True)

    def own(ref):
        return ref[1 : ref.shape[0] - 1, 1 : ref.shape[1] - 1]

    def flat(v):
        return v.reshape(-1, v.shape[-1])

    pair = s.pair

    def pool(v):
        v = v.reshape(X, Y, Z, LANES)
        v = v[0] + v[1]
        v = v.reshape(CY, 2, Z, LANES)
        v = v[:, 0] + v[:, 1]
        pair[0 : CY * Z] = v.reshape(CY * Z, LANES)
        return pair[pl.ds(0, VC, stride=2), :] + pair[pl.ds(1, VC, stride=2), :]

    def spread(v):
        pair[pl.ds(0, VC, stride=2), :] = v
        pair[pl.ds(1, VC, stride=2), :] = v
        u = pair[0 : CY * Z].reshape(CY, 1, Z, LANES)
        u = jnp.broadcast_to(u, (CY, 2, Z, LANES)).reshape(1, Y, Z, LANES)
        return jnp.broadcast_to(u, (X, Y, Z, LANES)).reshape(V, LANES)

    def stats(total_rows, count):
        half = total_rows.shape[0] // 2
        parts = [total_rows[i : i + 1] for i in range(2 * half)]
        mean = jnp.concatenate(parts[:half], 1) / count
        spread_v = jnp.concatenate(parts[half:], 1) / count - mean * mean
        return mean, lax.rsqrt(spread_v + EPS_NORM)

    def ready(zd, xd):
        p = (zd * nx + xd) * nn
        low = 16 * (lay.begin[p] - 1)
        return 3 if low < ROW_MID else 2 if low < ROW_PSI else 1 if low < ROW_DEC2 else 0

    units = [(zd, xd) for zd in range(nz) for xd in range(nx)]
    units_a, units_b, units_c, units_d = [
        [u for u in units if ready(*u) == k] for k in range(4)
    ]
    g_ref[0:32] = jnp.zeros((32, LANES), BF16)
    g_ref[ROW_PSI:ROWS_A] = jnp.zeros((ROWS_A - ROW_PSI, LANES), BF16)
    g_ref[ROW_TAIL:] = jnp.zeros((g_ref.shape[0] - ROW_TAIL, LANES), BF16)

    in_slots, in_send, in_recv = s.in_slots, s.in_send, s.in_recv

    def entry_grad(low):
        rows = [jnp.zeros((ROW_IN, LANES), F32)]
        for ab in range(9):
            a, b = ab // 3, ab % 3
            patch = entry[a + 1 : a + 1 + X, b + 1 : b + 1 + Y].reshape(V, LANES)
            block = dot_tn(patch, low)
            for c in range(3):
                rows.append(col_sum(block[c * Z : (c + 1) * Z]))
        return jnp.concatenate(rows, 0)

    def in_copy(k):
        return pltpu.make_async_remote_copy(
            in_slots.at[k, me],
            in_slots.at[k, me],
            in_send.at[k],
            in_recv.at[k],
            device_id=(0, 0),
            device_id_type=MESH,
        )

    def in_whole(k):
        others_in = in_slots.at[k, pl.ds(0, total - 1)]
        return pltpu.make_async_remote_copy(
            others_in, others_in, in_send.at[k], in_recv.at[k], device_id=(w, n), device_id_type=MESH
        )

    tap_at = iota((32, LANES), 0) == iota((32, LANES), 1) + ROW_IN

    def in_put(k, block):
        in_slots[k, me] = block.astype(in_slots.dtype)

        @pl.when(me != 0)
        def _():
            in_copy(k).start()

    cts, ct_send, ct_recv = s.cts, s.ct_send, s.ct_recv
    ct_rows = [ct_ref[...]] * 3 + [jnp.zeros((X * Y, LANES - 3 * Z), F32)]
    cts[4] = jnp.concatenate(ct_rows, 1)

    def ct_copy(i):
        dx, dy = DIRS[i]
        return pltpu.make_async_remote_copy(
            cts.at[4],
            cts.at[3 * (1 - dx) + 1 - dy],
            ct_send.at[i],
            ct_recv.at[i],
            device_id=(lax.rem(w + dx + nw, nw), lax.rem(n + dy + nn, nn)),
            device_id_type=MESH,
        )

    for i in range(8):
        ct_copy(i).start()

    step(gather_one, 1)

    quick_wait()
    tail = quick[32:48, :].astype(F32)
    used_rows = CLASSES * (C1 + 1) // LANES
    used_lanes = CLASSES * (C1 + 1) % LANES
    rolled = pltpu.roll(tail, LANES - used_lanes, 1)
    lane_id = iota((1, LANES), 1)

    def tail_row(q):
        r = used_rows + q
        return jnp.where(
            lane_id < LANES - used_lanes, rolled[r : r + 1], rolled[r + 1 : r + 2]
        )

    gains = [tail_row(q) for q in range(6)]
    shifts = [tail_row(6 + q) for q in range(6)]
    gain = [gains[0], gains[1], jnp.concatenate(gains[2:4], 1), gains[4], gains[5]]
    shift = [shifts[0], shifts[1], jnp.concatenate(shifts[2:4], 1), shifts[4], shifts[5]]

    def select_head(j, r):
        return onehot(
            LANES * r + iota((LANES, LANES), 0) == CLASSES * iota((LANES, LANES), 1) + j
        )

    tail_low = tail.astype(BF16)
    head_rows = []
    for j in range(CLASSES):
        row = None
        for r in range(CLASSES):
            part = dot(tail_low, select_head(j, r))[r : r + 1]
            row = part if row is None else row + part
        head_rows.append(row)
    head_t = jnp.concatenate(head_rows + [jnp.zeros((8 - CLASSES, LANES), F32)], 0).astype(BF16)
    bias_row = tail[used_rows : used_rows + 1]
    bias_col = jnp.sum(
        jnp.where(iota((8, LANES), 0) == iota((8, LANES), 1), bias_row, 0.0), axis=1, keepdims=True
    )
    bias_col = jnp.where(iota((8, 1), 0) < CLASSES, bias_col, 0.0)

    def pick_half(h, rows):
        return onehot(iota((2 * rows, rows), 0) == 2 * iota((2 * rows, rows), 1) + h)

    def widen(block, rows):
        block = block.astype(F32)
        lower = jnp.where(lane_id < GATE, block, 0.0).astype(BF16)
        upper = jnp.where(lane_id < GATE, pltpu.roll(block, GATE, 1), 0.0).astype(BF16)
        both = dot(pick_half(0, rows), lower) + dot(pick_half(1, rows), upper)
        return both.astype(BF16)

    def narrow_back(block, rows):
        low = block.astype(BF16)
        lower = dot_tn(pick_half(0, rows), low)
        upper = dot_tn(pick_half(1, rows), low)
        return (lower + pltpu.roll(upper, GATE, 1)).astype(BF16)

    front = quick[0:32, :].astype(F32)
    step(gather_two, 0)
    step(gather_one, 2)
    we = s.we
    for ab in range(9):
        taps = [
            jnp.broadcast_to(front[ROW_IN + 3 * ab + c : ROW_IN + 3 * ab + c + 1], (Z, LANES))
            for c in range(3)
        ]
        taps.append(jnp.zeros((LANES - 3 * Z, LANES), F32))
        we[ab * LANES : (ab + 1) * LANES] = jnp.concatenate(taps, 0).astype(BF16)

    shuffle = onehot(
        iota((C2, C2), 1)
        == jnp.bitwise_and(iota((C2, C2), 0), 1) * C1 + lax.shift_right_logical(iota((C2, C2), 0), 1)
    )
    valid = marks_ref[1:2].astype(F32)
    count_row = jnp.broadcast_to(jnp.sum(valid, axis=1, keepdims=True), (1, LANES))

    for i in range(8):
        ct_copy(i).wait_recv()

    entry = s.entry
    zz, ll = iota((Z, LANES), 0), iota((Z, LANES), 1)
    band = jnp.where((jnp.bitwise_and(ll, Z - 1) == zz + ll // Z - 1) & (ll < 3 * Z), 1.0, 0.0)
    for ex in range(X + 4):
        bx = (ex - 2 + X) // X
        lx = ex - 2 - (bx - 1) * X
        for ey in range(Y + 4):
            by = (ey - 2 + Y) // Y
            ly = ey - 2 - (by - 1) * Y
            row = cts[3 * bx + by, lx * Y + ly : lx * Y + ly + 1]
            entry[ex, ey] = (jnp.broadcast_to(row, (Z, LANES)) * band).astype(BF16)
    clear_edges(entry, 2)
    step(gather_two, 1)
    step(gather_three, 0)
    step(gather_one, 3)
    raw1 = s.raw1
    raw1[...] = conv(entry, we, 0, (XE, YE)).reshape(XE, YE, Z, LANES)
    mine = flat(own(raw1))
    ar_start(0, [col_sum(mine), col_sum(mine * mine), count_row])
    if quarter == 1:
        step(gather_two, 2)
        step(gather_three, 1)
    else:
        for d in range(1, nz):
            at_distance(d, gather_one)
        for k in range(3):
            gather(gather_two, k)
        for k in range(2):
            gather(gather_three, k)
    sums = ar_wait(0)
    valid_count = sums[2:3, 0:1]
    mean1, inv1 = stats(sums[0:2], voxels)
    v = (flat(raw1[...]) - mean1) * inv1 * gain[0] + shift[0]
    pad1 = s.pad1
    put_three(pad1, v * jax.nn.sigmoid(v), 0, C1)
    clear_edges(pad1, 1)

    gather(gather_two, 3)
    gather(gather_three, 2)
    gather(gather_three, 3)
    gather(gather_four, 0)
    raw2, low2 = s.raw2, s.low2
    mine = conv(pad1, w_ref, ROW_ENC, (X, Y))
    raw2[1 : XE - 1, 1 : YE - 1] = mine.reshape(X, Y, Z, C1)
    low2[1 : XE - 1, 1 : YE - 1] = mine.astype(BF16).reshape(X, Y, Z, C1)
    ar_start(1, [col_sum(mine), col_sum(mine * mine)])
    halo_start(0, low2)
    turn(s.turn2, ROW_ENC, C1)
    sums = ar_wait(1)
    mean2, inv2 = stats(sums[0:2], voxels)
    v = (mine - mean2) * inv2 * gain[1] + shift[1]
    skip_own = v * jax.nn.sigmoid(v)

    gather(gather_four, 1)
    pool_in = s.pool_in
    pool_in[1 : CX + 1, 1 : CY + 1] = (pool(skip_own) * 0.125).astype(BF16).reshape(CX, CY, CZ, C1)
    halo_start(1, pool_in)
    wm = s.wm
    for tap in range(27):
        part = dot_tn(shuffle, w_ref[ROW_MID + C2 * tap : ROW_MID + C2 * (tap + 1), :]).astype(BF16)
        wm[tap * C1 : (tap + 1) * C1, 0:LANES] = part[0:LANES]
        wm[tap * C1 : (tap + 1) * C1, LANES:C2] = part[LANES:C2]

    psi = w_ref[ROW_PSI : ROW_PSI + 16, :].astype(F32)[0:1]
    psi = jnp.where(lane_id < GATE, psi, 0.0)
    w_x = widen(w_ref[ROW_X : ROW_X + C1 // 2, :], C1 // 2)
    w_g = widen(w_ref[ROW_G : ROW_G + C2 // 2, :], C2 // 2)
    halo_wait(0, low2)
    merge_frame(raw2, low2)
    v = (flat(raw2[...]) - mean2) * inv2 * gain[1] + shift[1]
    skip = s.skip
    skip_all = v * jax.nn.sigmoid(v)
    skip[...] = skip_all.reshape(XE, YE, Z, C1)
    mix = s.mix
    mix[...] = dot(skip_all.astype(BF16), w_x).reshape(XE, YE, Z, LANES)
    halo_wait(1, pool_in)
    clear_edges(pool_in, 1)
    pad_mid = s.pad_mid
    put_three(pad_mid, flat(pool_in[...].astype(F32)), 0, C1)
    raw3, low3 = s.raw3, s.low3
    mine = conv(pad_mid, wm, 0, (CX, CY))
    raw3[1 : CX + 1, 1 : CY + 1] = mine.reshape(CX, CY, CZ, C2)
    low3[1 : CX + 1, 1 : CY + 1] = mine.astype(BF16).reshape(CX, CY, CZ, C2)
    sum_v, square_v = col_sum(mine), col_sum(mine * mine)
    ar_start(
        2, [sum_v[:, 0:C1], sum_v[:, C1:C2], square_v[:, 0:C1], square_v[:, C1:C2]]
    )
    halo_start(2, low3)
    in_put(
        0,
        entry_grad(((flat(own(raw1)) - mean1) * inv1).astype(BF16))
        + jnp.where(
            iota((32, LANES), 0) == 0,
            col_sum(jnp.where(tap_at, entry_grad(jnp.ones((V, LANES), BF16)), 0.0)),
            0.0,
        ),
    )
    sums = ar_wait(2)
    mean3, inv3 = stats(sums, coarse_voxels)
    halo_wait(2, low3)
    merge_frame(raw3, low3)
    v = (flat(raw3[...]) - mean3) * inv3 * gain[2] + shift[2]
    coarse = (v * jax.nn.sigmoid(v)).astype(BF16).reshape(CX + 2, CY + 2, CZ, C2)
    coarse_own = flat(coarse[1 : CX + 1, 1 : CY + 1])
    frame = (CY + 2) * CZ
    doubled = onehot(
        iota((2 * frame, frame), 1) == lax.shift_right_logical(iota((2 * frame, frame), 0), 1)
    )
    tall = s.tall
    for cx in range(CX + 2):
        tall[cx] = (
            dot(doubled, coarse[cx].reshape(frame, C2)).astype(BF16).reshape(CY + 2, Z, C2)
        )

    def expand(u):
        u = jnp.concatenate([u[(i + 1) // 2 : (i + 1) // 2 + 1] for i in range(XE)], 0)
        return jnp.concatenate([u[:, (j + 1) // 2 : (j + 1) // 2 + 1] for j in range(YE)], 1)

    gate_c = dot(flat(tall[...]), w_g).reshape(CX + 2, CY + 2, Z, LANES)
    mixed_in = flat(mix[...] + expand(gate_c))
    mix[...] = mixed_in.reshape(XE, YE, Z, LANES)
    mixed = mixed_in * jax.nn.sigmoid(mixed_in)
    att = jax.nn.sigmoid(jnp.sum(mixed * psi, axis=1, keepdims=True))
    attention = s.attention
    attention[...] = jnp.broadcast_to(att, (XE * YE * Z, LANES)).reshape(XE, YE, Z, LANES)
    pad_join = s.pad_join
    put_three(pad_join, flat(skip[...] * attention[...]), 0, C1 + C2)
    for half in range(2):
        piece = flat(tall[:, :, :, half * C1 : (half + 1) * C1].astype(F32))
        for c, part in enumerate(z_three(piece, Z)):
            lo = c * (C1 + C2) + C1 + half * C1
            pad_join[:, :, :, lo : lo + C1] = expand(part.reshape(CX + 2, CY + 2, Z, C1))
    clear_edges(pad_join, 1)

    gather(gather_four, 2)
    gather(gather_four, 3)
    raw4, low4 = s.raw4, s.low4
    mine = conv(pad_join, w_ref, ROW_DEC1, (X, Y))
    raw4[1 : XE - 1, 1 : YE - 1] = mine.reshape(X, Y, Z, C1)
    low4[1 : XE - 1, 1 : YE - 1] = mine.astype(BF16).reshape(X, Y, Z, C1)
    ar_start(3, [col_sum(mine), col_sum(mine * mine)])
    halo_start(3, low4)
    turn(s.turn5, ROW_DEC2, C1)
    sums = ar_wait(3)
    mean4, inv4 = stats(sums[0:2], voxels)
    halo_wait(3, low4)
    merge_frame(raw4, low4)
    v = (flat(raw4[...]) - mean4) * inv4 * gain[3] + shift[3]
    pad4 = s.pad4
    put_three(pad4, v * jax.nn.sigmoid(v), 0, C1)
    clear_edges(pad4, 1)

    raw5, low5 = s.raw5, s.low5
    mine = conv(pad4, w_ref, ROW_DEC2, (X, Y))
    raw5[1 : XE - 1, 1 : YE - 1] = mine.reshape(X, Y, Z, C1)
    low5[1 : XE - 1, 1 : YE - 1] = mine.astype(BF16).reshape(X, Y, Z, C1)
    ar_start(4, [col_sum(mine), col_sum(mine * mine)])
    halo_start(4, low5)
    turn(s.turn4, ROW_DEC1, C1 + C2)
    sums = ar_wait(4)
    mean5, inv5 = stats(sums[0:2], voxels)
    hat = (mine - mean5) * inv5
    v = hat * gain[4] + shift[4]
    sg = jax.nn.sigmoid(v)
    act = (v * sg).astype(BF16)

    logits = dot_nt(head_t, act) + bias_col
    real = iota((8, V), 0) < CLASSES
    logits = jnp.where(real, logits, -1e30)
    hot = iota((8, V), 0) == marks_ref[0:1]
    top = jnp.max(logits, axis=0, keepdims=True)
    log_total = top + jnp.log(jnp.sum(jnp.exp(logits - top), axis=0, keepdims=True))
    picked = jnp.sum(jnp.where(hot, logits, 0.0), axis=0, keepdims=True)
    loss = jnp.sum(valid * (log_total - picked), axis=1, keepdims=True)
    probs = jnp.exp(logits - log_total)
    g_logits = valid * (probs - jnp.where(hot, 1.0, 0.0)) / valid_count
    g_low = g_logits.astype(BF16)
    head_grad = dot(g_low, act)
    bias_grad = jnp.sum(g_low.astype(F32), axis=1, keepdims=True)
    bias_line = jnp.sum(
        jnp.where(iota((8, LANES), 0) == iota((8, LANES), 1), bias_grad, 0.0), axis=0, keepdims=True
    )
    dy = dot_tn(g_low, head_t) * silu_grad(v, sg)

    def norm_back(r, h, dy, hat, raw, mean, inv, gain_v, ext, count, names2, extra):
        dyf, dyl = names2
        ex, ey = ext[0] + 2, ext[1] + 2
        width = dy.shape[1]
        shaped = dy.reshape(ext + (width,))
        dyf[1 : ex - 1, 1 : ey - 1] = shaped
        dyl[1 : ex - 1, 1 : ey - 1] = shaped.astype(BF16)
        first, second = col_sum(dy), col_sum(dy * hat)
        rows = [first[:, i : i + LANES] for i in range(0, width, LANES)]
        rows += [second[:, i : i + LANES] for i in range(0, width, LANES)]
        ar_start(r, rows + extra)
        halo_start(h, dyl)
        return rows

    def norm_back_end(r, h, raw, mean, inv, gain_v, count, names2):
        dyf, dyl = names2
        sums = ar_wait(r)
        halo_wait(h, dyl)
        merge_frame(dyf, dyl)
        width = dyf.shape[3]
        k = width // LANES
        one = jnp.concatenate([sums[i : i + 1] for i in range(k)], 1)
        two = jnp.concatenate([sums[k + i : k + i + 1] for i in range(k)], 1)
        hat_all = (flat(raw[...]) - mean) * inv
        back = inv * gain_v * (flat(dyf[...]) - one / count - hat_all * (two / count))
        return sums, back

    grad_shift, grad_gain = {}, {}
    fine = (X, Y, Z)
    norm_back(5, 5, dy, hat, raw5, mean5, inv5, gain[4], fine, voxels, (s.dy5, s.dyl5),
              [jnp.broadcast_to(loss, (1, LANES))])
    halo_wait(4, low5)
    merge_frame(raw5, low5)
    sums, back = norm_back_end(5, 5, raw5, mean5, inv5, gain[4], voxels, (s.dy5, s.dyl5))
    grad_shift[4], grad_gain[4] = [sums[0:1]], [sums[1:2]]
    loss_row = sums[2:3]
    dpad = s.dpad5
    put_three(dpad, back, 0, C1)
    clear_edges(dpad, 1)
    grad_act = conv_in(dpad, s.turn5, ROW_DEC2, C1)
    hat = (flat(own(raw4)) - mean4) * inv4
    v = hat * gain[3] + shift[3]
    dy = grad_act * silu_grad(v, jax.nn.sigmoid(v))
    norm_back(6, 6, dy, hat, raw4, mean4, inv4, gain[3], fine, voxels, (s.dy4, s.dyl4), [])
    conv_grad(pad4, flat(own(dpad)[:, :, :, C1 : 2 * C1]), ROW_DEC2, (X, Y))
    red_one(units_a)
    red_two(units_a)
    sums, back = norm_back_end(6, 6, raw4, mean4, inv4, gain[3], voxels, (s.dy4, s.dyl4))
    grad_shift[3], grad_gain[3] = [sums[0:1]], [sums[1:2]]
    dpad = s.dpad4
    put_three(dpad, back, 0, C1)
    clear_edges(dpad, 1)
    low_raw4 = flat(own(dpad)[:, :, :, C1 : 2 * C1])
    grad_join = conv_in(dpad, s.turn4, ROW_DEC1, C1 + C2)

    grad_gated = grad_join[:, 0:C1]
    skip_own = flat(own(skip))
    att_own = flat(own(attention))
    mixed_own = flat(own(mix))
    sg = jax.nn.sigmoid(mixed_own)
    d_att = jnp.sum(grad_gated * skip_own, axis=1, keepdims=True)
    d_logit = d_att * att_own * (1.0 - att_own)
    psi_grad = col_sum(mixed_own * sg * d_logit)
    d_mixed = d_logit * psi * silu_grad(mixed_own, sg)
    low_fine = d_mixed.astype(BF16)
    low_gc = pool(d_mixed).astype(BF16)
    d_coarse = [
        pool(grad_join[:, C1 : 2 * C1]),
        pool(grad_join[:, 2 * C1 : 3 * C1]),
    ]
    d_coarse = jnp.concatenate(d_coarse, 1) + dot_nt(low_gc, w_g)
    d_coarse = d_coarse.astype(BF16).astype(F32)
    hat = (flat(own(raw3)) - mean3) * inv3
    v = hat * gain[2] + shift[2]
    dy = d_coarse * silu_grad(v, jax.nn.sigmoid(v))
    norm_back(7, 7, dy, hat, raw3, mean3, inv3, gain[2], (CX, CY, CZ), coarse_voxels, (s.dy3, s.dyl3), [])
    side_start([head_grad[0:1], head_grad[1:2], head_grad[2:3], bias_line, psi_grad])
    red_three(units_a)
    d_skip = s.d_skip
    d_skip[...] = grad_gated * att_own + dot_nt(low_fine, w_x)
    conv_grad(pad_join, low_raw4, ROW_DEC1, (X, Y))
    g_ref[ROW_X : ROW_X + C1 // 2, :] = narrow_back(
        dot_tn(skip_own.astype(BF16), low_fine), C1 // 2
    )
    g_ref[ROW_G : ROW_G + C2 // 2, :] = narrow_back(dot_tn(coarse_own, low_gc), C2 // 2)
    red_one(units_b)
    sums, back = norm_back_end(7, 7, raw3, mean3, inv3, gain[2], coarse_voxels, (s.dy3, s.dyl3))
    grad_shift[2], grad_gain[2] = [sums[0:1], sums[1:2]], [sums[2:3], sums[3:4]]
    dpad = s.dpad3
    put_three(dpad, back[:, 0:C1], 0, C2)
    put_three(dpad, back[:, C1:C2], C1, C2)
    clear_edges(dpad, 1)
    low_raw3 = flat(own(dpad)[:, :, :, C2 : 2 * C2])
    d_pool = conv_back(dpad, wm, 0, C1, C2, (CX, CY))
    grad_skip = d_skip[...] + spread(d_pool) * 0.125
    hat = (flat(own(raw2)) - mean2) * inv2
    v = hat * gain[1] + shift[1]
    dy = grad_skip * silu_grad(v, jax.nn.sigmoid(v))
    norm_back(8, 8, dy, hat, raw2, mean2, inv2, gain[1], fine, voxels, (s.dy2, s.dyl2), [])
    red_two(units_b)
    for ab in range(9):
        window = pad_mid[ab // 3 : ab // 3 + CX, ab % 3 : ab % 3 + CY].reshape(VC, 3 * C1)
        block = dot_tn(window, low_raw3).astype(BF16)
        for c in range(3):
            stacked = block[c * C1 : (c + 1) * C1]
            stacked = jnp.concatenate([stacked[:, 0:C1], stacked[:, C1:C2]], 0)
            lo = ROW_MID + (3 * ab + c) * C2
            g_ref[lo : lo + C2, :] = dot(shuffle, stacked).astype(BF16)
    red_one(units_c)
    red_four(units_a)
    red_two(units_c)
    sums, back = norm_back_end(8, 8, raw2, mean2, inv2, gain[1], voxels, (s.dy2, s.dyl2))
    grad_shift[1], grad_gain[1] = [sums[0:1]], [sums[1:2]]
    dpad = s.dpad2
    put_three(dpad, back, 0, C1)
    clear_edges(dpad, 1)
    low_raw2 = flat(own(dpad)[:, :, :, C1 : 2 * C1])
    conv_grad(pad1, low_raw2, ROW_ENC, (X, Y))
    red_one(units_d)
    red_between(units_a)
    units_b1 = [u for u in units_b if u[0] < nz - 1]
    units_b2 = [u for u in units_b if u[0] == nz - 1]
    red_three(units_b1)
    grad_act = conv_in(dpad, s.turn2, ROW_ENC, C1)
    hat1 = (flat(own(raw1)) - mean1) * inv1
    v = hat1 * gain[0] + shift[0]
    dy = grad_act * silu_grad(v, jax.nn.sigmoid(v))
    low_raw1 = dy.astype(BF16)
    red_two(units_d)
    red_three(units_b2)
    red_three(units_c)
    ar_start(9, [col_sum(dy), col_sum(dy * hat1)])
    entry_block = entry_grad(low_raw1)
    red_four(units_b1)
    red_three(units_d)
    red_four(units_b2)
    red_between(units_b1)
    red_four(units_c)
    in_put(1, entry_block)
    red_four(units_d)
    red_between(units_b2)
    red_between(units_c)
    red_between(units_d)

    sums = ar_wait(9)
    grad_shift[0], grad_gain[0] = [sums[0:1]], [sums[1:2]]
    side_whole().wait_recv()
    small = jnp.sum(side[...], axis=0)
    flat_rows = []
    for r in range(CLASSES):
        row = None
        for j in range(CLASSES):
            part = lax.dot_general(
                small,
                select_head(j, r).astype(F32),
                (((1,), (1,)), ((), ())),
                preferred_element_type=F32,
                precision=lax.Precision.HIGHEST,
            )[j : j + 1]
            row = part if row is None else row + part
        flat_rows.append(row)
    later = []
    for group in (grad_gain, grad_shift):
        for layer in range(5):
            later += group[layer]
    later = [pltpu.roll(row, used_lanes, 1) for row in later]
    flat_rows.append(jnp.where(lane_id < used_lanes, small[3:4], later[0]))
    for q in range(1, 12):
        flat_rows.append(jnp.where(lane_id < used_lanes, later[q - 1], later[q]))
    flat_rows.append(jnp.where(lane_id < used_lanes, later[11], 0.0))
    tail_grad = jnp.concatenate(flat_rows, 0)
    psi_row = jnp.where(lane_id < GATE, small[4:5], 0.0)
    scalar_out[...] = jnp.concatenate(
        [loss_row, jnp.broadcast_to(valid_count, (1, LANES)), jnp.zeros((6, LANES), F32)], 0
    )


    position = (
        me * lay.rows * LANES
        + iota((lay.rows, LANES), 0) * LANES
        + iota((lay.rows, LANES), 1)
    )
    limits = STARTS + (USED, total * lay.rows * LANES)

    def segment_lines(square):
        rows = []
        for k in range(len(limits) - 1):
            member = (position >= limits[k]) & (position < limits[k + 1])
            rows.append(col_sum(jnp.where(member, square, 0.0)))
        return rows

    weight_lines = segment_lines(param_ref[...] * param_ref[...])
    red_five(units)
    base = 16 * (begin - 1) - 16

    def put_row(row, block):
        at = row - base
        rows = block.shape[0]

        @pl.when((at >= 16) & (at + rows <= 16 + win_rows))
        def _():
            acc[pl.ds(pl.multiple_of(at, 16), rows), :] = block

    put_row(ROW_TAIL, tail_grad)
    put_row(ROW_PSI, jnp.concatenate([psi_row, jnp.zeros((15, LANES), F32)], 0))

    @pl.when(me == 0)
    def _():
        for k in range(2):
            in_whole(k).wait_recv()
        with_hat, with_dy = [jnp.sum(in_slots[k].astype(F32), axis=0) for k in range(2)]
        with_one = jnp.sum(jnp.where(tap_at, with_hat[0:1], 0.0), axis=1, keepdims=True)
        with_hat = jnp.where(iota((32, LANES), 0) < ROW_IN, 0.0, with_hat)
        entry_total = with_dy - with_one * (grad_shift[0][0] / voxels)
        entry_total = entry_total - with_hat * (grad_gain[0][0] / voxels)
        at = 16 - 16 * (lay.begin[0] - 1)
        acc[at : at + 32] = acc[at : at + 32] + entry_total * (inv1 * gain[0])

    grad_a = acc[pl.ds(16 + off_a, lay.rows), :]
    late = pltpu.roll(acc[pl.ds(16 + off_b + 1, lay.rows), :], LANES // 2, 1)
    early = pltpu.roll(acc[pl.ds(16 + off_b, lay.rows), :], LANES // 2, 1)
    grad_b = jnp.where(lane < LANES // 2, early, late)
    gradient = jnp.where(position < SPLIT, grad_a, grad_b)
    gradient = jnp.where(position < USED, gradient, 0.0)
    params = param_ref[...]
    new_first = BETA_ONE * first_ref[...] + (1.0 - BETA_ONE) * gradient
    new_second = BETA_TWO * second_ref[...] + (1.0 - BETA_TWO) * gradient * gradient
    first_out[...] = new_first
    second_out[...] = new_second
    update = (
        new_first
        / (1.0 - BETA_ONE**STEP)
        / (jnp.sqrt(new_second / (1.0 - BETA_TWO**STEP)) + EPS_ADAM)
        + DECAY_RATE * params
    )
    param_out[...] = update
    lines = weight_lines + segment_lines(update * update)
    lines = jnp.concatenate(lines, 0)
    lines = jnp.sum(lines, axis=1, keepdims=True)
    k = lines.shape[0]
    line = col_sum(jnp.where(iota((k, LANES), 0) == iota((k, LANES), 1), lines, 0.0))
    ar_start(10, [line])
    sums = ar_wait(10)[0:1]
    parts = len(limits) - 1
    roots = jnp.sqrt(sums)
    scale = jnp.zeros((lay.rows, LANES), F32)
    for k in range(parts):
        member = (position >= limits[k]) & (position < limits[k + 1])
        ratio = roots[:, k : k + 1] / roots[:, parts + k : parts + k + 1]
        scale = jnp.where(member, ratio, scale)
    param_out[...] = param_ref[...] - LEARN_RATE * scale * param_out[...]

    gather_end()
    quick_end()
    for zp in range(nz):

        @pl.when((here[0] >= zp) & (here[0] < nz - 1))
        def _():
            for piece in every:
                onward_copy(zp, True, piece).wait_send()

        @pl.when((here[0] <= zp) & (here[0] > 0))
        def _():
            for piece in every:
                onward_copy(zp, False, piece).wait_send()

    red_finish()

    @pl.when(me != 0)
    def _():
        for k in range(2):
            in_copy(k).wait_send()

    for r in range(N_AR):
        ar_whole(r).wait_send()
    side_whole().wait_send()
    for i in range(8):
        ct_copy(i).wait_send()
    for h, framed in enumerate(
        (s.low2, s.pool_in, s.low3, s.low4, s.low5, s.dyl5, s.dyl4, s.dyl3, s.dyl2)
    ):
        for i in range(8):
            halo_copy(h, framed, i).wait_send()


def step_call(nw, nn, ext, ct, marks, params, first, second):
    X, Y, Z = ext
    XE, YE = X + 2, Y + 2
    CX, CY, CZ = X // 2, Y // 2, Z // 2
    total = nw * nn
    framed = (XE, YE, Z)
    small = (CX + 2, CY + 2, CZ)
    dma = pltpu.SemaphoreType.DMA
    rows = params.shape[0]
    lay = Layout(rows * LANES, total)
    nz, nx, ny, nc = grid_of(nw, nn)
    oy = max(ny - 1, 1)
    half = 16 * (-(-lay.window // 32))
    low = lambda *shape: pltpu.VMEM(shape, BF16)
    scratch = dict(
        weights=low(lay.weight_rows, LANES),
        grads=low(lay.grad_rows, LANES),
        natural=pltpu.VMEM((rows + 112, LANES), F32),
        fix=low(total, lay.fix, LANES),
        quick=low(48, LANES),
        quick_send=dma((2,)),
        quick_recv=dma((2,)),
        onward_send=dma((nz, 2, PIECES)),
        gather_send=dma((PIECES,)),
        gather_recv=dma((total, PIECES)),
        red_c=low(nz, nx, ny, nc - 1, lay.window, LANES),
        red_dx=low(nz, nx, oy, half, LANES),
        red_dy=low(nz, nx, oy, lay.window - half, LANES),
        red_ex=low(nz, nx, lay.window, LANES),
        red_ey=low(nz, oy, lay.window, LANES),
        red_z=low(nz if nz == 4 else 1, nz, lay.window, LANES),
        send_core=dma((nz, nx, ny, nc - 1)),
        recv_core=dma((nz, nx, ny, nc - 1)),
        send_dx=dma((nz, nx, oy)),
        recv_dx=dma((nz, nx, oy)),
        send_dy=dma((nz, nx, oy)),
        recv_dy=dma((nz, nx, oy)),
        send_ex=dma((nz, nx)),
        recv_ex=dma((nz, nx)),
        send_ey=dma((nz, nx, oy)),
        recv_ey=dma((nz, oy)),
        send_z=dma((nz, nx, 2)),
        recv_z=dma((nz, nz, 2)),
        acc=pltpu.VMEM((lay.window + 48, LANES), F32),
        in_slots=pltpu.VMEM((2, total, 32, LANES), F32 if total <= 64 else BF16),
        in_send=dma((2,)),
        in_recv=dma((2,)),
        slots=pltpu.VMEM((N_AR, total, 4, LANES), F32),
        ar_send=dma((N_AR,)),
        ar_recv=dma((N_AR,)),
        side=pltpu.VMEM((total, 8, LANES), F32),
        side_send=dma,
        side_recv=dma,
        halo_send=dma((N_HALO, 8)),
        halo_recv=dma((N_HALO, 8)),
        cts=pltpu.VMEM((9, X * Y, LANES), F32),
        ct_send=dma((8,)),
        ct_recv=dma((8,)),
        pair=pltpu.VMEM((CY * Z, LANES), F32),
        we=pltpu.VMEM((9 * LANES, LANES), BF16),
        wm=pltpu.VMEM((27 * C1, C2), BF16),
        entry=pltpu.VMEM((X + 4, Y + 4, Z, LANES), BF16),
        raw1=pltpu.VMEM(framed + (C1,), F32),
        pad1=pltpu.VMEM(framed + (3 * C1,), BF16),
        raw2=pltpu.VMEM(framed + (C1,), F32),
        low2=pltpu.VMEM(framed + (C1,), BF16),
        pool_in=pltpu.VMEM(small + (C1,), BF16),
        skip=pltpu.VMEM(framed + (C1,), F32),
        mix=pltpu.VMEM(framed + (LANES,), F32),
        attention=pltpu.VMEM(framed + (LANES,), F32),
        pad_mid=pltpu.VMEM(small + (3 * C1,), BF16),
        raw3=pltpu.VMEM(small + (C2,), F32),
        low3=pltpu.VMEM(small + (C2,), BF16),
        tall=pltpu.VMEM((CX + 2, CY + 2, Z, C2), BF16),
        pad_join=pltpu.VMEM(framed + (3 * (C1 + C2),), BF16),
        raw4=pltpu.VMEM(framed + (C1,), F32),
        low4=pltpu.VMEM(framed + (C1,), BF16),
        pad4=pltpu.VMEM(framed + (3 * C1,), BF16),
        raw5=pltpu.VMEM(framed + (C1,), F32),
        low5=pltpu.VMEM(framed + (C1,), BF16),
        dy5=pltpu.VMEM(framed + (C1,), F32),
        dyl5=pltpu.VMEM(framed + (C1,), BF16),
        dpad5=pltpu.VMEM(framed + (3 * C1,), BF16),
        dy4=pltpu.VMEM(framed + (C1,), F32),
        dyl4=pltpu.VMEM(framed + (C1,), BF16),
        dpad4=pltpu.VMEM(framed + (3 * C1,), BF16),
        dy3=pltpu.VMEM(small + (C2,), F32),
        dyl3=pltpu.VMEM(small + (C2,), BF16),
        dpad3=pltpu.VMEM(small + (3 * C2,), BF16),
        dy2=pltpu.VMEM(framed + (C1,), F32),
        dyl2=pltpu.VMEM(framed + (C1,), BF16),
        dpad2=pltpu.VMEM(framed + (3 * C1,), BF16),
        d_skip=pltpu.VMEM((X * Y * Z, C1), F32),
    )
    if total <= 64:
        scratch.update(
            turn2=low(27 * C1, C1), turn4=low(27 * C1, C1 + C2), turn5=low(27 * C1, C1)
        )
    cfg = types.SimpleNamespace(nw=nw, nn=nn, ext=ext, names=tuple(scratch), lay=lay)
    vmem = pl.BlockSpec(memory_space=pltpu.VMEM)
    return pl.pallas_call(
        functools.partial(step_kernel, cfg),
        out_shape=(
            jax.ShapeDtypeStruct((rows, LANES), F32),
            jax.ShapeDtypeStruct((rows, LANES), F32),
            jax.ShapeDtypeStruct((rows, LANES), F32),
            jax.ShapeDtypeStruct((8, LANES), F32),
        ),
        in_specs=[vmem] * 5,
        out_specs=(vmem,) * 4,
        scratch_shapes=list(scratch.values()),
        compiler_params=pltpu.CompilerParams(
            collective_id=0, has_side_effects=True, vmem_limit_bytes=62 * 1024 * 1024
        ),
    )(ct, marks, params, first, second)


def on_device(params, first_moment, second_moment, ct_image, labels, valid_mask):
    ext = ct_image.shape
    ct = ct_image.astype(F32).reshape(-1, ext[2])
    new_params, new_first, new_second, scalars = step_call(
        lax.axis_size("wide"),
        lax.axis_size("narrow"),
        ext,
        ct,
        jnp.stack([labels.reshape(-1), valid_mask.reshape(-1)]),
        params.reshape(-1, LANES),
        first_moment.reshape(-1, LANES),
        second_moment.reshape(-1, LANES),
    )
    return (
        new_params.reshape(-1),
        new_first.reshape(-1),
        new_second.reshape(-1),
        scalars[0, 0],
        scalars[1, 0],
    )


def solution(mesh):
    in_specs = (
        P(("wide", "narrow")),
        P(("wide", "narrow")),
        P(("wide", "narrow")),
        P("wide", "narrow", None),
        P("wide", "narrow", None),
        P("wide", "narrow", None),
    )
    out_specs = (P(("wide", "narrow")), P(("wide", "narrow")), P(("wide", "narrow")), P(), P())
    return jax.shard_map(
        on_device, mesh=mesh, in_specs=in_specs, out_specs=out_specs, check_vma=False
    )
```

```python
import functools
import types

import jax
import jax.numpy as jnp
from jax import lax
from jax.experimental import pallas as pl
from jax.experimental.pallas import tpu as pltpu
from jax.sharding import PartitionSpec as P

C1 = 128
C2 = 256
GATE = 64
CLASSES = 3
STEP = 10

EPS_NORM = 1e-05
BETA_ONE = 0.9
BETA_TWO = 0.999
EPS_ADAM = 1e-06
DECAY_RATE = 0.01
LEARN_RATE = 0.3

F32 = jnp.float32
BF16 = jnp.bfloat16
MESH = pl.DeviceIdType.MESH
LANES = 128
TILE = 16 * LANES

LENGTHS = (
    27 * C1,
    27 * C1 * C1,
    27 * C1 * C2,
    C1 * GATE,
    C2 * GATE,
    GATE,
    27 * (C1 + C2) * C1,
    27 * C1 * C1,
    (C1 + 1) * CLASSES,
    4 * C1 + C2,
    4 * C1 + C2,
)
STARTS = tuple(sum(LENGTHS[:i]) for i in range(len(LENGTHS)))
USED = sum(LENGTHS)

FRONT = 32 * LANES - STARTS[1]
SPLIT = STARTS[6]
ROW_IN = STARTS[0] + FRONT
ROW_IN = ROW_IN // LANES
ROW_ENC = (STARTS[1] + FRONT) // LANES
ROW_MID = (STARTS[2] + FRONT) // LANES
ROW_X = (STARTS[3] + FRONT) // LANES
ROW_G = (STARTS[4] + FRONT) // LANES
ROW_PSI = (STARTS[5] + FRONT) // LANES
ROWS_A = -(-(SPLIT + FRONT) // TILE) * 16
ROW_DEC1 = ROWS_A
ROW_DEC2 = ROW_DEC1 + (STARTS[7] - SPLIT) // LANES
ROW_TAIL = ROW_DEC1 + (STARTS[8] - SPLIT) // LANES

DIRS = tuple((dx, dy) for dx in (-1, 0, 1) for dy in (-1, 0, 1) if (dx, dy) != (0, 0))

N_AR = 11
N_HALO = 9
PIECES = 3


def grid_of(nw, nn):
    nx = max(k for k in range(1, nw + 1) if nw % k == 0 and k * k <= nw)
    ny = max(nn // 2, 1)
    return nw // nx, nx, ny, nn // ny


class Layout:
    def __init__(self, shard_len, total):
        self.rows = shard_len // LANES
        self.total = total
        self.turn = -(-SPLIT // shard_len)
        self.shift_a = FRONT // LANES
        self.shift_b = ROWS_A - SPLIT // LANES - 1
        begin = [self.first(p) for p in range(total + 1)]
        edge = []
        for p in range(1, total + 1):
            low = self.rows * p + (self.shift_b if p >= self.turn else self.shift_a)
            edge.append(low // 16)
        self.body = min(edge[p] - begin[p] for p in range(total))
        self.gap = max(begin[p + 1] - begin[p] - self.body for p in range(total))
        self.begin = begin
        self.half = -(-self.body // 2)
        self.fix = 16 * (1 + self.gap)
        self.window = 16 * (1 + self.body + self.gap)
        self.weight_rows = 16 * begin[total]
        self.grad_rows = max(16 * (begin[p] - 1) for p in range(total)) + self.window
        self.grad_rows = max(self.grad_rows, self.weight_rows)

    def first(self, p):
        late = (p + self.total - self.turn) // self.total
        return (self.rows * p + self.shift_a + 15 + (self.shift_b + 1 - self.shift_a) * late) // 16


def dot(a, b):
    return jnp.dot(a, b, preferred_element_type=F32)


def dot_nt(a, b):
    return lax.dot_general(a, b, (((1,), (1,)), ((), ())), preferred_element_type=F32)


def dot_tn(a, b):
    return lax.dot_general(a, b, (((0,), (0,)), ((), ())), preferred_element_type=F32)


def iota(shape, dim):
    return lax.broadcasted_iota(jnp.int32, shape, dim)


def onehot(cond):
    return jnp.where(cond, 1.0, 0.0).astype(BF16)


def silu_grad(v, s):
    return s * (1.0 + v * (1.0 - s))


def step_kernel(
    cfg,
    ct_ref,
    marks_ref,
    param_ref,
    first_ref,
    second_ref,
    param_out,
    first_out,
    second_out,
    loss_out,
    count_out,
    *scr,
):
    s = types.SimpleNamespace(turn2=None, turn4=None, turn5=None)
    s.__dict__.update(zip(cfg.names, scr))
    w_ref, g_ref = s.weights, s.grads
    lay = cfg.lay
    nw, nn = cfg.nw, cfg.nn
    total = nw * nn
    X, Y, Z = cfg.ext
    XE, YE = X + 2, Y + 2
    CX, CY, CZ = X // 2, Y // 2, Z // 2
    V = X * Y * Z
    VC = CX * CY * CZ
    voxels = float(V * total)
    coarse_voxels = voxels / 8.0
    w = lax.axis_index("wide")
    n = lax.axis_index("narrow")
    me = w * nn + n

    def dev(p):
        return (p // nn, lax.rem(p, nn))

    barrier = pltpu.get_barrier_semaphore()

    def greet(d, carry):
        pl.semaphore_signal(
            barrier, inc=1, device_id=dev(lax.rem(me + d, total)), device_id_type=MESH
        )
        return carry

    lax.fori_loop(1, total, greet, 0)

    nz, nx, ny, nc = grid_of(nw, nn)
    here = (w // nx, lax.rem(w, nx), n // nc, lax.rem(n, nc))
    sizes = (nz, nx, ny, nc)

    def place(r):
        z, x, y, c = [
            h if d == 0 else lax.rem(h + d % k, k) for h, d, k in zip(here, r, sizes)
        ]
        return z * nx + x, y * nc + c

    def number(zp, r):
        a, b = place((0,) + r)
        return (zp * nx + lax.rem(a, nx)) * nn + b

    natural = s.natural
    lead = 32
    natural[0:lead] = jnp.zeros((lead, LANES), F32)
    natural[lead : lead + lay.rows] = param_ref[...]
    rest = natural.shape[0] - lead - lay.rows
    natural[lead + lay.rows :] = jnp.zeros((rest, LANES), F32)
    begin = lay.first(me)
    off_a = lay.rows * me + lay.shift_a - 16 * (begin - 1)
    off_b = off_a + lay.shift_b - lay.shift_a
    lane = iota((1, LANES), 1)
    span = 16 * (1 + lay.body + lay.gap)
    row_at = iota((span, LANES), 0) + 16 * (begin - 1)
    as_a = natural[pl.ds(lead - off_a, span), :]
    late = pltpu.roll(natural[pl.ds(lead - off_b, span), :], LANES // 2, 1)
    early = pltpu.roll(natural[pl.ds(lead - off_b - 1, span), :], LANES // 2, 1)
    as_b = jnp.where(lane < LANES // 2, early, late)
    share = jnp.where(row_at < ROWS_A, as_a, as_b).astype(BF16)
    fix = s.fix
    body = 16 * lay.body

    def at_tile(t):
        return pl.multiple_of(16 * t, 16)

    w_ref[pl.ds(at_tile(begin), body), :] = share[16 : 16 + body]
    fix[me] = jnp.concatenate([share[0:16], share[16 + body : 16 + body + 16 * lay.gap]], 0)

    gather_send, gather_recv = s.gather_send, s.gather_recv
    sent = [0] * PIECES
    every = (0, 1, 2)

    def flat_id(zp, r):
        x, y, c = [d % k for d, k in zip(r, sizes[1:])]
        return ((zp * nx + x) * ny + y) * nc + c

    def piece_ref(p, piece):
        if piece == 2:
            return fix.at[p]
        lo = 0 if piece == 0 else lay.half
        size = lay.half if piece == 0 else lay.body - lay.half
        return w_ref.at[pl.ds(at_tile(lay.first(p) + lo), 16 * size)]

    def gather_copy(zp, r, d, piece):
        ref = piece_ref(number(zp, r), piece)
        there = tuple(a - b for a, b in zip(r, d[1:]))
        return pltpu.make_async_remote_copy(
            ref,
            ref,
            gather_send.at[piece],
            gather_recv.at[flat_id(zp, there), piece],
            device_id=place(d),
            device_id_type=MESH,
        )

    def gather_push(zp, r, dests, pieces):
        for piece in pieces:
            for d in dests:
                gather_copy(zp, r, d, piece).start()

    def gather_take(zp, r, piece):
        gather_copy(zp, r, (0, 0, 0, 0), piece).wait_recv()

    along_x = [(0, k, 0, 0) for k in range(1, nx)]
    along_y = [(0, 0, k, 0) for k in range(1, ny)]
    sibling = [(0, 0, 0, k) for k in range(1, nc)]
    mine_r = (0, 0, 0)
    for piece in every:
        split = [len(along_y), len(along_x), len(along_x) + len(along_y)][piece]
        sent[piece] = nz * (len(along_x) + len(along_y) + len(sibling))
        first_hop = [(nx - 1) * len(along_y), (ny - 1) * len(along_x), (nx - 1) * len(along_y)]
        sent[piece] += nz * (first_hop[piece] + (nx * ny - 1) * len(sibling))

    onward_send = s.onward_send

    def onward_copy(zp, up, piece):
        ref = piece_ref(number(zp, mine_r), piece)
        return pltpu.make_async_remote_copy(
            ref,
            ref,
            onward_send.at[zp, int(up), piece],
            gather_recv.at[flat_id(zp, mine_r), piece],
            device_id=place((1 if up else nz - 1, 0, 0, 0)),
            device_id_type=MESH,
        )

    def onward(zp, up, piece):
        @pl.when(here[0] < nz - 1 if up else here[0] > 0)
        def _():
            onward_copy(zp, up, piece).start()

    def gather_own():
        for piece in every:
            for up in (True, False):
                onward(here[0], up, piece)
            gather_push(here[0], mine_r, along_x + along_y + sibling, (piece,))

    def at_distance(d, step):
        if d == 0:
            step(here[0], None)
            return

        @pl.when(here[0] - d >= 0)
        def _():
            step(here[0] - d, True)

        @pl.when(here[0] + d < nz)
        def _():
            step(here[0] + d, False)

    def gather_one(zp, up):
        for piece in every:
            gather_take(zp, mine_r, piece)
            onward(zp, up, piece)
            gather_push(zp, mine_r, along_x + along_y + sibling, (piece,))

    def gather_two(zp, up):
        for piece in every:
            for kx in range(1, nx):
                gather_take(zp, (kx, 0, 0), piece)
                if piece != 1:
                    gather_push(zp, (kx, 0, 0), along_y, (piece,))
                gather_push(zp, (kx, 0, 0), sibling, (piece,))
            for ky in range(1, ny):
                gather_take(zp, (0, ky, 0), piece)
                if piece == 1:
                    gather_push(zp, (0, ky, 0), along_x, (piece,))
                gather_push(zp, (0, ky, 0), sibling, (piece,))

    def gather_three(zp, up):
        for piece in every:
            for kx in range(1, nx):
                for ky in range(1, ny):
                    gather_take(zp, (kx, ky, 0), piece)
                    gather_push(zp, (kx, ky, 0), sibling, (piece,))

    def gather_four(zp):
        for kx in range(nx):
            for ky in range(ny):
                for kc in range(1, nc):
                    for piece in every:
                        gather_take(zp, (kx, ky, kc), piece)
        low, high = zp * nx * nn, (zp + 1) * nx * nn
        if zp == 0:
            w_ref[16 * (lay.begin[0] - 1) : 16 * lay.begin[0]] = fix[0, 0:16]
        else:
            put_gap(low - 1)
        for p in range(low, high - (zp < nz - 1)):
            put_gap(p)

    def put_gap(p):
        tile = lay.begin[p] + lay.body
        for i in range(lay.begin[p + 1] - tile):
            part = fix[p, 16 * (1 + i) : 16 * (2 + i)]
            if tile + i == lay.begin[p + 1] - 1 and p + 1 < total:
                part = part + fix[p + 1, 0:16]
            w_ref[16 * (tile + i) : 16 * (tile + i + 1)] = part

    quick, quick_send, quick_recv = s.quick, s.quick_send, s.quick_recv
    shard_len = lay.rows * LANES
    quick_parts = []
    for row, size in ((0, 32), (ROW_TAIL, 16)):
        owner = 0 if row == 0 else STARTS[8] // shard_len
        at = row - 16 * (lay.begin[owner] - 1)
        quick_parts.append((owner, at, size))

    def quick_copy(k, p):
        lo, size = (0, 32) if k == 0 else (32, 16)
        ref = quick.at[pl.ds(lo, size)]
        return pltpu.make_async_remote_copy(
            ref,
            ref,
            quick_send.at[k],
            quick_recv.at[k],
            device_id=dev(p),
            device_id_type=MESH,
        )

    for k, (owner, at, size) in enumerate(quick_parts):

        @pl.when(me == owner)
        def _():
            lo = 0 if k == 0 else 32
            quick[lo : lo + size] = share[at : at + size]

    pl.semaphore_wait(barrier, total - 1)
    for k, (owner, at, size) in enumerate(quick_parts):

        @pl.when(me == owner)
        def _():
            def push(d, carry):
                quick_copy(k, lax.rem(me + d, total)).start()
                return carry

            lax.fori_loop(1, total, push, 0)

    def quick_wait():
        for k, (owner, at, size) in enumerate(quick_parts):

            @pl.when(me != owner)
            def _():
                quick_copy(k, me).wait_recv()

    def quick_end():
        for k, (owner, at, size) in enumerate(quick_parts):

            @pl.when(me == owner)
            def _():
                whole = w_ref.at[pl.ds(0, (total - 1) * size)]
                pltpu.make_async_remote_copy(
                    whole,
                    whole,
                    quick_send.at[k],
                    quick_recv.at[k],
                    device_id=(w, n),
                    device_id_type=MESH,
                ).wait_send()

    quarter = nz // 4
    quarters = [range(k * quarter, (k + 1) * quarter) for k in range(4)]

    def gather(step, k):
        if step is gather_four:
            for zp in quarters[k]:
                step(zp)
            return
        for d in quarters[k]:
            at_distance(d, step)

    def step(what, d):
        if quarter == 1:
            gather(what, d)

    gather_own()

    def gather_end():
        for piece, count in enumerate(sent):
            if piece == 2:
                ref = fix
                unit = 1
            else:
                ref = w_ref
                unit = 16 * (lay.half if piece == 0 else lay.body - lay.half)
            most = ref.shape[0] // unit
            while count:
                k = min(count, most)
                whole = ref.at[pl.ds(0, k * unit)]
                pltpu.make_async_remote_copy(
                    whole,
                    whole,
                    gather_send.at[piece],
                    gather_recv.at[0, piece],
                    device_id=(w, n),
                    device_id_type=MESH,
                ).wait_send()
                count -= k

    cc, dx_in, dy_in = s.red_c, s.red_dx, s.red_dy
    ex_in, ey_in, zz_in = s.red_ex, s.red_ey, s.red_z
    win_rows = lay.window
    mid_row = 16 * (-(-win_rows // 32))
    halves = (pl.ds(0, mid_row), pl.ds(mid_row, win_rows - mid_row))
    acc = s.acc
    sent_red = []

    def grad_window(zd, xd, ry, rc):
        y = lax.rem(here[2] + ry, ny) if ry else here[2]
        c = lax.rem(here[3] + rc, nc) if rc else here[3]
        p = (zd * nx + xd) * nn + y * nc + c
        return pl.ds(at_tile(lay.first(p) - 1), win_rows)

    def red_copy(step, at_send, at_recv, source, target, to):
        return pltpu.make_async_remote_copy(
            source,
            target,
            step[0].at[at_send],
            step[1].at[at_recv],
            device_id=to,
            device_id_type=MESH,
        )

    def in_place(zd, xd):
        return here[1] == xd

    def off_place(zd, xd):
        return here[1] != xd

    def red_go(cond, copy):
        if cond is None:
            copy.start()
        else:

            @pl.when(cond)
            def _():
                copy.start()

        sent_red.append((cond, copy))

    def others(size):
        return range(1, size)

    def copy_core(zd, xd, ry, k):
        return red_copy(
            (s.send_core, s.recv_core),
            (zd, xd, ry, k - 1),
            (zd, xd, ry, k - 1),
            g_ref.at[grad_window(zd, xd, ry, k)],
            cc.at[zd, xd, ry, k - 1],
            place((0, 0, 0, k)),
        )

    def copy_dx(zd, xd, ry, xs):
        return red_copy(
            (s.send_dx, s.recv_dx),
            (zd, xd, ry - 1),
            (zd, xs, ry - 1),
            cc.at[zd, xd, ry, 0, halves[0]],
            dx_in.at[zd, xs, ry - 1],
            (here[0] * nx + xd, n),
        )

    def copy_dy(zd, xd, ry):
        return red_copy(
            (s.send_dy, s.recv_dy),
            (zd, xd, ry - 1),
            (zd, xd, ny - ry - 1),
            cc.at[zd, xd, ry, 0, halves[1]],
            dy_in.at[zd, xd, ny - ry - 1],
            place((0, 0, ry, 0)),
        )

    def copy_ex(zd, xd, xs):
        return red_copy(
            (s.send_ex, s.recv_ex), (zd, xd), (zd, xs), cc.at[zd, xd, 0, 0], ex_in.at[zd, xs], (here[0] * nx + xd, n)
        )

    def copy_ey(zd, xd, ry):
        return red_copy(
            (s.send_ey, s.recv_ey),
            (zd, xd, ry - 1),
            (zd, ny - ry - 1),
            cc.at[zd, xd, ry, 0],
            ey_in.at[zd, ny - ry - 1],
            place((0, 0, ry, 0)),
        )

    def way_along_z(zd):
        if nz != 4:
            return [], [zs for zs in range(nz) if zs != zd], None, None
        lead = 2 if zd < 2 else 1
        far = 3 if zd < 2 else 0
        near = zd + 1 - 2 * (zd % 2)
        return [(far, lead)], [near, lead], far, lead

    def copy_z(zd, xd, zs, to, h):
        return red_copy(
            (s.send_z, s.recv_z),
            (zd, xd, h),
            (zd, zs, h),
            cc.at[zd, xd, 0, 0, halves[h]],
            zz_in.at[zd if nz == 4 else 0, zs, halves[h]],
            (to * nx + xd, n),
        )

    def red_one(units):
        for zd, xd in units:
            for ry in range(ny):
                for k in others(nc):
                    red_go(None, copy_core(zd, xd, ry, k))

    def red_two(units):
        for zd, xd in units:
            for ry in reversed(range(ny)):
                part = g_ref[grad_window(zd, xd, ry, 0), :]
                for k in others(nc):
                    copy_core(zd, xd, ry, k).wait_recv()
                    part = part + cc[zd, xd, ry, k - 1]
                cc[zd, xd, ry, 0] = part
                if ry:
                    red_go(off_place(zd, xd), copy_dx(zd, xd, ry, here[1]))
                    red_go(off_place(zd, xd), copy_dy(zd, xd, ry))

    def red_three(units):
        for zd, xd in units:

            @pl.when(in_place(zd, xd))
            def _():
                for ry in others(ny):
                    part = cc[zd, xd, ry, 0, halves[0]]
                    for xs in range(nx):
                        if xs != xd:
                            copy_dx(zd, xd, ry, xs).wait_recv()
                            part = part + dx_in[zd, xs, ry - 1]
                    cc[zd, xd, ry, 0, halves[0]] = part
                    copy_ey(zd, xd, ry).start()

            @pl.when(off_place(zd, xd))
            def _():
                part = cc[zd, xd, 0, 0, halves[1]]
                for sy in others(ny):
                    copy_dy(zd, xd, ny - sy).wait_recv()
                    part = part + dy_in[zd, xd, sy - 1]
                cc[zd, xd, 0, 0, halves[1]] = part
                copy_ex(zd, xd, here[1]).start()

            for ry in others(ny):
                sent_red.append((in_place(zd, xd), copy_ey(zd, xd, ry)))
            sent_red.append((off_place(zd, xd), copy_ex(zd, xd, here[1])))

    def red_four(units):
        for zd, xd in units:

            @pl.when(in_place(zd, xd))
            def _():
                part = cc[zd, xd, 0, 0].astype(F32)
                for xs in range(nx):
                    if xs != xd:
                        copy_ex(zd, xd, xs).wait_recv()
                        part = part + ex_in[zd, xs].astype(F32)
                for sy in others(ny):
                    copy_ey(zd, xd, ny - sy).wait_recv()
                    part = part + ey_in[zd, sy - 1].astype(F32)
                cc[zd, xd, 0, 0] = part.astype(BF16)
                hops, ends, far, lead = way_along_z(zd)
                for h in range(2):
                    for zs in range(nz):
                        if zs in (zd, lead):
                            continue

                        @pl.when(here[0] == zs)
                        def _():
                            copy_z(zd, xd, zs, lead if zs == far else zd, h).start()

            hops, ends, far, lead = way_along_z(zd)
            for zs in range(nz):
                if zs != zd:
                    for h in range(2):
                        to = lead if zs == far else zd
                        sent_red.append(
                            (in_place(zd, xd) & (here[0] == zs), copy_z(zd, xd, zs, to, h))
                        )

    def red_between(units):
        for zd, xd in units:
            hops, ends, far, lead = way_along_z(zd)
            if not hops:
                continue

            @pl.when(in_place(zd, xd) & (here[0] == lead))
            def _():
                for h in range(2):
                    copy_z(zd, xd, far, lead, h).wait_recv()
                    part = cc[zd, xd, 0, 0, halves[h]]
                    cc[zd, xd, 0, 0, halves[h]] = part + zz_in[zd, far, halves[h]]
                    copy_z(zd, xd, lead, zd, h).start()

    def red_five(units):
        for zd, xd in units:

            @pl.when(in_place(zd, xd) & (here[0] == zd))
            def _():
                part = cc[zd, xd, 0, 0].astype(F32)
                hops, ends, far, lead = way_along_z(zd)
                for zs in ends:
                    for h in range(2):
                        copy_z(zd, xd, zs, zd, h).wait_recv()
                    part = part + zz_in[zd if nz == 4 else 0, zs].astype(F32)
                acc[16 : 16 + win_rows] = part

    def red_finish():
        for cond, copy in sent_red:
            if cond is None:
                copy.wait_send()
            else:

                @pl.when(cond)
                def _():
                    copy.wait_send()

    slots, ar_send, ar_recv = s.slots, s.ar_send, s.ar_recv

    def to_all(copy):
        if total > 64:

            def push(d, carry):
                copy(dev(lax.rem(me + d, total))).start()
                return carry

            lax.fori_loop(1, total, push, 0)
            return
        upper = (2 * here[0]) // nz
        for i in range(nz):
            zp = (1 - upper) * (nz - 1 - i) + upper * i
            for rx in reversed(range(nx)):
                for ry in reversed(range(ny)):
                    for rc in reversed(range(nc)):
                        a, b = place((0, rx, ry, rc))
                        target = (zp * nx + lax.rem(a, nx), b)
                        if rx or ry or rc:
                            copy(target).start()
                        else:

                            @pl.when(zp != here[0])
                            def _():
                                copy(target).start()

    def ar_start(r, rows):
        rows = list(rows) + [jnp.zeros((1, LANES), F32)] * (4 - len(rows))
        slots[r, me] = jnp.concatenate(rows, 0)

        def copy(target):
            return pltpu.make_async_remote_copy(
                slots.at[r, me],
                slots.at[r, me],
                ar_send.at[r],
                ar_recv.at[r],
                device_id=target,
                device_id_type=MESH,
            )

        to_all(copy)

    def ar_whole(r):
        others = slots.at[r, pl.ds(0, total - 1)]
        return pltpu.make_async_remote_copy(
            others, others, ar_send.at[r], ar_recv.at[r], device_id=(w, n), device_id_type=MESH
        )

    def ar_wait(r):
        ar_whole(r).wait_recv()
        return jnp.sum(slots[r], axis=0)

    side, side_send, side_recv = s.side, s.side_send, s.side_recv

    def side_start(rows):
        rows = list(rows) + [jnp.zeros((1, LANES), F32)] * (8 - len(rows))
        side[me] = jnp.concatenate(rows, 0)

        def copy(target):
            return pltpu.make_async_remote_copy(
                side.at[me],
                side.at[me],
                side_send,
                side_recv,
                device_id=target,
                device_id_type=MESH,
            )

        to_all(copy)

    def side_whole():
        others = side.at[pl.ds(0, total - 1)]
        return pltpu.make_async_remote_copy(
            others, others, side_send, side_recv, device_id=(w, n), device_id_type=MESH
        )

    halo_send, halo_recv = s.halo_send, s.halo_recv

    def halo_copy(h, ref, i):
        dx, dy = DIRS[i]
        ex, ey = ref.shape[0] - 2, ref.shape[1] - 2

        def source(d, size):
            return pl.ds(1, size) if d == 0 else pl.ds(size if d > 0 else 1, 1)

        def target(d, size):
            return pl.ds(1, size) if d == 0 else pl.ds(0 if d > 0 else size + 1, 1)

        return pltpu.make_async_remote_copy(
            ref.at[source(dx, ex), source(dy, ey)],
            ref.at[target(dx, ex), target(dy, ey)],
            halo_send.at[h, i],
            halo_recv.at[h, i],
            device_id=(lax.rem(w + dx + nw, nw), lax.rem(n + dy + nn, nn)),
            device_id_type=MESH,
        )

    def halo_start(h, ref):
        for i in range(8):
            halo_copy(h, ref, i).start()

    def halo_wait(h, ref):
        for i in range(8):
            halo_copy(h, ref, i).wait_recv()

    def clear_edges(ref, depth):
        ex, ey = ref.shape[0], ref.shape[1]

        @pl.when(w == 0)
        def _():
            ref[0:depth] = jnp.zeros((depth,) + ref.shape[1:], ref.dtype)

        @pl.when(w == nw - 1)
        def _():
            ref[ex - depth : ex] = jnp.zeros((depth,) + ref.shape[1:], ref.dtype)

        @pl.when(n == 0)
        def _():
            ref[:, 0:depth] = jnp.zeros((ex, depth) + ref.shape[2:], ref.dtype)

        @pl.when(n == nn - 1)
        def _():
            ref[:, ey - depth : ey] = jnp.zeros((ex, depth) + ref.shape[2:], ref.dtype)

    def z_three(flat, length):
        rows = flat.shape[0]
        at = jnp.bitwise_and(iota(flat.shape, 0), length - 1)
        before = jnp.where(at == 0, 0.0, pltpu.roll(flat, 1, 0))
        after = jnp.where(at == length - 1, 0.0, pltpu.roll(flat, rows - 1, 0))
        return before.astype(BF16), flat.astype(BF16), after.astype(BF16)

    def put_three(ref, flat, base, stride):
        shape = ref.shape[:3] + (LANES,)
        for c, part in enumerate(z_three(flat, ref.shape[2])):
            lo = c * stride + base
            ref[:, :, :, lo : lo + LANES] = part.reshape(shape)

    def merge_frame(full, low):
        ex, ey = full.shape[0], full.shape[1]
        full[0] = low[0].astype(F32)
        full[ex - 1] = low[ex - 1].astype(F32)
        full[1 : ex - 1, 0] = low[1 : ex - 1, 0].astype(F32)
        full[1 : ex - 1, ey - 1] = low[1 : ex - 1, ey - 1].astype(F32)

    def conv(ref, weight, row0, ext):
        x, y = ext
        rows = x * y * ref.shape[2]
        depth = ref.shape[3]
        acc = None
        for ab in range(9):
            a, b = ab // 3, ab % 3
            window = ref[a : a + x, b : b + y].reshape(rows, depth)
            part = dot(window, weight[row0 + ab * depth : row0 + (ab + 1) * depth, :])
            acc = part if acc is None else acc + part
        return acc

    def conv_back(ref, weight, row0, cin, cout, ext):
        x, y = ext
        rows = x * y * ref.shape[2]
        acc = None
        for ab in range(9):
            a, b = ab // 3, ab % 3
            for c in range(3):
                window = ref[a : a + x, b : b + y, :, c * cout : (c + 1) * cout]
                tap = 26 - (3 * ab + c)
                part = dot_nt(
                    window.reshape(rows, cout),
                    weight[row0 + tap * cin : row0 + (tap + 1) * cin, :],
                )
                acc = part if acc is None else acc + part
        return acc

    def turn(turned, row0, cin):
        if turned is None:
            return
        for tap in range(27):
            block = w_ref[row0 + (26 - tap) * cin : row0 + (27 - tap) * cin, :]
            turned[tap * C1 : (tap + 1) * C1, :] = block.T

    def conv_in(ref, turned, row0, cin):
        if turned is None:
            return conv_back(ref, w_ref, row0, cin, C1, (X, Y))
        return conv(ref, turned, 0, (X, Y))

    def conv_grad(ref, low, row0, ext):
        x, y = ext
        rows = x * y * ref.shape[2]
        depth = ref.shape[3]
        for ab in range(9):
            a, b = ab // 3, ab % 3
            window = ref[a : a + x, b : b + y].reshape(rows, depth)
            g_ref[row0 + ab * depth : row0 + (ab + 1) * depth, :] = dot_tn(window, low).astype(BF16)

    def col_sum(v):
        return jnp.sum(v, axis=0, keepdims=True)

    def own(ref):
        return ref[1 : ref.shape[0] - 1, 1 : ref.shape[1] - 1]

    def flat(v):
        return v.reshape(-1, v.shape[-1])

    pair = s.pair

    def pool(v):
        v = v.reshape(X, Y, Z, LANES)
        v = v[0] + v[1]
        v = v.reshape(CY, 2, Z, LANES)
        v = v[:, 0] + v[:, 1]
        pair[0 : CY * Z] = v.reshape(CY * Z, LANES)
        return pair[pl.ds(0, VC, stride=2), :] + pair[pl.ds(1, VC, stride=2), :]

    def spread(v):
        pair[pl.ds(0, VC, stride=2), :] = v
        pair[pl.ds(1, VC, stride=2), :] = v
        u = pair[0 : CY * Z].reshape(CY, 1, Z, LANES)
        u = jnp.broadcast_to(u, (CY, 2, Z, LANES)).reshape(1, Y, Z, LANES)
        return jnp.broadcast_to(u, (X, Y, Z, LANES)).reshape(V, LANES)

    def stats(total_rows, count):
        half = total_rows.shape[0] // 2
        parts = [total_rows[i : i + 1] for i in range(2 * half)]
        mean = jnp.concatenate(parts[:half], 1) / count
        spread_v = jnp.concatenate(parts[half:], 1) / count - mean * mean
        return mean, lax.rsqrt(spread_v + EPS_NORM)

    def ready(zd, xd):
        p = (zd * nx + xd) * nn
        low = 16 * (lay.begin[p] - 1)
        return 3 if low < ROW_MID else 2 if low < ROW_PSI else 1 if low < ROW_DEC2 else 0

    units = [(zd, xd) for zd in range(nz) for xd in range(nx)]
    units_a, units_b, units_c, units_d = [
        [u for u in units if ready(*u) == k] for k in range(4)
    ]
    g_ref[0:32] = jnp.zeros((32, LANES), BF16)
    g_ref[ROW_PSI:ROWS_A] = jnp.zeros((ROWS_A - ROW_PSI, LANES), BF16)
    g_ref[ROW_TAIL:] = jnp.zeros((g_ref.shape[0] - ROW_TAIL, LANES), BF16)

    in_slots, in_send, in_recv = s.in_slots, s.in_send, s.in_recv

    def entry_grad(low):
        rows = [jnp.zeros((ROW_IN, LANES), F32)]
        for ab in range(9):
            a, b = ab // 3, ab % 3
            patch = entry[a + 1 : a + 1 + X, b + 1 : b + 1 + Y].reshape(V, LANES)
            block = dot_tn(patch, low)
            for c in range(3):
                rows.append(col_sum(block[c * Z : (c + 1) * Z]))
        return jnp.concatenate(rows, 0)

    def in_copy(k):
        return pltpu.make_async_remote_copy(
            in_slots.at[k, me],
            in_slots.at[k, me],
            in_send.at[k],
            in_recv.at[k],
            device_id=(0, 0),
            device_id_type=MESH,
        )

    def in_whole(k):
        others_in = in_slots.at[k, pl.ds(0, total - 1)]
        return pltpu.make_async_remote_copy(
            others_in, others_in, in_send.at[k], in_recv.at[k], device_id=(w, n), device_id_type=MESH
        )

    tap_at = iota((32, LANES), 0) == iota((32, LANES), 1) + ROW_IN

    def in_put(k, block):
        in_slots[k, me] = block.astype(in_slots.dtype)

        @pl.when(me != 0)
        def _():
            in_copy(k).start()

    cts, ct_send, ct_recv = s.cts, s.ct_send, s.ct_recv
    ct_rows = [ct_ref[...]] * 3 + [jnp.zeros((X * Y, LANES - 3 * Z), F32)]
    cts[4] = jnp.concatenate(ct_rows, 1)

    def ct_copy(i):
        dx, dy = DIRS[i]
        return pltpu.make_async_remote_copy(
            cts.at[4],
            cts.at[3 * (1 - dx) + 1 - dy],
            ct_send.at[i],
            ct_recv.at[i],
            device_id=(lax.rem(w + dx + nw, nw), lax.rem(n + dy + nn, nn)),
            device_id_type=MESH,
        )

    for i in range(8):
        ct_copy(i).start()

    step(gather_one, 1)

    quick_wait()
    tail = quick[32:48, :].astype(F32)
    used_rows = CLASSES * (C1 + 1) // LANES
    used_lanes = CLASSES * (C1 + 1) % LANES
    rolled = pltpu.roll(tail, LANES - used_lanes, 1)
    lane_id = iota((1, LANES), 1)

    def tail_row(q):
        r = used_rows + q
        return jnp.where(
            lane_id < LANES - used_lanes, rolled[r : r + 1], rolled[r + 1 : r + 2]
        )

    gains = [tail_row(q) for q in range(6)]
    shifts = [tail_row(6 + q) for q in range(6)]
    gain = [gains[0], gains[1], jnp.concatenate(gains[2:4], 1), gains[4], gains[5]]
    shift = [shifts[0], shifts[1], jnp.concatenate(shifts[2:4], 1), shifts[4], shifts[5]]

    def select_head(j, r):
        return onehot(
            LANES * r + iota((LANES, LANES), 0) == CLASSES * iota((LANES, LANES), 1) + j
        )

    tail_low = tail.astype(BF16)
    head_rows = []
    for j in range(CLASSES):
        row = None
        for r in range(CLASSES):
            part = dot(tail_low, select_head(j, r))[r : r + 1]
            row = part if row is None else row + part
        head_rows.append(row)
    head_t = jnp.concatenate(head_rows + [jnp.zeros((8 - CLASSES, LANES), F32)], 0).astype(BF16)
    bias_row = tail[used_rows : used_rows + 1]
    bias_col = jnp.sum(
        jnp.where(iota((8, LANES), 0) == iota((8, LANES), 1), bias_row, 0.0), axis=1, keepdims=True
    )
    bias_col = jnp.where(iota((8, 1), 0) < CLASSES, bias_col, 0.0)

    def pick_half(h, rows):
        return onehot(iota((2 * rows, rows), 0) == 2 * iota((2 * rows, rows), 1) + h)

    def widen(block, rows):
        block = block.astype(F32)
        lower = jnp.where(lane_id < GATE, block, 0.0).astype(BF16)
        upper = jnp.where(lane_id < GATE, pltpu.roll(block, GATE, 1), 0.0).astype(BF16)
        both = dot(pick_half(0, rows), lower) + dot(pick_half(1, rows), upper)
        return both.astype(BF16)

    def narrow_back(block, rows):
        low = block.astype(BF16)
        lower = dot_tn(pick_half(0, rows), low)
        upper = dot_tn(pick_half(1, rows), low)
        return (lower + pltpu.roll(upper, GATE, 1)).astype(BF16)

    front = quick[0:32, :].astype(F32)
    step(gather_two, 0)
    step(gather_one, 2)
    we = s.we
    for ab in range(9):
        taps = [
            jnp.broadcast_to(front[ROW_IN + 3 * ab + c : ROW_IN + 3 * ab + c + 1], (Z, LANES))
            for c in range(3)
        ]
        taps.append(jnp.zeros((LANES - 3 * Z, LANES), F32))
        we[ab * LANES : (ab + 1) * LANES] = jnp.concatenate(taps, 0).astype(BF16)

    shuffle = onehot(
        iota((C2, C2), 1)
        == jnp.bitwise_and(iota((C2, C2), 0), 1) * C1 + lax.shift_right_logical(iota((C2, C2), 0), 1)
    )
    valid = marks_ref[1:2].astype(F32)
    count_row = jnp.broadcast_to(jnp.sum(valid, axis=1, keepdims=True), (1, LANES))

    for i in range(8):
        ct_copy(i).wait_recv()

    entry = s.entry
    zz, ll = iota((Z, LANES), 0), iota((Z, LANES), 1)
    band = jnp.where((jnp.bitwise_and(ll, Z - 1) == zz + ll // Z - 1) & (ll < 3 * Z), 1.0, 0.0)
    for ex in range(X + 4):
        bx = (ex - 2 + X) // X
        lx = ex - 2 - (bx - 1) * X
        for ey in range(Y + 4):
            by = (ey - 2 + Y) // Y
            ly = ey - 2 - (by - 1) * Y
            row = cts[3 * bx + by, lx * Y + ly : lx * Y + ly + 1]
            entry[ex, ey] = (jnp.broadcast_to(row, (Z, LANES)) * band).astype(BF16)
    clear_edges(entry, 2)
    step(gather_two, 1)
    step(gather_three, 0)
    step(gather_one, 3)
    raw1 = s.raw1
    raw1[...] = conv(entry, we, 0, (XE, YE)).reshape(XE, YE, Z, LANES)
    mine = flat(own(raw1))
    ar_start(0, [col_sum(mine), col_sum(mine * mine), count_row])
    if quarter == 1:
        step(gather_two, 2)
        step(gather_three, 1)
    else:
        for d in range(1, nz):
            at_distance(d, gather_one)
        for k in range(3):
            gather(gather_two, k)
        for k in range(2):
            gather(gather_three, k)
    sums = ar_wait(0)
    valid_count = sums[2:3, 0:1]
    mean1, inv1 = stats(sums[0:2], voxels)
    v = (flat(raw1[...]) - mean1) * inv1 * gain[0] + shift[0]
    pad1 = s.pad1
    put_three(pad1, v * jax.nn.sigmoid(v), 0, C1)
    clear_edges(pad1, 1)

    gather(gather_two, 3)
    gather(gather_three, 2)
    gather(gather_three, 3)
    gather(gather_four, 0)
    raw2, low2 = s.raw2, s.low2
    mine = conv(pad1, w_ref, ROW_ENC, (X, Y))
    raw2[1 : XE - 1, 1 : YE - 1] = mine.reshape(X, Y, Z, C1)
    low2[1 : XE - 1, 1 : YE - 1] = mine.astype(BF16).reshape(X, Y, Z, C1)
    ar_start(1, [col_sum(mine), col_sum(mine * mine)])
    halo_start(0, low2)
    turn(s.turn2, ROW_ENC, C1)
    sums = ar_wait(1)
    mean2, inv2 = stats(sums[0:2], voxels)
    v = (mine - mean2) * inv2 * gain[1] + shift[1]
    skip_own = v * jax.nn.sigmoid(v)

    gather(gather_four, 1)
    pool_in = s.pool_in
    pool_in[1 : CX + 1, 1 : CY + 1] = (pool(skip_own) * 0.125).astype(BF16).reshape(CX, CY, CZ, C1)
    halo_start(1, pool_in)
    wm = s.wm
    for tap in range(27):
        part = dot_tn(shuffle, w_ref[ROW_MID + C2 * tap : ROW_MID + C2 * (tap + 1), :]).astype(BF16)
        wm[tap * C1 : (tap + 1) * C1, 0:LANES] = part[0:LANES]
        wm[tap * C1 : (tap + 1) * C1, LANES:C2] = part[LANES:C2]

    psi = w_ref[ROW_PSI : ROW_PSI + 16, :].astype(F32)[0:1]
    psi = jnp.where(lane_id < GATE, psi, 0.0)
    w_x = widen(w_ref[ROW_X : ROW_X + C1 // 2, :], C1 // 2)
    w_g = widen(w_ref[ROW_G : ROW_G + C2 // 2, :], C2 // 2)
    halo_wait(0, low2)
    merge_frame(raw2, low2)
    v = (flat(raw2[...]) - mean2) * inv2 * gain[1] + shift[1]
    skip = s.skip
    skip_all = v * jax.nn.sigmoid(v)
    skip[...] = skip_all.reshape(XE, YE, Z, C1)
    mix = s.mix
    mix[...] = dot(skip_all.astype(BF16), w_x).reshape(XE, YE, Z, LANES)
    halo_wait(1, pool_in)
    clear_edges(pool_in, 1)
    pad_mid = s.pad_mid
    put_three(pad_mid, flat(pool_in[...].astype(F32)), 0, C1)
    raw3, low3 = s.raw3, s.low3
    mine = conv(pad_mid, wm, 0, (CX, CY))
    raw3[1 : CX + 1, 1 : CY + 1] = mine.reshape(CX, CY, CZ, C2)
    low3[1 : CX + 1, 1 : CY + 1] = mine.astype(BF16).reshape(CX, CY, CZ, C2)
    sum_v, square_v = col_sum(mine), col_sum(mine * mine)
    ar_start(
        2, [sum_v[:, 0:C1], sum_v[:, C1:C2], square_v[:, 0:C1], square_v[:, C1:C2]]
    )
    halo_start(2, low3)
    in_put(
        0,
        entry_grad(((flat(own(raw1)) - mean1) * inv1).astype(BF16))
        + jnp.where(
            iota((32, LANES), 0) == 0,
            col_sum(jnp.where(tap_at, entry_grad(jnp.ones((V, LANES), BF16)), 0.0)),
            0.0,
        ),
    )
    sums = ar_wait(2)
    mean3, inv3 = stats(sums, coarse_voxels)
    halo_wait(2, low3)
    merge_frame(raw3, low3)
    v = (flat(raw3[...]) - mean3) * inv3 * gain[2] + shift[2]
    coarse = (v * jax.nn.sigmoid(v)).astype(BF16).reshape(CX + 2, CY + 2, CZ, C2)
    coarse_own = flat(coarse[1 : CX + 1, 1 : CY + 1])
    frame = (CY + 2) * CZ
    doubled = onehot(
        iota((2 * frame, frame), 1) == lax.shift_right_logical(iota((2 * frame, frame), 0), 1)
    )
    tall = s.tall
    for cx in range(CX + 2):
        tall[cx] = (
            dot(doubled, coarse[cx].reshape(frame, C2)).astype(BF16).reshape(CY + 2, Z, C2)
        )

    def expand(u):
        u = jnp.concatenate([u[(i + 1) // 2 : (i + 1) // 2 + 1] for i in range(XE)], 0)
        return jnp.concatenate([u[:, (j + 1) // 2 : (j + 1) // 2 + 1] for j in range(YE)], 1)

    gate_c = dot(flat(tall[...]), w_g).reshape(CX + 2, CY + 2, Z, LANES)
    mixed_in = flat(mix[...] + expand(gate_c))
    mix[...] = mixed_in.reshape(XE, YE, Z, LANES)
    mixed = mixed_in * jax.nn.sigmoid(mixed_in)
    att = jax.nn.sigmoid(jnp.sum(mixed * psi, axis=1, keepdims=True))
    attention = s.attention
    attention[...] = jnp.broadcast_to(att, (XE * YE * Z, LANES)).reshape(XE, YE, Z, LANES)
    pad_join = s.pad_join
    put_three(pad_join, flat(skip[...] * attention[...]), 0, C1 + C2)
    for half in range(2):
        piece = flat(tall[:, :, :, half * C1 : (half + 1) * C1].astype(F32))
        for c, part in enumerate(z_three(piece, Z)):
            lo = c * (C1 + C2) + C1 + half * C1
            pad_join[:, :, :, lo : lo + C1] = expand(part.reshape(CX + 2, CY + 2, Z, C1))
    clear_edges(pad_join, 1)

    gather(gather_four, 2)
    gather(gather_four, 3)
    raw4, low4 = s.raw4, s.low4
    mine = conv(pad_join, w_ref, ROW_DEC1, (X, Y))
    raw4[1 : XE - 1, 1 : YE - 1] = mine.reshape(X, Y, Z, C1)
    low4[1 : XE - 1, 1 : YE - 1] = mine.astype(BF16).reshape(X, Y, Z, C1)
    ar_start(3, [col_sum(mine), col_sum(mine * mine)])
    halo_start(3, low4)
    turn(s.turn5, ROW_DEC2, C1)
    sums = ar_wait(3)
    mean4, inv4 = stats(sums[0:2], voxels)
    halo_wait(3, low4)
    merge_frame(raw4, low4)
    v = (flat(raw4[...]) - mean4) * inv4 * gain[3] + shift[3]
    pad4 = s.pad4
    put_three(pad4, v * jax.nn.sigmoid(v), 0, C1)
    clear_edges(pad4, 1)

    raw5, low5 = s.raw5, s.low5
    mine = conv(pad4, w_ref, ROW_DEC2, (X, Y))
    raw5[1 : XE - 1, 1 : YE - 1] = mine.reshape(X, Y, Z, C1)
    low5[1 : XE - 1, 1 : YE - 1] = mine.astype(BF16).reshape(X, Y, Z, C1)
    ar_start(4, [col_sum(mine), col_sum(mine * mine)])
    halo_start(4, low5)
    turn(s.turn4, ROW_DEC1, C1 + C2)
    sums = ar_wait(4)
    mean5, inv5 = stats(sums[0:2], voxels)
    hat = (mine - mean5) * inv5
    v = hat * gain[4] + shift[4]
    sg = jax.nn.sigmoid(v)
    act = (v * sg).astype(BF16)

    logits = dot_nt(head_t, act) + bias_col
    real = iota((8, V), 0) < CLASSES
    logits = jnp.where(real, logits, -1e30)
    hot = iota((8, V), 0) == marks_ref[0:1]
    top = jnp.max(logits, axis=0, keepdims=True)
    log_total = top + jnp.log(jnp.sum(jnp.exp(logits - top), axis=0, keepdims=True))
    picked = jnp.sum(jnp.where(hot, logits, 0.0), axis=0, keepdims=True)
    loss = jnp.sum(valid * (log_total - picked), axis=1, keepdims=True)
    probs = jnp.exp(logits - log_total)
    g_logits = valid * (probs - jnp.where(hot, 1.0, 0.0)) / valid_count
    g_low = g_logits.astype(BF16)
    head_grad = dot(g_low, act)
    bias_grad = jnp.sum(g_low.astype(F32), axis=1, keepdims=True)
    bias_line = jnp.sum(
        jnp.where(iota((8, LANES), 0) == iota((8, LANES), 1), bias_grad, 0.0), axis=0, keepdims=True
    )
    dy = dot_tn(g_low, head_t) * silu_grad(v, sg)

    def norm_back(r, h, dy, hat, raw, mean, inv, gain_v, ext, count, names2, extra):
        dyf, dyl = names2
        ex, ey = ext[0] + 2, ext[1] + 2
        width = dy.shape[1]
        shaped = dy.reshape(ext + (width,))
        dyf[1 : ex - 1, 1 : ey - 1] = shaped
        dyl[1 : ex - 1, 1 : ey - 1] = shaped.astype(BF16)
        first, second = col_sum(dy), col_sum(dy * hat)
        rows = [first[:, i : i + LANES] for i in range(0, width, LANES)]
        rows += [second[:, i : i + LANES] for i in range(0, width, LANES)]
        ar_start(r, rows + extra)
        halo_start(h, dyl)
        return rows

    def norm_back_end(r, h, raw, mean, inv, gain_v, count, names2):
        dyf, dyl = names2
        sums = ar_wait(r)
        halo_wait(h, dyl)
        merge_frame(dyf, dyl)
        width = dyf.shape[3]
        k = width // LANES
        one = jnp.concatenate([sums[i : i + 1] for i in range(k)], 1)
        two = jnp.concatenate([sums[k + i : k + i + 1] for i in range(k)], 1)
        hat_all = (flat(raw[...]) - mean) * inv
        back = inv * gain_v * (flat(dyf[...]) - one / count - hat_all * (two / count))
        return sums, back

    grad_shift, grad_gain = {}, {}
    fine = (X, Y, Z)
    norm_back(5, 5, dy, hat, raw5, mean5, inv5, gain[4], fine, voxels, (s.dy5, s.dyl5),
              [jnp.broadcast_to(loss, (1, LANES))])
    halo_wait(4, low5)
    merge_frame(raw5, low5)
    sums, back = norm_back_end(5, 5, raw5, mean5, inv5, gain[4], voxels, (s.dy5, s.dyl5))
    grad_shift[4], grad_gain[4] = [sums[0:1]], [sums[1:2]]
    loss_row = sums[2:3]
    dpad = s.dpad5
    put_three(dpad, back, 0, C1)
    clear_edges(dpad, 1)
    grad_act = conv_in(dpad, s.turn5, ROW_DEC2, C1)
    hat = (flat(own(raw4)) - mean4) * inv4
    v = hat * gain[3] + shift[3]
    dy = grad_act * silu_grad(v, jax.nn.sigmoid(v))
    norm_back(6, 6, dy, hat, raw4, mean4, inv4, gain[3], fine, voxels, (s.dy4, s.dyl4), [])
    conv_grad(pad4, flat(own(dpad)[:, :, :, C1 : 2 * C1]), ROW_DEC2, (X, Y))
    red_one(units_a)
    red_two(units_a)
    sums, back = norm_back_end(6, 6, raw4, mean4, inv4, gain[3], voxels, (s.dy4, s.dyl4))
    grad_shift[3], grad_gain[3] = [sums[0:1]], [sums[1:2]]
    dpad = s.dpad4
    put_three(dpad, back, 0, C1)
    clear_edges(dpad, 1)
    low_raw4 = flat(own(dpad)[:, :, :, C1 : 2 * C1])
    grad_join = conv_in(dpad, s.turn4, ROW_DEC1, C1 + C2)

    grad_gated = grad_join[:, 0:C1]
    skip_own = flat(own(skip))
    att_own = flat(own(attention))
    mixed_own = flat(own(mix))
    sg = jax.nn.sigmoid(mixed_own)
    d_att = jnp.sum(grad_gated * skip_own, axis=1, keepdims=True)
    d_logit = d_att * att_own * (1.0 - att_own)
    psi_grad = col_sum(mixed_own * sg * d_logit)
    d_mixed = d_logit * psi * silu_grad(mixed_own, sg)
    low_fine = d_mixed.astype(BF16)
    low_gc = pool(d_mixed).astype(BF16)
    d_coarse = [
        pool(grad_join[:, C1 : 2 * C1]),
        pool(grad_join[:, 2 * C1 : 3 * C1]),
    ]
    d_coarse = jnp.concatenate(d_coarse, 1) + dot_nt(low_gc, w_g)
    d_coarse = d_coarse.astype(BF16).astype(F32)
    hat = (flat(own(raw3)) - mean3) * inv3
    v = hat * gain[2] + shift[2]
    dy = d_coarse * silu_grad(v, jax.nn.sigmoid(v))
    norm_back(7, 7, dy, hat, raw3, mean3, inv3, gain[2], (CX, CY, CZ), coarse_voxels, (s.dy3, s.dyl3), [])
    side_start([head_grad[0:1], head_grad[1:2], head_grad[2:3], bias_line, psi_grad])
    red_three(units_a)
    d_skip = s.d_skip
    d_skip[...] = grad_gated * att_own + dot_nt(low_fine, w_x)
    conv_grad(pad_join, low_raw4, ROW_DEC1, (X, Y))
    g_ref[ROW_X : ROW_X + C1 // 2, :] = narrow_back(
        dot_tn(skip_own.astype(BF16), low_fine), C1 // 2
    )
    g_ref[ROW_G : ROW_G + C2 // 2, :] = narrow_back(dot_tn(coarse_own, low_gc), C2 // 2)
    red_one(units_b)
    sums, back = norm_back_end(7, 7, raw3, mean3, inv3, gain[2], coarse_voxels, (s.dy3, s.dyl3))
    grad_shift[2], grad_gain[2] = [sums[0:1], sums[1:2]], [sums[2:3], sums[3:4]]
    dpad = s.dpad3
    put_three(dpad, back[:, 0:C1], 0, C2)
    put_three(dpad, back[:, C1:C2], C1, C2)
    clear_edges(dpad, 1)
    low_raw3 = flat(own(dpad)[:, :, :, C2 : 2 * C2])
    d_pool = conv_back(dpad, wm, 0, C1, C2, (CX, CY))
    grad_skip = d_skip[...] + spread(d_pool) * 0.125
    hat = (flat(own(raw2)) - mean2) * inv2
    v = hat * gain[1] + shift[1]
    dy = grad_skip * silu_grad(v, jax.nn.sigmoid(v))
    norm_back(8, 8, dy, hat, raw2, mean2, inv2, gain[1], fine, voxels, (s.dy2, s.dyl2), [])
    red_two(units_b)
    for ab in range(9):
        window = pad_mid[ab // 3 : ab // 3 + CX, ab % 3 : ab % 3 + CY].reshape(VC, 3 * C1)
        block = dot_tn(window, low_raw3).astype(BF16)
        for c in range(3):
            stacked = block[c * C1 : (c + 1) * C1]
            stacked = jnp.concatenate([stacked[:, 0:C1], stacked[:, C1:C2]], 0)
            lo = ROW_MID + (3 * ab + c) * C2
            g_ref[lo : lo + C2, :] = dot(shuffle, stacked).astype(BF16)
    red_one(units_c)
    red_four(units_a)
    red_two(units_c)
    sums, back = norm_back_end(8, 8, raw2, mean2, inv2, gain[1], voxels, (s.dy2, s.dyl2))
    grad_shift[1], grad_gain[1] = [sums[0:1]], [sums[1:2]]
    dpad = s.dpad2
    put_three(dpad, back, 0, C1)
    clear_edges(dpad, 1)
    low_raw2 = flat(own(dpad)[:, :, :, C1 : 2 * C1])
    conv_grad(pad1, low_raw2, ROW_ENC, (X, Y))
    red_one(units_d)
    red_between(units_a)
    units_b1 = [u for u in units_b if u[0] < nz - 1]
    units_b2 = [u for u in units_b if u[0] == nz - 1]
    red_three(units_b1)
    grad_act = conv_in(dpad, s.turn2, ROW_ENC, C1)
    hat1 = (flat(own(raw1)) - mean1) * inv1
    v = hat1 * gain[0] + shift[0]
    dy = grad_act * silu_grad(v, jax.nn.sigmoid(v))
    low_raw1 = dy.astype(BF16)
    red_two(units_d)
    red_three(units_b2)
    red_three(units_c)
    ar_start(9, [col_sum(dy), col_sum(dy * hat1)])
    entry_block = entry_grad(low_raw1)
    red_four(units_b1)
    red_three(units_d)
    red_four(units_b2)
    red_between(units_b1)
    red_four(units_c)
    in_put(1, entry_block)
    red_four(units_d)
    red_between(units_b2)
    red_between(units_c)
    red_between(units_d)

    sums = ar_wait(9)
    grad_shift[0], grad_gain[0] = [sums[0:1]], [sums[1:2]]
    side_whole().wait_recv()
    small = jnp.sum(side[...], axis=0)
    flat_rows = []
    for r in range(CLASSES):
        row = None
        for j in range(CLASSES):
            part = lax.dot_general(
                small,
                select_head(j, r).astype(F32),
                (((1,), (1,)), ((), ())),
                preferred_element_type=F32,
                precision=lax.Precision.HIGHEST,
            )[j : j + 1]
            row = part if row is None else row + part
        flat_rows.append(row)
    later = []
    for group in (grad_gain, grad_shift):
        for layer in range(5):
            later += group[layer]
    later = [pltpu.roll(row, used_lanes, 1) for row in later]
    flat_rows.append(jnp.where(lane_id < used_lanes, small[3:4], later[0]))
    for q in range(1, 12):
        flat_rows.append(jnp.where(lane_id < used_lanes, later[q - 1], later[q]))
    flat_rows.append(jnp.where(lane_id < used_lanes, later[11], 0.0))
    tail_grad = jnp.concatenate(flat_rows, 0)
    psi_row = jnp.where(lane_id < GATE, small[4:5], 0.0)
    loss_out[...] = loss_row[:, 0:1]
    count_out[...] = valid_count


    position = (
        me * lay.rows * LANES
        + iota((lay.rows, LANES), 0) * LANES
        + iota((lay.rows, LANES), 1)
    )
    limits = STARTS + (USED, total * lay.rows * LANES)

    def segment_lines(square):
        rows = []
        for k in range(len(limits) - 1):
            member = (position >= limits[k]) & (position < limits[k + 1])
            rows.append(col_sum(jnp.where(member, square, 0.0)))
        return rows

    weight_lines = segment_lines(param_ref[...] * param_ref[...])
    red_five(units)
    base = 16 * (begin - 1) - 16

    def put_row(row, block):
        at = row - base
        rows = block.shape[0]

        @pl.when((at >= 16) & (at + rows <= 16 + win_rows))
        def _():
            acc[pl.ds(pl.multiple_of(at, 16), rows), :] = block

    put_row(ROW_TAIL, tail_grad)
    put_row(ROW_PSI, jnp.concatenate([psi_row, jnp.zeros((15, LANES), F32)], 0))

    @pl.when(me == 0)
    def _():
        for k in range(2):
            in_whole(k).wait_recv()
        with_hat, with_dy = [jnp.sum(in_slots[k].astype(F32), axis=0) for k in range(2)]
        with_one = jnp.sum(jnp.where(tap_at, with_hat[0:1], 0.0), axis=1, keepdims=True)
        with_hat = jnp.where(iota((32, LANES), 0) < ROW_IN, 0.0, with_hat)
        entry_total = with_dy - with_one * (grad_shift[0][0] / voxels)
        entry_total = entry_total - with_hat * (grad_gain[0][0] / voxels)
        at = 16 - 16 * (lay.begin[0] - 1)
        acc[at : at + 32] = acc[at : at + 32] + entry_total * (inv1 * gain[0])

    grad_a = acc[pl.ds(16 + off_a, lay.rows), :]
    late = pltpu.roll(acc[pl.ds(16 + off_b + 1, lay.rows), :], LANES // 2, 1)
    early = pltpu.roll(acc[pl.ds(16 + off_b, lay.rows), :], LANES // 2, 1)
    grad_b = jnp.where(lane < LANES // 2, early, late)
    gradient = jnp.where(position < SPLIT, grad_a, grad_b)
    gradient = jnp.where(position < USED, gradient, 0.0)
    params = param_ref[...]
    new_first = BETA_ONE * first_ref[...] + (1.0 - BETA_ONE) * gradient
    new_second = BETA_TWO * second_ref[...] + (1.0 - BETA_TWO) * gradient * gradient
    first_out[...] = new_first
    second_out[...] = new_second
    update = (
        new_first
        / (1.0 - BETA_ONE**STEP)
        / (jnp.sqrt(new_second / (1.0 - BETA_TWO**STEP)) + EPS_ADAM)
        + DECAY_RATE * params
    )
    param_out[...] = update
    lines = weight_lines + segment_lines(update * update)
    lines = jnp.concatenate(lines, 0)
    lines = jnp.sum(lines, axis=1, keepdims=True)
    k = lines.shape[0]
    line = col_sum(jnp.where(iota((k, LANES), 0) == iota((k, LANES), 1), lines, 0.0))
    ar_start(10, [line])
    sums = ar_wait(10)[0:1]
    parts = len(limits) - 1
    roots = jnp.sqrt(sums)
    scale = jnp.zeros((lay.rows, LANES), F32)
    for k in range(parts):
        member = (position >= limits[k]) & (position < limits[k + 1])
        ratio = roots[:, k : k + 1] / roots[:, parts + k : parts + k + 1]
        scale = jnp.where(member, ratio, scale)
    param_out[...] = param_ref[...] - LEARN_RATE * scale * param_out[...]

    gather_end()
    quick_end()
    for zp in range(nz):

        @pl.when((here[0] >= zp) & (here[0] < nz - 1))
        def _():
            for piece in every:
                onward_copy(zp, True, piece).wait_send()

        @pl.when((here[0] <= zp) & (here[0] > 0))
        def _():
            for piece in every:
                onward_copy(zp, False, piece).wait_send()

    red_finish()

    @pl.when(me != 0)
    def _():
        for k in range(2):
            in_copy(k).wait_send()

    for r in range(N_AR):
        ar_whole(r).wait_send()
    side_whole().wait_send()
    for i in range(8):
        ct_copy(i).wait_send()
    for h, framed in enumerate(
        (s.low2, s.pool_in, s.low3, s.low4, s.low5, s.dyl5, s.dyl4, s.dyl3, s.dyl2)
    ):
        for i in range(8):
            halo_copy(h, framed, i).wait_send()


def step_call(nw, nn, ext, ct, marks, params, first, second):
    X, Y, Z = ext
    XE, YE = X + 2, Y + 2
    CX, CY, CZ = X // 2, Y // 2, Z // 2
    total = nw * nn
    framed = (XE, YE, Z)
    small = (CX + 2, CY + 2, CZ)
    dma = pltpu.SemaphoreType.DMA
    rows = params.shape[0]
    lay = Layout(rows * LANES, total)
    nz, nx, ny, nc = grid_of(nw, nn)
    oy = max(ny - 1, 1)
    half = 16 * (-(-lay.window // 32))
    low = lambda *shape: pltpu.VMEM(shape, BF16)
    scratch = dict(
        weights=low(lay.weight_rows, LANES),
        grads=low(lay.grad_rows, LANES),
        natural=pltpu.VMEM((rows + 112, LANES), F32),
        fix=low(total, lay.fix, LANES),
        quick=low(48, LANES),
        quick_send=dma((2,)),
        quick_recv=dma((2,)),
        onward_send=dma((nz, 2, PIECES)),
        gather_send=dma((PIECES,)),
        gather_recv=dma((total, PIECES)),
        red_c=low(nz, nx, ny, nc - 1, lay.window, LANES),
        red_dx=low(nz, nx, oy, half, LANES),
        red_dy=low(nz, nx, oy, lay.window - half, LANES),
        red_ex=low(nz, nx, lay.window, LANES),
        red_ey=low(nz, oy, lay.window, LANES),
        red_z=low(nz if nz == 4 else 1, nz, lay.window, LANES),
        send_core=dma((nz, nx, ny, nc - 1)),
        recv_core=dma((nz, nx, ny, nc - 1)),
        send_dx=dma((nz, nx, oy)),
        recv_dx=dma((nz, nx, oy)),
        send_dy=dma((nz, nx, oy)),
        recv_dy=dma((nz, nx, oy)),
        send_ex=dma((nz, nx)),
        recv_ex=dma((nz, nx)),
        send_ey=dma((nz, nx, oy)),
        recv_ey=dma((nz, oy)),
        send_z=dma((nz, nx, 2)),
        recv_z=dma((nz, nz, 2)),
        acc=pltpu.VMEM((lay.window + 48, LANES), F32),
        in_slots=pltpu.VMEM((2, total, 32, LANES), F32 if total <= 64 else BF16),
        in_send=dma((2,)),
        in_recv=dma((2,)),
        slots=pltpu.VMEM((N_AR, total, 4, LANES), F32),
        ar_send=dma((N_AR,)),
        ar_recv=dma((N_AR,)),
        side=pltpu.VMEM((total, 8, LANES), F32),
        side_send=dma,
        side_recv=dma,
        halo_send=dma((N_HALO, 8)),
        halo_recv=dma((N_HALO, 8)),
        cts=pltpu.VMEM((9, X * Y, LANES), F32),
        ct_send=dma((8,)),
        ct_recv=dma((8,)),
        pair=pltpu.VMEM((CY * Z, LANES), F32),
        we=pltpu.VMEM((9 * LANES, LANES), BF16),
        wm=pltpu.VMEM((27 * C1, C2), BF16),
        entry=pltpu.VMEM((X + 4, Y + 4, Z, LANES), BF16),
        raw1=pltpu.VMEM(framed + (C1,), F32),
        pad1=pltpu.VMEM(framed + (3 * C1,), BF16),
        raw2=pltpu.VMEM(framed + (C1,), F32),
        low2=pltpu.VMEM(framed + (C1,), BF16),
        pool_in=pltpu.VMEM(small + (C1,), BF16),
        skip=pltpu.VMEM(framed + (C1,), F32),
        mix=pltpu.VMEM(framed + (LANES,), F32),
        attention=pltpu.VMEM(framed + (LANES,), F32),
        pad_mid=pltpu.VMEM(small + (3 * C1,), BF16),
        raw3=pltpu.VMEM(small + (C2,), F32),
        low3=pltpu.VMEM(small + (C2,), BF16),
        tall=pltpu.VMEM((CX + 2, CY + 2, Z, C2), BF16),
        pad_join=pltpu.VMEM(framed + (3 * (C1 + C2),), BF16),
        raw4=pltpu.VMEM(framed + (C1,), F32),
        low4=pltpu.VMEM(framed + (C1,), BF16),
        pad4=pltpu.VMEM(framed + (3 * C1,), BF16),
        raw5=pltpu.VMEM(framed + (C1,), F32),
        low5=pltpu.VMEM(framed + (C1,), BF16),
        dy5=pltpu.VMEM(framed + (C1,), F32),
        dyl5=pltpu.VMEM(framed + (C1,), BF16),
        dpad5=pltpu.VMEM(framed + (3 * C1,), BF16),
        dy4=pltpu.VMEM(framed + (C1,), F32),
        dyl4=pltpu.VMEM(framed + (C1,), BF16),
        dpad4=pltpu.VMEM(framed + (3 * C1,), BF16),
        dy3=pltpu.VMEM(small + (C2,), F32),
        dyl3=pltpu.VMEM(small + (C2,), BF16),
        dpad3=pltpu.VMEM(small + (3 * C2,), BF16),
        dy2=pltpu.VMEM(framed + (C1,), F32),
        dyl2=pltpu.VMEM(framed + (C1,), BF16),
        dpad2=pltpu.VMEM(framed + (3 * C1,), BF16),
        d_skip=pltpu.VMEM((X * Y * Z, C1), F32),
    )
    if total <= 64:
        scratch.update(
            turn2=low(27 * C1, C1), turn4=low(27 * C1, C1 + C2), turn5=low(27 * C1, C1)
        )
    cfg = types.SimpleNamespace(nw=nw, nn=nn, ext=ext, names=tuple(scratch), lay=lay)
    vmem = pl.BlockSpec(memory_space=pltpu.VMEM)
    return pl.pallas_call(
        functools.partial(step_kernel, cfg),
        out_shape=(
            jax.ShapeDtypeStruct((rows, LANES), F32),
            jax.ShapeDtypeStruct((rows, LANES), F32),
            jax.ShapeDtypeStruct((rows, LANES), F32),
            jax.ShapeDtypeStruct((1, 1), F32),
            jax.ShapeDtypeStruct((1, 1), F32),
        ),
        in_specs=[vmem] * 5,
        out_specs=(vmem,) * 5,
        scratch_shapes=list(scratch.values()),
        compiler_params=pltpu.CompilerParams(
            collective_id=0, has_side_effects=True, vmem_limit_bytes=62 * 1024 * 1024
        ),
    )(ct, marks, params, first, second)


def on_device(params, first_moment, second_moment, ct_image, labels, valid_mask):
    ext = ct_image.shape
    ct = ct_image.astype(F32).reshape(-1, ext[2])
    new_params, new_first, new_second, loss_sum, valid_count = step_call(
        lax.axis_size("wide"),
        lax.axis_size("narrow"),
        ext,
        ct,
        jnp.stack([labels.reshape(-1), valid_mask.reshape(-1)]),
        params.reshape(-1, LANES),
        first_moment.reshape(-1, LANES),
        second_moment.reshape(-1, LANES),
    )
    return (
        new_params.reshape(-1),
        new_first.reshape(-1),
        new_second.reshape(-1),
        loss_sum.reshape(()),
        valid_count.reshape(()),
    )


def solution(mesh):
    in_specs = (
        P(("wide", "narrow")),
        P(("wide", "narrow")),
        P(("wide", "narrow")),
        P("wide", "narrow", None),
        P("wide", "narrow", None),
        P("wide", "narrow", None),
    )
    out_specs = (P(("wide", "narrow")), P(("wide", "narrow")), P(("wide", "narrow")), P(), P())
    return jax.shard_map(
        on_device, mesh=mesh, in_specs=in_specs, out_specs=out_specs, check_vma=False
    )
```
